32 devices in a mesh: rep: 4 (over z), fsdp: 8 (over y, x, core).
Axes of the slice: x: 2, y: 2, z: 4, core: 2. Of those that a mesh axis runs over, the one named last changes fastest.
Arguments:
- input_map: bfloat16 [256, 32, 32, 128], P(('rep', 'fsdp')), may hold values from -6 to 6
- valid_size: int32 [256, 2], P(('rep', 'fsdp')), may hold values from 8 to 32
- gain_one: bfloat16 [128], P('fsdp'), may hold values from 0.25 to 1.75
- bias_one: bfloat16 [128], P('fsdp'), may hold values from -3 to 3
- w_hcycle: bfloat16 [128, 128], P('fsdp'), may hold values from -0.5 to 0.5
- b_hcycle: bfloat16 [128], P('fsdp'), may hold values from -3 to 3
- w_wcycle: bfloat16 [128, 128], P('fsdp'), may hold values from -0.5 to 0.5
- b_wcycle: bfloat16 [128], P('fsdp'), may hold values from -3 to 3
- w_channel: bfloat16 [128, 128], P('fsdp'), may hold values from -0.5 to 0.5
- w_reduce: bfloat16 [128, 32], P('fsdp'), may hold values from -1 to 1
- b_reduce: bfloat16 [32], P('fsdp'), may hold values from -3 to 3
- w_expand: bfloat16 [32, 384], P('fsdp'), may hold values from -1.5 to 1.5
- b_expand: bfloat16 [384], P('fsdp'), may hold values from -3 to 3
- w_proj: bfloat16 [128, 128], P('fsdp'), may hold values from -0.75 to 0.75
- b_proj: bfloat16 [128], P('fsdp'), may hold values from -3 to 3
- gain_two: bfloat16 [128], P('fsdp'), may hold values from 0.25 to 1.75
- bias_two: bfloat16 [128], P('fsdp'), may hold values from -3 to 3
- w_up: bfloat16 [128, 512], P('fsdp'), may hold values from -0.5 to 0.5
- b_up: bfloat16 [512], P('fsdp'), may hold values from -3 to 3
- w_down: bfloat16 [512, 128], P('fsdp'), may hold values from -0.375 to 0.375
- b_down: bfloat16 [128], P('fsdp'), may hold values from -3 to 3
- w_conv: bfloat16 [3, 3, 128, 320], P(None, None, 'fsdp'), may hold values from -0.1875 to 0.1875
- b_conv: bfloat16 [320], P('fsdp'), may hold values from -3 to 3
- cotangent: bfloat16 [256, 16, 16, 320], P(('rep', 'fsdp')), may hold values from -6 to 6
Outputs:
- output_map: bfloat16 [256, 16, 16, 320], P(('rep', 'fsdp'))
- input_grad: float32 [256, 32, 32, 128], P(('rep', 'fsdp'))
- grad_gain_one: float32 [128], P('fsdp')
- grad_bias_one: float32 [128], P('fsdp')
- grad_w_hcycle: float32 [128, 128], P('fsdp')
- grad_b_hcycle: float32 [128], P('fsdp')
- grad_w_wcycle: float32 [128, 128], P('fsdp')
- grad_b_wcycle: float32 [128], P('fsdp')
- grad_w_channel: float32 [128, 128], P('fsdp')
- grad_w_reduce: float32 [128, 32], P('fsdp')
- grad_b_reduce: float32 [32], P('fsdp')
- grad_w_expand: float32 [32, 384], P('fsdp')
- grad_b_expand: float32 [384], P('fsdp')
- grad_w_proj: float32 [128, 128], P('fsdp')
- grad_b_proj: float32 [128], P('fsdp')
- grad_gain_two: float32 [128], P('fsdp')
- grad_bias_two: float32 [128], P('fsdp')
- grad_w_up: float32 [128, 512], P('fsdp')
- grad_b_up: float32 [512], P('fsdp')
- grad_w_down: float32 [512, 128], P('fsdp')
- grad_b_down: float32 [128], P('fsdp')
- grad_w_conv: float32 [3, 3, 128, 320], P(None, None, 'fsdp')
- grad_b_conv: float32 [320], P('fsdp')
The draws below stay inside these ranges and needn't reach their ends.
Inputs may be any that keep to these rules, and one draw needn't show every extreme that they name: valid_size[n, 0] is the valid height and valid_size[n, 1] the valid width of image n; the rest of its map is padding.
All inputs are finite; a program needn't handle non-finite values.
Results may differ from the reference program's by a relative error of at most 0.0072.
Values may be sent and summed in bfloat16 or wider, within the bound.
No kernel may reach another device: no remote copies, remote signals or barrier semaphores. Data moves between devices by JAX's collectives and lax.ppermute only.
A program may use at most 192 MiB of HBM per device.

```python
import jax
import jax.numpy as jnp
from jax import lax

D = 128
FF = 512
R = 32
CO = 320
MAP = 32
IMAGES = 256


def with_ends(drawn, key, low, high):
    longest = drawn.shape.index(max(drawn.shape))
    spots = []
    for shift in (0, 1):
        where = [jax.random.randint(jax.random.fold_in(key, axis), (), 0, length) for axis, length in enumerate(drawn.shape)]
        where[longest] = (where[longest] + shift) % drawn.shape[longest]
        spots.append(tuple(where))
    return drawn.at[spots[0]].set(low).at[spots[1]].set(high)


def shard_levels(own_key, shape, cuts, smallest, high):
    level, own = 1.0, jax.random.fold_in(own_key, 6)
    for axis_at, blocks in cuts:
        heights = jnp.exp(jax.random.uniform(jax.random.fold_in(own, axis_at), (blocks,), jnp.float32, smallest / len(cuts), high / len(cuts)))
        level = level * jnp.repeat(heights, shape[axis_at] // blocks).reshape([-1 if axis == axis_at else 1 for axis in range(len(shape))])
    return level


def centred(rng, extent, scale, limit, cuts=(), dtype=jnp.bfloat16):
    values = jax.random.normal(rng, extent, jnp.float32) * scale
    if len(cuts) > 0:
        values = shard_levels(rng, extent, cuts, -0.22, 0.18) * values
    return jnp.clip(values, min=-limit, max=limit).astype(dtype)


def setup_inputs(seed: int = 0) -> dict:
    key_list = jax.random.split(jax.random.key(seed), 25)
    return {
        "input_map": centred(key_list[0], (IMAGES, MAP, MAP, D), 1.0, 6.0, ((0, 32),)),
        "valid_size": with_ends(jax.random.randint(key_list[1], (IMAGES, 2), MAP // 4, MAP + 1), jax.random.fold_in(key_list[1], 1), MAP // 4, MAP).astype(jnp.int32),
        "gain_one": jnp.clip(1.0 + 0.15 * jax.random.normal(key_list[2], (D,), jnp.float32), 0.25, 1.75).astype(jnp.bfloat16),
        "bias_one": centred(key_list[3], (D,), 0.5, 3.0, ((0, 8),)),
        "w_hcycle": centred(key_list[4], (D, D), D ** -0.5, 0.5, ((0, 8),)),
        "b_hcycle": centred(key_list[5], (D,), 0.5, 3.0, ((0, 8),)),
        "w_wcycle": centred(key_list[6], (D, D), D ** -0.5, 0.5, ((0, 8),)),
        "b_wcycle": centred(key_list[7], (D,), 0.5, 3.0, ((0, 8),)),
        "w_channel": centred(key_list[8], (D, D), D ** -0.5, 0.5, ((0, 8),)),
        "w_reduce": centred(key_list[9], (D, R), (D // 4) ** -0.5, 1.0, ((0, 8),)),
        "b_reduce": centred(key_list[10], (R,), 0.5, 3.0, ((0, 8),)),
        "w_expand": centred(key_list[11], (R, 3 * D), (R // 2) ** -0.5, 1.5, ((0, 8),)),
        "b_expand": centred(key_list[12], (3 * D,), 0.5, 3.0, ((0, 8),)),
        "w_proj": centred(key_list[13], (D, D), (D // 2) ** -0.5, 0.75, ((0, 8),)),
        "b_proj": centred(key_list[14], (D,), 0.5, 3.0, ((0, 8),)),
        "gain_two": jnp.clip(1.0 + 0.15 * jax.random.normal(key_list[15], (D,), jnp.float32), 0.25, 1.75).astype(jnp.bfloat16),
        "bias_two": centred(key_list[16], (D,), 0.5, 3.0, ((0, 8),)),
        "w_up": centred(key_list[17], (D, FF), D ** -0.5, 0.5, ((0, 8),)),
        "b_up": centred(key_list[18], (FF,), 0.5, 3.0, ((0, 8),)),
        "w_down": centred(key_list[19], (FF, D), (FF // 2) ** -0.5, 0.375, ((0, 8),)),
        "b_down": centred(key_list[20], (D,), 0.5, 3.0, ((0, 8),)),
        "w_conv": centred(key_list[21], (3, 3, D, CO), (9 * D) ** -0.5, 0.1875, ((2, 8),)),
        "b_conv": centred(key_list[22], (CO,), 0.5, 3.0, ((0, 8),)),
        "cotangent": centred(key_list[23], (IMAGES, MAP // 2, MAP // 2, CO), 1.0, 6.0, ((0, 32),)),
    }


@jax.custom_vjp
def low(v):
    return lax.optimization_barrier(v.astype(jnp.bfloat16)).astype(jnp.float32)

@jax.custom_vjp
def low_back(v):
    return v

def low_keep(v):
    return (low(v), None)

def low_pass(kept, grad):
    return (grad,)

def back_keep(v):
    return (v, None)

def back_low(kept, grad):
    return (low(grad),)
low.defvjp(low_keep, low_pass)
low_back.defvjp(back_keep, back_low)

def layer_norm(values, scales, shifts):
    centre = values - lax.optimization_barrier(jnp.mean(values, axis=-1, keepdims=True))
    spread = lax.optimization_barrier(jnp.mean(centre * centre, axis=-1, keepdims=True))
    return centre * lax.rsqrt(spread + 1e-05) * scales + shifts

def cycle(values, axis_dim, direction):
    length = values.shape[axis_dim]
    channel = lax.broadcasted_iota(jnp.int32, (values.shape[-1],), 0)
    offsets = direction * ((channel + 1) % 3 - 1)
    zero_row = jnp.zeros_like(lax.slice_in_dim(values, 0, 1, axis=axis_dim))
    ahead = jnp.concatenate([lax.slice_in_dim(values, 1, length, axis=axis_dim), zero_row], axis=axis_dim)
    behind = jnp.concatenate([zero_row, lax.slice_in_dim(values, 0, length - 1, axis=axis_dim)], axis=axis_dim)
    return jnp.where(offsets == 1, ahead, jnp.where(offsets == -1, behind, values))

def patches(values):
    side = values.shape[1]
    padded = jnp.pad(values, ((0, 0), (1, 1), (1, 1), (0, 0)))
    pieces = [padded[:, row_off:row_off + side:2, col_off:col_off + side:2, :] for row_off in range(3) for col_off in range(3)]
    return jnp.concatenate(pieces, axis=-1)

def gelu_exact(values):
    return jax.nn.gelu(values, approximate=False)

def reweight(pooled, w_reduce, b_reduce, w_expand, b_expand):
    hidden = gelu_exact(jnp.dot(pooled, w_reduce, precision=lax.Precision.HIGHEST) + b_reduce)
    logits = jnp.dot(hidden, w_expand, precision=lax.Precision.HIGHEST) + b_expand
    logits = logits.reshape(pooled.shape[0], pooled.shape[1], 3)
    return jax.nn.softmax(logits, axis=-1)

def valid_mask(valid_size, side):
    rows_at = lax.broadcasted_iota(jnp.int32, (1, side, side, 1), 1)
    cols_at = lax.broadcasted_iota(jnp.int32, (1, side, side, 1), 2)
    inside = (rows_at < valid_size[:, 0].reshape(-1, 1, 1, 1)) & (cols_at < valid_size[:, 1].reshape(-1, 1, 1, 1))
    count = (valid_size[:, 0] * valid_size[:, 1]).astype(jnp.float32)
    return (inside.astype(jnp.float32), count)

def mat_high(left, right):
    return jnp.dot(left, right, precision=lax.Precision.HIGHEST)

def forward(images, valid_size, params):
    gain_one, bias_one, w_hcycle, b_hcycle, w_wcycle, b_wcycle, w_channel, w_reduce, b_reduce, w_expand, b_expand, w_proj, b_proj, gain_two, bias_two, w_up, b_up, w_down, b_down, w_conv, b_conv = params
    inside, count = valid_mask(valid_size, images.shape[1])
    normed = low(layer_norm(images, gain_one, bias_one))
    mix_height = low_back(mat_high(cycle(normed, 1, 1), w_hcycle) + b_hcycle)
    mix_width = low_back(mat_high(cycle(normed, 2, 1), w_wcycle) + b_wcycle)
    mix_chan = low_back(mat_high(normed, w_channel))
    summed = mix_height + mix_width + mix_chan
    pooled = lax.optimization_barrier(jnp.sum(summed * inside, axis=(1, 2))) / count[:, None]
    mixing = reweight(pooled, w_reduce, b_reduce, w_expand, b_expand)
    mixed = low(mix_height * mixing[:, None, None, :, 0] + mix_width * mixing[:, None, None, :, 1] + mix_chan * mixing[:, None, None, :, 2])
    first = images + low_back(mat_high(mixed, w_proj) + b_proj)
    normed_two = low(layer_norm(first, gain_two, bias_two))
    hidden_pre = low_back(mat_high(normed_two, w_up) + b_up)
    activated = low(gelu_exact(hidden_pre))
    second = first + low_back(mat_high(activated, w_down) + b_down)
    lowered = low(second)
    return mat_high(patches(lowered), w_conv.reshape(-1, w_conv.shape[-1])) + b_conv

def reference(input_map, valid_size, gain_one, bias_one, w_hcycle, b_hcycle, w_wcycle, b_wcycle, w_channel, w_reduce, b_reduce, w_expand, b_expand, w_proj, b_proj, gain_two, bias_two, w_up, b_up, w_down, b_down, w_conv, b_conv, cotangent):
    params = tuple((weight_arr.astype(jnp.float32) for weight_arr in (gain_one, bias_one, w_hcycle, b_hcycle, w_wcycle, b_wcycle, w_channel, w_reduce, b_reduce, w_expand, b_expand, w_proj, b_proj, gain_two, bias_two, w_up, b_up, w_down, b_down, w_conv, b_conv)))
    images = input_map.astype(jnp.float32)
    group = 4
    blocks = images.shape[0] // group

    def split(array):
        return array.reshape((blocks, group) + array.shape[1:])

    def one_group(totals, pieces):
        block_images, block_valid, block_cot = pieces

        def local(inputs, weights):
            return forward(inputs, block_valid, weights)
        result, pullback = jax.vjp(local, block_images, params)
        grad_images, grad_params = pullback(block_cot.astype(jnp.float32))
        return (jax.tree.map(jnp.add, totals, grad_params), (result.astype(jnp.bfloat16), grad_images))
    zeros = tuple((jnp.zeros(weight_arr.shape, jnp.float32) for weight_arr in params))
    totals, (outputs, grads) = lax.scan(one_group, zeros, (split(images), split(valid_size), split(cotangent)))
    output_map = outputs.reshape((-1,) + outputs.shape[2:])
    input_grad = grads.reshape((-1,) + grads.shape[2:])
    return (output_map, input_grad, totals[0], totals[1], totals[2], totals[3], totals[4], totals[5], totals[6], totals[7], totals[8], totals[9], totals[10], totals[11], totals[12], totals[13], totals[14], totals[15], totals[16], totals[17], totals[18], totals[19], totals[20])
```

```python
import functools

import jax
import jax.numpy as jnp
from jax import lax
from jax.experimental import pallas as pl
from jax.experimental.pallas import tpu as pltpu
from jax.sharding import PartitionSpec as P

BF = jnp.bfloat16
F32 = jnp.float32
HIGH = lax.Precision.HIGHEST
EPS = 1e-05

SHARDS = 8
B_HEIGHT, B_WIDTH, B_CHANNEL, B_PROJ, B_REDUCE = 0, 1, 2, 3, 4
B_EXPAND, B_UP, B_DOWN, B_CONV, B_VEC = 5, 8, 12, 16, 43
BLOCKS = 44
ROWS = 16 * BLOCKS
TAPS = (4, 5, 7, 8, 3, 6, 1, 2, 0)
(V_GAIN1, V_BIAS1, V_BH, V_BW, V_BR, V_BE, V_BP, V_GAIN2, V_BIAS2, V_BUP, V_BDOWN, V_BCONV) = range(12)
LENGTHS = (16, 16, 16, 16, 4, 48, 16, 16, 16, 64, 16, 40)
G1_CONV, G1_UP, G1_DOWN, G1_PROJ, G1_VEC, G1_BLOCKS = 0, 27, 31, 35, 36, 37
G1_BCONV, G1_BUP, G1_BDOWN, G1_BPROJ, G1_GAIN2, G1_BIAS2 = 0, 3, 7, 8, 9, 10
G2_HEIGHT, G2_WIDTH, G2_CHANNEL, G2_REDUCE, G2_EXPAND, G2_VEC, G2_BLOCKS = 0, 1, 2, 3, 4, 5, 6
G2_GAIN1, G2_BIAS1, G2_BH, G2_BW, G2_BR, G2_BE = 0, 1, 2, 3, 4, 5


def iota(shape, axis):
    return lax.broadcasted_iota(jnp.int32, shape, axis)


def dot(left, right):
    return jnp.dot(left, right, preferred_element_type=F32)


def dot_nt(left, right):
    return lax.dot_general(left, right, (((1,), (1,)), ((), ())), preferred_element_type=F32)


def dot_tn(left, right):
    return lax.dot_general(left, right, (((0,), (0,)), ((), ())), preferred_element_type=F32)


def dot_high(left, right):
    return jnp.dot(left, right, preferred_element_type=F32, precision=HIGH)


def dot_nt_high(left, right):
    return lax.dot_general(
        left, right, (((1,), (1,)), ((), ())), preferred_element_type=F32, precision=HIGH
    )


def dot_tn_high(left, right):
    return lax.dot_general(
        left, right, (((0,), (0,)), ((), ())), preferred_element_type=F32, precision=HIGH
    )


def fold8(values):
    rows, cols = values.shape
    return jnp.sum(values.reshape(rows // 8, 8, cols), axis=0)


def lane_mean(values):
    return jnp.mean(values, axis=-1, keepdims=True)


def gelu_both(values):
    cdf = 0.5 + 0.5 * lax.erf(values * 0.7071067811865476)
    slope = cdf + values * (jnp.exp(-0.5 * (values * values)) * 0.3989422804014327)
    return values * cdf, slope


def block(packed, at):
    return packed[:, 16 * at : 16 * at + 16, :].reshape(128, 128)


def branch_weights(packed):
    return [block(packed, at) for at in (B_HEIGHT, B_WIDTH, B_CHANNEL)]


def spread_matrix():
    unit, lane = iota((128, 128), 0), iota((128, 128), 1)
    return ((lane == 16 * (unit // 4) + unit % 4) & (unit < 32)).astype(BF)


def pick_matrix(k):
    return (iota((384, 128), 0) == 3 * iota((384, 128), 1) + k).astype(BF)


def head_weights(packed, vec):
    w_reduce = dot(block(packed, B_REDUCE), spread_matrix())
    expand = [block(packed, B_EXPAND + b) for b in range(3)]
    w_expand, b_expand = [], []
    for k in range(3):
        pick = pick_matrix(k)
        w_expand.append(sum(dot(expand[b], pick[128 * b : 128 * b + 128]) for b in range(3)))
        b_expand.append(dot(vec[:, 0:384].astype(BF), pick)[V_BE : V_BE + 1, :])
    return w_reduce, w_expand, b_expand


def head_forward(sums, counts, branches, head, vec):
    w_reduce, w_expand, b_expand = head
    pooled = sum(dot_high(s, w.astype(F32)) for s, w in zip(sums, branches)) / counts
    pooled = pooled + (vec[V_BH : V_BH + 1, 0:128] + vec[V_BW : V_BW + 1, 0:128])
    pre = dot_high(pooled, w_reduce) + vec[V_BR : V_BR + 1, 0:128]
    hidden, slope = gelu_both(pre)
    logits = [dot_high(hidden, w) + b for w, b in zip(w_expand, b_expand)]
    top = jnp.maximum(jnp.maximum(logits[0], logits[1]), logits[2])
    powers = [jnp.exp(v - top) for v in logits]
    total = powers[0] + powers[1] + powers[2]
    return pooled, hidden, slope, [v / total for v in powers]


def count_column(valid_ref):
    return (valid_ref[:, 0:1] * valid_ref[:, 1:2]).astype(F32)


def channel_offsets():
    return (iota((1, 32, 128), 2) + 1) % 3 - 1


def inside_map(valid_ref, image):
    shape = (32, 32, 128)
    size = valid_ref[pl.ds(image, 1), :]
    wide = (iota((1, 32, 128), 1) < size[:, 1:2].reshape(1, 1, 1)).astype(F32)
    high = (iota((32, 1, 128), 0) < size[:, 0:1].reshape(1, 1, 1)).astype(F32)
    return jnp.broadcast_to(wide, shape) * jnp.broadcast_to(high, shape)


def place_of(placed):
    if not placed:
        return 0, 0
    shard = lax.axis_index("fsdp")
    return shard // 2, lax.rem(shard, 2)


def pack_kernel(*refs):
    (gain_one, bias_one, w_h, b_h, w_w, b_w, w_c, w_red, b_red, w_exp, b_exp, w_proj, b_proj,
     gain_two, bias_two, w_up, b_up, w_down, b_down, w_conv, b_conv, out, vec) = refs

    def put(at, values):
        out[16 * at : 16 * at + values.shape[0], 0 : values.shape[1]] = values

    put(B_HEIGHT, w_h[...])
    put(B_WIDTH, w_w[...])
    put(B_CHANNEL, w_c[...])
    put(B_PROJ, w_proj[...])
    blank = jnp.zeros((16, 128), BF)
    put(B_REDUCE, blank)
    put(B_REDUCE, w_red[...])
    for b in range(3):
        vec[...] = jnp.zeros((16, 128), F32)
        vec[0:4, :] = w_exp[:, 128 * b : 128 * b + 128].astype(F32)
        put(B_EXPAND + b, vec[...].astype(BF))
    for b in range(4):
        put(B_UP + b, w_up[:, 128 * b : 128 * b + 128])
    put(B_DOWN, w_down[...])
    for at, tap in enumerate(TAPS):
        kernel = w_conv.at[tap // 3, tap % 3]
        put(B_CONV + 3 * at, kernel[:, 0:128])
        put(B_CONV + 3 * at + 1, kernel[:, 128:256])
        put(B_CONV + 3 * at + 2, blank)
        put(B_CONV + 3 * at + 2, kernel[:, 256:320])
    vec[...] = jnp.zeros((16, 128), F32)
    vectors = (gain_one, bias_one, b_h, b_w, b_red, b_exp, b_proj, gain_two, bias_two, b_up, b_down, b_conv)
    for row, (values, length) in enumerate(zip(vectors, LENGTHS)):
        vec[row : row + 1, 0:length] = values[...].astype(F32).reshape(1, length)
    put(B_VEC, vec[...].astype(BF))


def vector_table(packed):
    shards = packed[:, 16 * B_VEC : 16 * B_VEC + 16, :].reshape(128, 128)
    table = jnp.zeros((16, 512), F32)
    rows = iota((16, 512), 0)
    for length in (16, 4, 48, 64, 40):
        step = 16 if length == 4 else length
        lane = iota((128, 512), 1)
        source = iota((128, 512), 0)
        pick = ((source == lane % step) & (source < length)).astype(BF)
        spread = dot(shards, pick)
        mine = (source // 16) == (lane // step)
        whole = jnp.sum(jnp.where(mine, spread, 0.0).reshape(8, 16, 512), axis=0)
        held = functools.reduce(
            jnp.logical_or, [rows == v for v, size in enumerate(LENGTHS) if size == length]
        )
        table = jnp.where(held, whole, table)
    return table


def mixer_kernel(placed, valid, x_ref, mine, other, cat_ref, mix_ref, sums_ref, vec_ref, pk_ref, pad):
    step, steps, count = pl.program_id(0), pl.num_programs(0), x_ref.shape[0]

    @pl.when(step == 0)
    def _():
        core = place_of(placed)[1]
        for chip in range(4):
            pk_ref[2 * chip + core] = mine[chip]
            pk_ref[2 * chip + (1 - core)] = other[chip]
        vec_ref[...] = vector_table(pk_ref)
        pad[...] = jnp.zeros(pad.shape, F32)

    gain = vec_ref[V_GAIN1 : V_GAIN1 + 1, 0:128]
    bias = vec_ref[V_BIAS1 : V_BIAS1 + 1, 0:128]
    values = x_ref[...].reshape(count * 1024, 128).astype(F32)
    centre = values - lane_mean(values)
    scale = lax.rsqrt(lane_mean(centre * centre) + EPS)
    normed = centre * scale * gain + bias
    pad[:, 1:33, 8:40, :] = normed.reshape(count, 32, 32, 128)

    offsets = channel_offsets()
    forth, back = offsets == 1, offsets == -1
    for m in range(count):
        here = pad[m, 1:33, 8:40, :]
        high = jnp.where(
            forth, pad[m, 2:34, 8:40, :], jnp.where(back, pad[m, 0:32, 8:40, :], here)
        )
        wide = jnp.where(
            forth, pad[m, 1:33, 9:41, :], jnp.where(back, pad[m, 1:33, 7:39, :], here)
        )
        image = step * count + m
        inside = inside_map(valid, image)
        for k, branch in enumerate((high, wide, here)):
            cat_ref[image, :, 128 * k : 128 * k + 128] = branch.reshape(1024, 128).astype(BF)
            total = jnp.sum((branch * inside).reshape(1024, 128), axis=0, keepdims=True)
            sums_ref[pl.ds(8 * k + image, 1), :] = total

    @pl.when(step == steps - 1)
    def _():
        vec = vec_ref[...]
        sums = [sums_ref[8 * k : 8 * k + 8, :] for k in range(3)]
        head = head_weights(pk_ref, vec)
        counts = count_column(valid)
        mixing = head_forward(sums, counts, branch_weights(pk_ref), head, vec)[3]
        for k in range(3):
            mix_ref[8 * k : 8 * k + 8, :] = mixing[k]


def mlp_kernel(
    placed, x_ref, cat_ref, mix_ref, cot_ref, vec_ref, pk_ref,
    map_ref, gfirst_ref, gm_ref, keep_ref, send_ref,
    wcat, wproj, wup, wdown, wconv,
    gsec, low, act, ghid, norm2, mixed_s, gtail, gbranch, pm, cotp, cots, cotf,
    a_conv, a_up, a_down, a_proj, a_bconv, a_bup, a_bdown, a_bproj, a_gain2, a_bias2,
):
    step, steps, count = pl.program_id(0), pl.num_programs(0), x_ref.shape[0]

    @pl.when(step == 0)
    def _():
        for k, weight in enumerate(branch_weights(pk_ref)):
            wcat[128 * k : 128 * k + 128, :] = weight
        wproj[...] = block(pk_ref, B_PROJ)
        for b in range(4):
            wup[:, 128 * b : 128 * b + 128] = block(pk_ref, B_UP + b)
        wdown[...] = pk_ref[:, 16 * B_DOWN : 16 * B_DOWN + 64, :].reshape(512, 128)
        for at in range(9):
            for b in range(3):
                wconv[128 * at : 128 * at + 128, 128 * b : 128 * b + 128] = block(
                    pk_ref, B_CONV + 3 * at + b
                )
        for ref in (low, cotp, cots, cotf, a_conv, a_up, a_down, a_proj, a_bconv, a_bup,
                    a_bdown, a_bproj, a_gain2, a_bias2):
            ref[...] = jnp.zeros(ref.shape, ref.dtype)

    def row(at, width=128):
        return vec_ref[at : at + 1, 0:width]

    for m in range(count):
        cot = cot_ref[m]
        cotp[m, 0:256, 0:320] = cot
        cotf[0:256, 0:320] = cot.astype(F32)
        ahead = cotf[1:257, :]
        ahead = jnp.where(iota(ahead.shape, 0) % 16 == 15, 0.0, ahead)
        cots[m, 0:256, :] = ahead.astype(BF)
        a_bconv[...] += fold8(cotf[0:256, :])
    flat = (count * 256, 384)
    cot_here, cot_right = cotp[:, 0:256, :].reshape(flat), cots[:, 0:256, :].reshape(flat)
    cot_below, cot_both = cotp[:, 16:272, :].reshape(flat), cots[:, 16:272, :].reshape(flat)
    pair_a = dot_nt(cot_here, wconv[0:256, :])
    pair_b = dot_nt(cot_here, wconv[256:512, :])
    pair_c = dot_nt(cot_right, wconv[512:768, :])
    pair_d = dot_nt(cot_below, wconv[768:1024, :])
    last = dot_nt(cot_both, wconv[1024:1152, :])
    planes = (
        (pair_a[:, 0:128], pair_a[:, 128:256] + pair_c[:, 0:128]),
        (
            pair_b[:, 0:128] + pair_d[:, 0:128],
            pair_b[:, 128:256] + pair_c[:, 128:256] + pair_d[:, 128:256] + last,
        ),
    )
    for p in range(2):
        for s in range(2):
            plane = planes[p][s]
            for i in range(16 * count):
                gsec[2 * i + p, pl.ds(s, 16, stride=2), :] = plane[16 * i : 16 * i + 16, :]

    for m in range(count):
        mixing = [mix_ref[pl.ds(8 * k + step * count + m, 1), :] for k in range(3)]
        scaled = jnp.concatenate(
            [(wcat[128 * k : 128 * k + 128, :].astype(F32) * mixing[k]).astype(BF) for k in range(3)],
            axis=0,
        )
        mixed_bias = row(V_BH) * mixing[0] + row(V_BW) * mixing[1]
        mixed_s[1024 * m : 1024 * m + 1024, :] = (dot(cat_ref[step * count + m], scaled) + mixed_bias).astype(BF)
    pixels = 1024 * count
    first = x_ref[...].reshape(pixels, 128).astype(F32) + (dot(mixed_s[...], wproj[...]) + row(V_BP))
    centre = first - lane_mean(first)
    scale = lax.rsqrt(lane_mean(centre * centre) + EPS)
    unit = centre * scale
    normed = (unit * row(V_GAIN2) + row(V_BIAS2)).astype(BF)
    norm2[...] = normed
    grad_second = gsec[...].reshape(pixels, 128)
    tail = grad_second.astype(BF)
    gtail[...] = tail
    a_bdown[...] += fold8(tail.astype(F32))
    for b in range(2):
        cols = slice(256 * b, 256 * b + 256)
        hidden = dot(normed, wup[:, cols]) + vec_ref[V_BUP : V_BUP + 1, cols]
        value, slope = gelu_both(hidden)
        act[:, cols] = value.astype(BF)
        grad_hidden = (dot_nt(tail, wdown[cols, :]) * slope).astype(BF)
        ghid[:, cols] = grad_hidden
        a_bup[:, cols] += fold8(grad_hidden.astype(F32))
    second = first + (dot(act[...], wdown[...]) + row(V_BDOWN))
    low[:, 1:33, 8:40, :] = second.reshape(count, 32, 32, 128)
    grad_normed = dot_nt(ghid[...], wup[...])
    weighted = grad_normed * unit
    a_gain2[...] += fold8(weighted)
    a_bias2[...] += fold8(grad_normed)
    scaled_grad = grad_normed * row(V_GAIN2)
    grad_first = grad_second + scale * (
        scaled_grad - lane_mean(scaled_grad) - unit * lane_mean(scaled_grad * unit)
    )
    here = pl.ds(step * count, count)
    gfirst_ref[here] = grad_first.reshape(count, 1024, 128)
    branch = grad_first.astype(BF)
    gbranch[...] = branch
    a_bproj[...] += fold8(branch.astype(F32))
    gm_ref[here] = dot_nt(branch, wproj[...]).astype(BF).reshape(count, 1024, 128)
    a_up[...] += dot_tn(norm2[...], ghid[...])
    a_down[...] += dot_tn(gtail[...], act[...])
    a_proj[...] += dot_tn(mixed_s[...], gbranch[...])

    for at, tap in enumerate(TAPS):
        r, s = tap // 3, tap % 3
        for m in range(count):
            patch = low[m, pl.ds(r, 16, stride=2), pl.ds(7 + s, 16, stride=2), :]
            pm[256 * m : 256 * m + 256, 128 * at : 128 * at + 128] = patch.reshape(256, 128).astype(BF)
    out = dot(pm[...], wconv[...]) + row(V_BCONV, 384)
    map_ref[...] = out[:, 0:320].astype(BF).reshape(count, 256, 320)
    a_conv[...] += dot_tn(pm[...], cot_here)

    @pl.when(step == steps - 1)
    def _():
        chip, core = place_of(placed)[0:2]
        vectors = jnp.concatenate(
            [jnp.sum(a_bconv[:, 128 * b : 128 * b + 128], axis=0, keepdims=True) for b in range(3)]
            + [jnp.sum(a_bup[:, 128 * b : 128 * b + 128], axis=0, keepdims=True) for b in range(4)]
            + [jnp.sum(ref[...], axis=0, keepdims=True) for ref in (a_bdown, a_bproj, a_gain2, a_bias2)]
            + [jnp.zeros((5, 128), F32)],
            axis=0,
        ).astype(BF)
        down = [a_down[:, 128 * b : 128 * b + 128].T for b in range(4)]

        def piece(at, shard):
            rows = slice(16 * shard, 16 * shard + 16)
            if at < G1_UP:
                t, b = at // 3, at % 3
                return a_conv[128 * t + 16 * shard : 128 * t + 16 * shard + 16, 128 * b : 128 * b + 128]
            if at < G1_DOWN:
                b = at - G1_UP
                return a_up[rows, 128 * b : 128 * b + 128]
            if at < G1_PROJ:
                start = 64 * (shard % 2) + 16 * (at - G1_DOWN)
                return down[shard // 2][start : start + 16, :]
            return a_proj[rows, :]

        for peer in range(4):
            to = lax.bitwise_xor(chip, peer)
            for at in range(G1_BLOCKS - 1):
                one, two = piece(at, 2 * peer).astype(BF), piece(at, 2 * peer + 1).astype(BF)
                keep_ref[to, 16 * at : 16 * at + 16, :] = jnp.where(core == 0, one, two)
                send_ref[to, 16 * at : 16 * at + 16, :] = jnp.where(core == 0, two, one)
            keep_ref[to, 16 * G1_VEC : 16 * G1_VEC + 16, :] = vectors
            send_ref[to, 16 * G1_VEC : 16 * G1_VEC + 16, :] = vectors


def branch_kernel(
    placed, valid, x_ref, cat_ref, mix_ref, sums_ref, gm_ref, gfirst_ref, vec_ref, pk_ref,
    grad_ref, keep_ref, send_ref,
    wcat, wcat_f, dmix, spread, high_s, wide_s, a_cat, a_bias, a_gain1, a_bias1, grads,
):
    step, steps, count = pl.program_id(0), pl.num_programs(0) // 2, x_ref.shape[0]

    @pl.when(step == 0)
    def _():
        for k, weight in enumerate(branch_weights(pk_ref)):
            wcat[128 * k : 128 * k + 128, :] = weight
            wcat_f[128 * k : 128 * k + 128, :] = weight.astype(F32)
        for ref in (high_s, wide_s, a_cat, a_bias, a_gain1, a_bias1, grads):
            ref[...] = jnp.zeros(ref.shape, ref.dtype)

    def row(at, width=128):
        return vec_ref[at : at + 1, 0:width]

    @pl.when(step < steps)
    def _():
        biases = (row(V_BH), row(V_BW), jnp.zeros((1, 128), F32))
        for m in range(count):
            grad_mixed = gm_ref[step * count + m]
            outer = dot_tn(cat_ref[step * count + m], grad_mixed)
            total = jnp.sum(grad_mixed.astype(F32), axis=0, keepdims=True)
            for k in range(3):
                at = 8 * k + step * count + m
                part = outer[128 * k : 128 * k + 128, :]
                mixing = mix_ref[pl.ds(at, 1), :]
                share = jnp.sum(part * wcat_f[128 * k : 128 * k + 128, :], axis=0, keepdims=True)
                dmix[pl.ds(at, 1), :] = share + biases[k] * total
                a_cat[128 * k : 128 * k + 128, :] += part * mixing
                a_bias[k : k + 1, :] += mixing * total

    @pl.when(step == steps - 1)
    def _():
        vec = vec_ref[...]
        sums = [sums_ref[8 * k : 8 * k + 8, :] for k in range(3)]
        head = head_weights(pk_ref, vec)
        counts = count_column(valid)
        branches = [wcat[128 * k : 128 * k + 128, :] for k in range(3)]
        pooled, hidden, slope, mixing = head_forward(sums, counts, branches, head, vec)
        w_reduce, w_expand, _ = head
        grads_mix = [dmix[8 * k : 8 * k + 8, :] for k in range(3)]
        mean = sum(m * g for m, g in zip(mixing, grads_mix))
        grad_logits = [m * (g - mean) for m, g in zip(mixing, grads_mix)]
        grad_hidden = sum(dot_nt_high(g, w) for g, w in zip(grad_logits, w_expand))
        grad_pre = grad_hidden * slope
        grad_pooled = dot_nt_high(grad_pre, w_reduce)
        per_pixel = grad_pooled / counts
        unspread = spread_matrix()
        grads[0:128, :] = dot_nt_high(dot_tn_high(pooled, grad_pre), unspread.astype(F32))
        for b in range(3):
            grads[128 * (b + 1) : 128 * (b + 2), :] = sum(
                dot_nt_high(
                    dot_tn_high(hidden, grad_logits[k]),
                    pick_matrix(k)[128 * b : 128 * b + 128].astype(F32),
                )
                for k in range(3)
            )
            wide_row = sum(
                dot_nt_high(grad_logits[k], pick_matrix(k)[128 * b : 128 * b + 128].astype(F32))
                for k in range(3)
            )
            a_bias[4 + b : 5 + b, :] = jnp.sum(wide_row, axis=0, keepdims=True)
        a_bias[3:4, :] = jnp.sum(grad_pre, axis=0, keepdims=True)
        pooled_sum = jnp.sum(grad_pooled, axis=0, keepdims=True)
        for k in range(3):
            a_cat[128 * k : 128 * k + 128, :] += dot_tn_high(sums[k], per_pixel)
            a_bias[k : k + 1, :] += pooled_sum
            spread[8 * k : 8 * k + 8, :] = dot_nt_high(
                per_pixel, wcat_f[128 * k : 128 * k + 128, :]
            )

    @pl.when(step >= steps)
    def _():
        offsets = channel_offsets()
        forth, back_c = offsets == 1, offsets == -1
        for m in range(count):
            image = (step - steps) * count + m
            scaled = jnp.concatenate(
                [
                    (wcat_f[128 * k : 128 * k + 128, :] * mix_ref[pl.ds(8 * k + image, 1), :]).astype(BF)
                    for k in range(3)
                ],
                axis=0,
            )
            back = dot_nt(gm_ref[image], scaled)
            inside = inside_map(valid, image)
            parts = [
                back[:, 128 * k : 128 * k + 128].reshape(32, 32, 128)
                + inside * spread[pl.ds(8 * k + image, 1), :].reshape(1, 1, 128)
                for k in range(3)
            ]
            high_s[m, 1:33, :, :] = parts[0]
            wide_s[m, :, 8:40, :] = parts[1]
            high = jnp.where(
                forth, high_s[m, 0:32, :, :], jnp.where(back_c, high_s[m, 2:34, :, :], parts[0])
            )
            wide = jnp.where(
                forth, wide_s[m, :, 7:39, :], jnp.where(back_c, wide_s[m, :, 9:41, :], parts[1])
            )
            grad_ref[m] = (parts[2] + (high + wide)).reshape(1024, 128)
        pixels = 1024 * count
        grad_normed = grad_ref[...].reshape(pixels, 128)
        values = x_ref[...].reshape(pixels, 128).astype(F32)
        centre = values - lane_mean(values)
        scale = lax.rsqrt(lane_mean(centre * centre) + EPS)
        unit = centre * scale
        weighted = grad_normed * unit
        a_gain1[...] += fold8(weighted)
        a_bias1[...] += fold8(grad_normed)
        gain = row(V_GAIN1)
        scaled_grad = grad_normed * gain
        here = pl.ds((step - steps) * count, count)
        grad = gfirst_ref[here].reshape(pixels, 128) + scale * (
            scaled_grad - lane_mean(scaled_grad) - unit * lane_mean(weighted * gain)
        )
        grad_ref[...] = grad.reshape(count, 1024, 128)

    @pl.when(step == 2 * steps - 1)
    def _():
        chip, core = place_of(placed)[0:2]
        vectors = jnp.concatenate(
            [
                jnp.sum(a_gain1[...], axis=0, keepdims=True),
                jnp.sum(a_bias1[...], axis=0, keepdims=True),
                a_bias[0:2, :],
                a_bias[3:7, :],
                jnp.zeros((8, 128), F32),
            ],
            axis=0,
        ).astype(BF)

        def piece(at, shard):
            rows = slice(16 * shard, 16 * shard + 16)
            if at < G2_REDUCE:
                return a_cat[128 * at + 16 * shard : 128 * at + 16 * shard + 16, :]
            if at == G2_REDUCE:
                return grads[rows, :]
            return jnp.concatenate(
                [grads[128 * (b + 1) + 16 * shard : 128 * (b + 1) + 16 * shard + 4, :] for b in range(3)]
                + [jnp.zeros((4, 128), F32)],
                axis=0,
            )

        for peer in range(4):
            to = lax.bitwise_xor(chip, peer)
            for at in range(G2_BLOCKS - 1):
                one, two = piece(at, 2 * peer).astype(BF), piece(at, 2 * peer + 1).astype(BF)
                keep_ref[to, 16 * at : 16 * at + 16, :] = jnp.where(core == 0, one, two)
                send_ref[to, 16 * at : 16 * at + 16, :] = jnp.where(core == 0, two, one)
            keep_ref[to, 16 * G2_VEC : 16 * G2_VEC + 16, :] = vectors
            send_ref[to, 16 * G2_VEC : 16 * G2_VEC + 16, :] = vectors


def sds(shape, dtype):
    return jax.ShapeDtypeStruct(shape, dtype)


def whole(shape):
    return pl.BlockSpec(shape, lambda s: (0,) * len(shape))


def params(mega):
    return pltpu.CompilerParams(vmem_limit_bytes=mega * 1024 * 1024)


VMEM_SPEC = pl.BlockSpec(memory_space=pltpu.VMEM)


def in_vmem(value):
    return pltpu.with_memory_space_constraint(value, pltpu.VMEM)


def per_step(shape, index):
    return pl.BlockSpec(shape, lambda s: (index(s),) + (0,) * (len(shape) - 1))


def same(step):
    return step


MIXER_IMAGES, MLP_IMAGES, BRANCH_IMAGES = 2, 2, 2
MIXER_MB, MLP_MB, BRANCH_MB = 16, 40, 20


def run_mixer(placed, valid, x, mine, other):
    images, count = x.shape[0], MIXER_IMAGES
    return pl.pallas_call(
        functools.partial(mixer_kernel, placed),
        grid=(images // count,),
        in_specs=[VMEM_SPEC, per_step((count, 1024, 128), same), VMEM_SPEC, VMEM_SPEC],
        out_specs=[
            VMEM_SPEC, whole((24, 128)), whole((24, 128)), whole((16, 512)), VMEM_SPEC,
        ],
        out_shape=[
            pltpu.VMEM((images, 1024, 384), BF),
            sds((24, 128), F32),
            sds((24, 128), F32),
            sds((16, 512), F32),
            pltpu.VMEM((SHARDS, ROWS, 128), BF),
        ],
        scratch_shapes=[pltpu.VMEM((count, 34, 48, 128), F32)],
        compiler_params=params(MIXER_MB),
        name="mixer",
    )(valid, x, mine, other)


def run_mlp(placed, x, cat, mix, cot, vec, packed):
    images, count = x.shape[0], MLP_IMAGES
    pixels = 1024 * count
    g1 = (4, 16 * G1_BLOCKS, 128)
    maps = per_step((count, 1024, 128), same)
    shapes = [
        ((384, 128), BF), ((128, 128), BF), ((128, 512), BF), ((512, 128), BF), ((1152, 384), BF),
        ((32 * count, 32, 128), F32), ((count, 34, 48, 128), F32),
        ((pixels, 512), BF), ((pixels, 512), BF), ((pixels, 128), BF), ((pixels, 128), BF),
        ((pixels, 128), BF), ((pixels, 128), BF), ((256 * count, 1152), BF),
        ((count, 272, 384), BF), ((count, 272, 384), BF), ((264, 384), F32),
        ((1152, 384), F32), ((128, 512), F32), ((128, 512), F32), ((128, 128), F32),
        ((8, 384), F32), ((8, 512), F32), ((8, 128), F32), ((8, 128), F32), ((8, 128), F32), ((8, 128), F32),
    ]
    return pl.pallas_call(
        functools.partial(mlp_kernel, placed),
        grid=(images // count,),
        in_specs=[
            maps,
            VMEM_SPEC,
            whole((24, 128)),
            per_step((count, 256, 320), same),
            whole((16, 512)),
            VMEM_SPEC,
        ],
        out_specs=[per_step((count, 256, 320), same), VMEM_SPEC, VMEM_SPEC, whole(g1), whole(g1)],
        out_shape=[
            sds((images, 256, 320), BF),
            pltpu.VMEM((images, 1024, 128), F32),
            pltpu.VMEM((images, 1024, 128), BF),
            sds(g1, BF),
            sds(g1, BF),
        ],
        scratch_shapes=[pltpu.VMEM(*shape) for shape in shapes],
        compiler_params=params(MLP_MB),
        name="mlp",
    )(x, in_vmem(cat), mix, cot, vec, in_vmem(packed))


def run_branches(placed, valid, x, cat, mix, sums, gm, gfirst, vec, packed):
    images, count = x.shape[0], BRANCH_IMAGES
    steps = images // count
    g2 = (4, 16 * G2_BLOCKS, 128)
    late = per_step((count, 1024, 128), lambda s: jnp.maximum(s - steps, 0))
    shapes = [
        ((384, 128), BF), ((384, 128), F32), ((24, 128), F32), ((24, 128), F32),
        ((count, 34, 32, 128), F32), ((count, 32, 48, 128), F32), ((384, 128), F32),
        ((8, 128), F32), ((8, 128), F32), ((8, 128), F32), ((512, 128), F32),
    ]
    return pl.pallas_call(
        functools.partial(branch_kernel, placed),
        grid=(2 * steps,),
        in_specs=[
            VMEM_SPEC,
            late,
            VMEM_SPEC,
            whole((24, 128)),
            whole((24, 128)),
            VMEM_SPEC,
            VMEM_SPEC,
            whole((16, 512)),
            VMEM_SPEC,
        ],
        out_specs=[late, whole(g2), whole(g2)],
        out_shape=[sds((images, 1024, 128), F32), sds(g2, BF), sds(g2, BF)],
        scratch_shapes=[pltpu.VMEM(*shape) for shape in shapes],
        compiler_params=params(BRANCH_MB),
        name="branches",
    )(valid, x, in_vmem(cat), mix, sums, in_vmem(gm), in_vmem(gfirst), vec, in_vmem(packed))


def pack_weights(weights):
    return pl.pallas_call(
        pack_kernel,
        out_shape=sds((ROWS, 128), BF),
        in_specs=[VMEM_SPEC] * 21,
        out_specs=VMEM_SPEC,
        scratch_shapes=[pltpu.VMEM((16, 128), F32)],
        name="pack",
    )(*weights)


def sum_pair_kernel(keep, got, own, *rest):
    own[...] = keep[0].astype(F32) + got[0].astype(F32)
    for peer, out in enumerate(rest):
        out[...] = (keep[peer + 1].astype(F32) + got[peer + 1].astype(F32)).astype(BF)


def sum_four_kernel(own, one, two, three, total, low):
    value = own[...] + one[...].astype(F32) + two[...].astype(F32) + three[...].astype(F32)
    total[...] = value
    low[...] = value.astype(BF)


def reduce_tree(keep, send, shards, copies):
    rows = keep.shape[1]
    got = lax.ppermute(send, "fsdp", [(i, i ^ 1) for i in range(shards)])
    own, *others = pl.pallas_call(
        sum_pair_kernel,
        out_shape=[sds((rows, 128), F32)] + [sds((rows, 128), BF)] * 3,
        in_specs=[VMEM_SPEC] * 2,
        out_specs=[VMEM_SPEC] * 4,
        name="sum_pair",
    )(keep, got)
    moved = [
        lax.ppermute(value, "fsdp", [(i, i ^ (2 * (peer + 1))) for i in range(shards)])
        for peer, value in enumerate(others)
    ]
    total, low = pl.pallas_call(
        sum_four_kernel,
        out_shape=[sds((rows, 128), F32), sds((rows, 128), BF)],
        in_specs=[VMEM_SPEC] * 4,
        out_specs=[VMEM_SPEC] * 2,
        name="sum_four",
    )(own, *moved)
    return [total] + [
        lax.ppermute(low, "rep", [(i, (i + k) % copies) for i in range(copies)])
        for k in range(1, copies)
    ]


def finish_kernel(*refs):
    (one0, one1, one2, one3, two0, two1, two2, two3,
     gain_one, bias_one, w_h, b_h, w_w, b_w, w_c, w_red, b_red, w_exp, b_exp, w_proj, b_proj,
     gain_two, bias_two, w_up, b_up, w_down, b_down, w_conv, b_conv) = refs
    shard = lax.axis_index("fsdp")

    def first(at, rows=16):
        here = slice(16 * at, 16 * at + rows)
        return (one0[here, :] + one1[here, :].astype(F32)) + (
            one2[here, :].astype(F32) + one3[here, :].astype(F32)
        )

    def second(at, rows=16):
        here = slice(16 * at, 16 * at + rows)
        return (two0[here, :] + two1[here, :].astype(F32)) + (
            two2[here, :].astype(F32) + two3[here, :].astype(F32)
        )

    w_h[...] = second(G2_HEIGHT)
    w_w[...] = second(G2_WIDTH)
    w_c[...] = second(G2_CHANNEL)
    w_red[...] = second(G2_REDUCE)[:, 0:32]
    expand = second(G2_EXPAND)
    for b in range(3):
        w_exp[:, 128 * b : 128 * b + 128] = expand[4 * b : 4 * b + 4, :]
    w_proj[...] = first(G1_PROJ)
    for b in range(4):
        w_up[:, 128 * b : 128 * b + 128] = first(G1_UP + b)
    w_down[...] = first(G1_DOWN, 64)
    for at, tap in enumerate(TAPS):
        kernel = w_conv.at[tap // 3, tap % 3]
        for b in range(3):
            width = 128 if b < 2 else 64
            kernel[:, 128 * b : 128 * b + width] = first(G1_CONV + 3 * at + b)[:, 0:width]
    table_one, table_two = first(G1_VEC), second(G2_VEC)

    def share(table, row, blocks, length, stride):
        total = jnp.zeros((1, 128), F32)
        for b in range(blocks):
            pick = iota((128, 128), 0) + 128 * b == iota((128, 128), 1) + shard * stride
            total = total + dot_high(table, pick.astype(F32))[row + b : row + b + 1, :]
        return total[:, 0:length].reshape(length)

    gain_one[...] = share(table_two, G2_GAIN1, 1, 16, 16)
    bias_one[...] = share(table_two, G2_BIAS1, 1, 16, 16)
    b_h[...] = share(table_two, G2_BH, 1, 16, 16)
    b_w[...] = share(table_two, G2_BW, 1, 16, 16)
    b_red[...] = share(table_two, G2_BR, 1, 4, 16)
    b_exp[...] = share(table_two, G2_BE, 3, 48, 48)
    b_proj[...] = share(table_one, G1_BPROJ, 1, 16, 16)
    gain_two[...] = share(table_one, G1_GAIN2, 1, 16, 16)
    bias_two[...] = share(table_one, G1_BIAS2, 1, 16, 16)
    b_up[...] = share(table_one, G1_BUP, 4, 64, 64)
    b_down[...] = share(table_one, G1_BDOWN, 1, 16, 16)
    b_conv[...] = share(table_one, G1_BCONV, 3, 40, 40)


def finish(sums, weights):
    return pl.pallas_call(
        finish_kernel,
        out_shape=[sds(w.shape, F32) for w in weights],
        in_specs=[VMEM_SPEC] * 8,
        out_specs=[VMEM_SPEC] * 21,
        name="finish",
    )(*sums)


def compute(placed, input_map, valid_size, cotangent, mine, other):
    images = input_map.shape[0]
    x = input_map.reshape(images, 1024, 128)
    cot = cotangent.reshape(images, 256, 320)
    cat, mix, sums, vec, packed = run_mixer(placed, valid_size, x, mine, other)
    out, gfirst, gm, keep1, send1 = run_mlp(placed, x, cat, mix, cot, vec, packed)
    input_grad, keep2, send2 = run_branches(placed, valid_size, x, cat, mix, sums, gm, gfirst, vec, packed)
    return (
        out.reshape(images, 16, 16, 320),
        input_grad.reshape(images, 32, 32, 128),
        (keep1, send1, keep2, send2),
    )


def pack_whole(weights):
    (gain_one, bias_one, w_h, b_h, w_w, b_w, w_c, w_red, b_red, w_exp, b_exp, w_proj, b_proj,
     gain_two, bias_two, w_up, b_up, w_down, b_down, w_conv, b_conv) = weights

    def split(weight):
        weight = weight.reshape(SHARDS, weight.shape[0] // SHARDS, weight.shape[1])
        rows, cols = -weight.shape[1] % 16, -weight.shape[2] % 128
        weight = jnp.pad(weight, ((0, 0), (0, rows), (0, cols)))
        return [weight[:, :, at : at + 128] for at in range(0, weight.shape[2], 128)]

    pieces = split(w_h) + split(w_w) + split(w_c) + split(w_proj) + split(w_red) + split(w_exp)
    pieces = pieces + split(w_up) + split(w_down)
    for tap in TAPS:
        pieces = pieces + split(w_conv[tap // 3, tap % 3])
    vectors = (gain_one, bias_one, b_h, b_w, b_red, b_exp, b_proj, gain_two, bias_two, b_up, b_down, b_conv)
    rows = [
        jnp.pad(v.reshape(SHARDS, 1, v.shape[0] // SHARDS), ((0, 0), (0, 0), (0, 128 - v.shape[0] // SHARDS)))
        for v in vectors
    ]
    rows = rows + [jnp.zeros((SHARDS, 4, 128), BF)]
    return jnp.concatenate(pieces + [jnp.concatenate(rows, axis=1)], axis=1)


def unpack_whole(sums):
    one = jnp.stack([sums[0], sums[1]], axis=1).reshape(SHARDS, -1, 128).astype(F32)
    two = jnp.stack([sums[2], sums[3]], axis=1).reshape(SHARDS, -1, 128).astype(F32)

    def join(buffer, at, blocks, rows=16):
        parts = [buffer[:, 16 * (at + b) : 16 * (at + b) + rows, :] for b in range(blocks)]
        return jnp.concatenate(parts, axis=2).reshape(SHARDS * rows, 128 * blocks)

    def vector(buffer, at, row, blocks=1):
        return buffer[0, 16 * at + row : 16 * at + row + blocks, :].reshape(128 * blocks)

    expand = two[:, 16 * G2_EXPAND : 16 * G2_EXPAND + 12, :].reshape(SHARDS, 3, 4, 128)
    taps = [join(one, G1_CONV + 3 * TAPS.index(tap), 3)[:, 0:320] for tap in range(9)]
    return (
        vector(two, G2_VEC, G2_GAIN1),
        vector(two, G2_VEC, G2_BIAS1),
        join(two, G2_HEIGHT, 1),
        vector(two, G2_VEC, G2_BH),
        join(two, G2_WIDTH, 1),
        vector(two, G2_VEC, G2_BW),
        join(two, G2_CHANNEL, 1),
        join(two, G2_REDUCE, 1)[:, 0:32],
        vector(two, G2_VEC, G2_BR).reshape(SHARDS, 16)[:, 0:4].reshape(32),
        expand.transpose(0, 2, 1, 3).reshape(32, 384),
        vector(two, G2_VEC, G2_BE, 3),
        join(one, G1_PROJ, 1),
        vector(one, G1_VEC, G1_BPROJ),
        vector(one, G1_VEC, G1_GAIN2),
        vector(one, G1_VEC, G1_BIAS2),
        join(one, G1_UP, 4),
        vector(one, G1_VEC, G1_BUP, 4),
        one[:, 16 * G1_DOWN : 16 * G1_DOWN + 64, :].reshape(512, 128),
        vector(one, G1_VEC, G1_BDOWN),
        jnp.stack(taps).reshape(3, 3, 128, 320),
        vector(one, G1_VEC, G1_BCONV, 3)[0:320],
    )


def shards_of(mesh):
    shards, copies = mesh.shape["fsdp"], mesh.shape["rep"]

    def eight(input_map, valid_size, *rest):
        weights, cotangent = rest[:-1], rest[-1]
        groups = [list(range(core, shards, 2)) for core in range(2)]
        mine = lax.all_gather(pack_weights(weights), "fsdp", axis=0, axis_index_groups=groups)
        other = lax.ppermute(mine, "fsdp", [(i, i ^ 1) for i in range(shards)])
        out, input_grad, sums = compute(True, input_map, valid_size, cotangent, mine, other)
        one = reduce_tree(sums[0], sums[1], shards, copies)
        two = reduce_tree(sums[2], sums[3], shards, copies)
        return (out, input_grad) + tuple(finish(one + two, weights))

    def general(input_map, valid_size, *rest):
        weights, cotangent = rest[:-1], rest[-1]
        dims = [2 if w.ndim == 4 else 0 for w in weights]
        full = [lax.all_gather(w, "fsdp", axis=d, tiled=True) for w, d in zip(weights, dims)]
        packed = pack_whole(full)
        out, input_grad, sums = compute(
            False, input_map, valid_size, cotangent, packed[0::2], packed[1::2]
        )
        grads = [
            lax.psum_scatter(g, "fsdp", scatter_dimension=d, tiled=True)
            for g, d in zip(unpack_whole(sums), dims)
        ]
        return (out, input_grad) + tuple(lax.psum(grads, "rep"))

    return eight if shards == SHARDS and copies == 4 else general


def solution(mesh):
    maps = P(("rep", "fsdp"), None, None, None)
    vector, matrix = P("fsdp"), P("fsdp", None)
    weights = (
        vector, vector, matrix, vector, matrix, vector, matrix, matrix, vector, matrix, vector,
        matrix, vector, vector, vector, matrix, vector, matrix, vector,
        P(None, None, "fsdp", None), vector,
    )
    return jax.shard_map(
        shards_of(mesh),
        mesh=mesh,
        in_specs=(maps, P(("rep", "fsdp"), None)) + weights + (maps,),
        out_specs=(maps, maps) + weights,
        check_vma=False,
    )
```

```python
import functools

import jax
import jax.numpy as jnp
from jax import lax
from jax.experimental import pallas as pl
from jax.experimental.pallas import tpu as pltpu
from jax.sharding import PartitionSpec as P

BF = jnp.bfloat16
F32 = jnp.float32
HIGH = lax.Precision.HIGHEST
EPS = 1e-05

SHARDS = 8
B_HEIGHT, B_WIDTH, B_CHANNEL, B_PROJ, B_REDUCE = 0, 1, 2, 3, 4
B_EXPAND, B_UP, B_DOWN, B_CONV, B_VEC = 5, 8, 12, 16, 43
BLOCKS = 44
ROWS = 16 * BLOCKS
TAPS = (4, 5, 7, 8, 3, 6, 1, 2, 0)
(V_GAIN1, V_BIAS1, V_BH, V_BW, V_BR, V_BE, V_BP, V_GAIN2, V_BIAS2, V_BUP, V_BDOWN, V_BCONV) = range(12)
LENGTHS = (16, 16, 16, 16, 4, 48, 16, 16, 16, 64, 16, 40)
G1_CONV, G1_EDGE, G1_UP, G1_DOWN, G1_PROJ, G1_VEC, G1_VEC_LOW, G1_BLOCKS = 0, 18, 23, 27, 31, 32, 33, 34
G1_BCONV, G1_BUP, G1_BDOWN, G1_BPROJ, G1_GAIN2, G1_BIAS2 = 0, 3, 7, 8, 9, 10
G2_HEIGHT, G2_WIDTH, G2_CHANNEL, G2_REDUCE, G2_EXPAND, G2_VEC, G2_BLOCKS = 0, 1, 2, 3, 4, 5, 6
G2_GAIN1, G2_BIAS1, G2_BH, G2_BW, G2_BR, G2_BE = 0, 1, 2, 3, 4, 5


def iota(shape, axis):
    return lax.broadcasted_iota(jnp.int32, shape, axis)


def dot(left, right):
    return jnp.dot(left, right, preferred_element_type=F32)


def dot_nt(left, right):
    return lax.dot_general(left, right, (((1,), (1,)), ((), ())), preferred_element_type=F32)


def dot_tn(left, right):
    return lax.dot_general(left, right, (((0,), (0,)), ((), ())), preferred_element_type=F32)


def dot_high(left, right):
    return jnp.dot(left, right, preferred_element_type=F32, precision=HIGH)


def dot_nt_high(left, right):
    return lax.dot_general(
        left, right, (((1,), (1,)), ((), ())), preferred_element_type=F32, precision=HIGH
    )


def dot_tn_high(left, right):
    return lax.dot_general(
        left, right, (((0,), (0,)), ((), ())), preferred_element_type=F32, precision=HIGH
    )


def fold8(values):
    rows, cols = values.shape
    return jnp.sum(values.reshape(rows // 8, 8, cols), axis=0)


def lane_mean(values):
    return jnp.mean(values, axis=-1, keepdims=True)


def gelu_both(values):
    cdf = 0.5 + 0.5 * lax.erf(values * 0.7071067811865476)
    slope = cdf + values * (jnp.exp(-0.5 * (values * values)) * 0.3989422804014327)
    return values * cdf, slope


def split_low(values):
    high = values.astype(BF).astype(F32)
    return high, (values - high).astype(BF).astype(F32)


def block(packed, at):
    return packed[:, 16 * at : 16 * at + 16, :].reshape(128, 128)


def branch_weights(packed):
    return [block(packed, at) for at in (B_HEIGHT, B_WIDTH, B_CHANNEL)]


def spread_matrix():
    unit, lane = iota((128, 128), 0), iota((128, 128), 1)
    return ((lane == 16 * (unit // 4) + unit % 4) & (unit < 32)).astype(BF)


def pick_matrix(k):
    return (iota((384, 128), 0) == 3 * iota((384, 128), 1) + k).astype(BF)


def head_weights(packed, vec):
    w_reduce = dot(block(packed, B_REDUCE), spread_matrix())
    expand = jnp.concatenate([block(packed, B_EXPAND + b) for b in range(3)], axis=1)
    picks = jnp.concatenate([pick_matrix(k) for k in range(3)], axis=1)
    w_expand = dot(expand, picks)
    b_expand = dot(vec[:, 0:384].astype(BF), picks)[V_BE : V_BE + 1, :]
    return w_reduce, w_expand, b_expand


def head_forward(sums, counts, branches, head, vec):
    w_reduce, w_expand, b_expand = head
    pooled = dot_high(jnp.concatenate(sums, axis=1), branches.astype(F32)) / counts
    pooled = pooled + (vec[V_BH : V_BH + 1, 0:128] + vec[V_BW : V_BW + 1, 0:128])
    pre = dot_high(pooled, w_reduce) + vec[V_BR : V_BR + 1, 0:128]
    hidden, slope = gelu_both(pre)
    joined = dot_high(hidden, w_expand) + b_expand
    logits = [joined[:, 128 * k : 128 * k + 128] for k in range(3)]
    top = jnp.maximum(jnp.maximum(logits[0], logits[1]), logits[2])
    powers = [jnp.exp(v - top) for v in logits]
    total = powers[0] + powers[1] + powers[2]
    return pooled, hidden, slope, [v / total for v in powers]


def column(row_values):
    stacked = jnp.where(iota((8, 128), 0) == 0, row_values, 0.0)
    return dot_tn(stacked.astype(BF), jnp.ones((8, 128), BF))


def inside_counts(valid_ref):
    high, wide = valid_ref[:, 0:1].astype(F32), valid_ref[:, 1:2].astype(F32)
    offsets = jnp.broadcast_to(channel_offsets()[0, 0:1, :], (8, 128))

    def kept(size):
        full = jnp.broadcast_to(size, (8, 128))
        return full - jnp.where(offsets == 1, jnp.where(full == 32.0, 1.0, 0.0), 0.0) - jnp.where(
            offsets == -1, 1.0, 0.0
        )

    return [kept(high) * wide, kept(wide) * high, jnp.broadcast_to(high * wide, (8, 128))]


def count_column(valid_ref):
    return (valid_ref[:, 0:1] * valid_ref[:, 1:2]).astype(F32)


def channel_offsets():
    return (iota((1, 32, 128), 2) + 1) % 3 - 1


def shifted_masks(valid_ref, image):
    size = valid_ref[pl.ds(image, 1), :]
    masks = []
    for axis, shape in ((0, (32, 1, 128)), (1, (1, 32, 128))):
        limit = size[:, axis : axis + 1].reshape(1, 1, 1)
        at = iota(shape, axis)
        taker = at - ((iota(shape, 2) + 1) % 3 - 1)
        masks.append((at < limit).astype(F32))
        masks.append(((taker >= 0) & (taker < limit)).astype(F32))
    return masks


def class_sums(maps, masks):
    row, row_taker, col, col_taker = masks

    def by_row(mask):
        return jnp.sum((maps * mask).reshape(32, 4, 8, 128), axis=1)

    plain, taken = by_row(col), by_row(col_taker)
    return [
        jnp.sum(jnp.sum(rows * mask, axis=0), axis=0, keepdims=True)
        for rows, mask in ((plain, row_taker), (taken, row), (plain, row))
    ]


def place_of(placed):
    if not placed:
        return 0, 0
    shard = lax.axis_index("fsdp")
    return shard // 2, lax.rem(shard, 2)


def pack_kernel(*refs):
    (gain_one, bias_one, w_h, b_h, w_w, b_w, w_c, w_red, b_red, w_exp, b_exp, w_proj, b_proj,
     gain_two, bias_two, w_up, b_up, w_down, b_down, w_conv, b_conv, out, vec) = refs

    def put(at, values):
        out[16 * at : 16 * at + values.shape[0], 0 : values.shape[1]] = values

    put(B_HEIGHT, w_h[...])
    put(B_WIDTH, w_w[...])
    put(B_CHANNEL, w_c[...])
    put(B_PROJ, w_proj[...])
    blank = jnp.zeros((16, 128), BF)
    put(B_REDUCE, blank)
    put(B_REDUCE, w_red[...])
    for b in range(3):
        vec[...] = jnp.zeros((16, 128), F32)
        vec[0:4, :] = w_exp[:, 128 * b : 128 * b + 128].astype(F32)
        put(B_EXPAND + b, vec[...].astype(BF))
    for b in range(4):
        put(B_UP + b, w_up[:, 128 * b : 128 * b + 128])
    put(B_DOWN, w_down[...])
    for at, tap in enumerate(TAPS):
        kernel = w_conv.at[tap // 3, tap % 3]
        put(B_CONV + 3 * at, kernel[:, 0:128])
        put(B_CONV + 3 * at + 1, kernel[:, 128:256])
        put(B_CONV + 3 * at + 2, blank)
        put(B_CONV + 3 * at + 2, kernel[:, 256:320])
    vec[...] = jnp.zeros((16, 128), F32)
    vectors = (gain_one, bias_one, b_h, b_w, b_red, b_exp, b_proj, gain_two, bias_two, b_up, b_down, b_conv)
    for row, (values, length) in enumerate(zip(vectors, LENGTHS)):
        vec[row : row + 1, 0:length] = values[...].astype(F32).reshape(1, length)
    put(B_VEC, vec[...].astype(BF))


def vector_table(packed):
    shards = packed[:, 16 * B_VEC : 16 * B_VEC + 16, :].reshape(128, 128)
    table = jnp.zeros((16, 512), F32)
    rows = iota((16, 512), 0)
    for length in (16, 4, 48, 64, 40):
        step = 16 if length == 4 else length
        lane = iota((128, 512), 1)
        source = iota((128, 512), 0)
        pick = ((source == lane % step) & (source < length)).astype(BF)
        spread = dot(shards, pick)
        mine = (source // 16) == (lane // step)
        whole = jnp.sum(jnp.where(mine, spread, 0.0).reshape(8, 16, 512), axis=0)
        held = functools.reduce(
            jnp.logical_or, [rows == v for v, size in enumerate(LENGTHS) if size == length]
        )
        table = jnp.where(held, whole, table)
    return table


def unit_kernel(valid, x_ref, unit_ref, low_ref, sums_ref):
    step, count = pl.program_id(0), x_ref.shape[0]
    values = x_ref[...].reshape(count * 1024, 128).astype(F32)
    centre = values - lane_mean(values)
    scale = lax.rsqrt(lane_mean(centre * centre) + EPS)
    unit = centre * scale
    here = pl.ds(step * count, count)
    unit_ref[here] = unit.reshape(count, 1024, 128)
    low_ref[here] = unit.astype(BF).reshape(count, 1024, 128)
    for m in range(count):
        image = step * count + m
        maps = unit[1024 * m : 1024 * m + 1024].reshape(32, 32, 128)
        for k, total in enumerate(class_sums(maps, shifted_masks(valid, image))):
            sums_ref[pl.ds(8 * k + image, 1), :] = total


def norm_kernel(
    placed, valid, unit_ref, mine, other, norm_ref, sums_ref, mix_ref, vec_ref, pk_ref
):
    step, steps, count = pl.program_id(0), pl.num_programs(0), unit_ref.shape[0]

    @pl.when(step == 0)
    def _():
        chip, core = place_of(placed)
        for peer in range(4):
            shard = 2 * lax.bitwise_xor(chip, peer)
            pk_ref[shard + core] = mine[peer]
            pk_ref[shard + (1 - core)] = other[peer]
        vec_ref[...] = vector_table(pk_ref)

    gain = vec_ref[V_GAIN1 : V_GAIN1 + 1, 0:128]
    bias = vec_ref[V_BIAS1 : V_BIAS1 + 1, 0:128]
    for m in range(count):
        image = step * count + m
        low = (unit_ref[m] * gain + bias).astype(BF)
        norm_ref[image] = low
        maps = low.astype(F32).reshape(32, 32, 128)
        for k, total in enumerate(class_sums(maps, shifted_masks(valid, image))):
            sums_ref[pl.ds(8 * k + image, 1), :] = total

    @pl.when(step == steps - 1)
    def _():
        vec = vec_ref[...]
        sums = [sums_ref[8 * k : 8 * k + 8, :] for k in range(3)]
        head = head_weights(pk_ref, vec)
        branches = jnp.concatenate(branch_weights(pk_ref), axis=0)
        mixing = head_forward(sums, count_column(valid), branches, head, vec)[3]
        for k in range(3):
            mix_ref[8 * k : 8 * k + 8, :] = mixing[k]


def mlp_kernel(
    placed, x_ref, norm_ref, mix_ref, cot_ref, vec_ref, pk_ref,
    pm_ref, gfirst_ref, gcat_ref, dmix_ref, keep_ref, send_ref,
    wcat, wproj, wup, wdown, wconv,
    gsec, low, act, ghid, norm2, mixes, mixed_s, gtail, gbranch, npad, gpad, cotp, cots, cotf,
    a_conv, a_up, a_down, a_proj, a_bconv, a_bup, a_bdown, a_bproj, a_gain2, a_bias2,
):
    step, steps, count = pl.program_id(0), pl.num_programs(0), x_ref.shape[0]

    @pl.when(step == 0)
    def _():
        for k, weight in enumerate(branch_weights(pk_ref)):
            wcat[128 * k : 128 * k + 128, :] = weight
        wproj[...] = block(pk_ref, B_PROJ)
        for b in range(4):
            wup[:, 128 * b : 128 * b + 128] = block(pk_ref, B_UP + b)
        wdown[...] = pk_ref[:, 16 * B_DOWN : 16 * B_DOWN + 64, :].reshape(512, 128)
        for at in range(9):
            for b in range(3):
                wconv[128 * at : 128 * at + 128, 128 * b : 128 * b + 128] = block(
                    pk_ref, B_CONV + 3 * at + b
                )
        for ref in (low, npad, gpad, cotp, cots, cotf, a_conv, a_up, a_down, a_proj, a_bconv, a_bup,
                    a_bdown, a_bproj, a_gain2, a_bias2):
            ref[...] = jnp.zeros(ref.shape, ref.dtype)

    def row(at, width=128):
        return vec_ref[at : at + 1, 0:width]

    images = range(count)
    maps = [step * count + m for m in images]
    pixels = [slice(1024 * m, 1024 * m + 1024) for m in images]

    offsets = channel_offsets()
    forth, back = offsets == 1, offsets == -1
    for m in images:
        mixing = [mix_ref[pl.ds(8 * k + maps[m], 1), :] for k in range(3)]
        biases = (row(V_BH), row(V_BW), 0.0)
        normed = norm_ref[maps[m]]
        here = normed.astype(F32).reshape(32, 32, 128)
        npad[m, 1:33, 8:40, :] = here
        high = jnp.where(
            forth, npad[m, 2:34, 8:40, :], jnp.where(back, npad[m, 0:32, 8:40, :], here)
        )
        wide = jnp.where(
            forth, npad[m, 1:33, 9:41, :], jnp.where(back, npad[m, 1:33, 7:39, :], here)
        )
        shifted = (high.reshape(1024, 128).astype(BF), wide.reshape(1024, 128).astype(BF), normed)
        mixed = 0.0
        for k in range(3):
            branch = dot(shifted[k], wcat[128 * k : 128 * k + 128, :]) + biases[k]
            mixes[pixels[m], 128 * k : 128 * k + 128] = branch
            mixed = mixed + branch * mixing[k]
        mixed_s[pixels[m], :] = mixed.astype(BF)
    first, unit, scale = [None] * count, [None] * count, [None] * count
    for m in images:
        added = dot(mixed_s[pixels[m], :], wproj[...]) + row(V_BP)
        first[m] = x_ref[m].astype(F32) + added
        centre = first[m] - lane_mean(first[m])
        scale[m] = lax.rsqrt(lane_mean(centre * centre) + EPS)
        unit[m] = centre * scale[m]
        norm2[pixels[m], :] = (unit[m] * row(V_GAIN2) + row(V_BIAS2)).astype(BF)

    for m in images:
        cot = cot_ref[m]
        cotp[m, 0:256, 0:320] = cot
        cotf[0:256, 0:320] = cot.astype(F32)
        ahead = cotf[1:257, :]
        ahead = jnp.where(iota(ahead.shape, 0) % 16 == 15, 0.0, ahead)
        cots[m, 0:256, :] = ahead.astype(BF)
        a_bconv[...] += fold8(cotf[0:256, :])
    flat = (count * 256, 384)
    cot_here, cot_right = cotp[:, 0:256, :].reshape(flat), cots[:, 0:256, :].reshape(flat)
    cot_below, cot_both = cotp[:, 16:272, :].reshape(flat), cots[:, 16:272, :].reshape(flat)
    pair_a = dot_nt(cot_here, wconv[0:256, :])
    pair_b = dot_nt(cot_here, wconv[256:512, :])
    pair_c = dot_nt(cot_right, wconv[512:768, :])
    pair_d = dot_nt(cot_below, wconv[768:1024, :])
    last = dot_nt(cot_both, wconv[1024:1152, :])
    planes = (
        (pair_a[:, 0:128], pair_a[:, 128:256] + pair_c[:, 0:128]),
        (
            pair_b[:, 0:128] + pair_d[:, 0:128],
            pair_b[:, 128:256] + pair_c[:, 128:256] + pair_d[:, 128:256] + last,
        ),
    )
    for p in range(2):
        for s in range(2):
            plane = planes[p][s]
            for i in range(16 * count):
                gsec[2 * i + p, pl.ds(s, 16, stride=2), :] = plane[16 * i : 16 * i + 16, :]

    grad_second = [gsec[32 * m : 32 * m + 32].reshape(1024, 128) for m in images]
    for m in images:
        tail = grad_second[m].astype(BF)
        gtail[pixels[m], :] = tail
        a_bdown[...] += fold8(grad_second[m])
        for b in range(2):
            cols = slice(256 * b, 256 * b + 256)
            hidden = dot(norm2[pixels[m], :], wup[:, cols]) + vec_ref[V_BUP : V_BUP + 1, cols]
            grad_act = dot_nt(tail, wdown[cols, :])
            value, slope = gelu_both(hidden)
            act[pixels[m], cols] = value.astype(BF)
            grad_hidden = grad_act * slope
            ghid[pixels[m], cols] = grad_hidden.astype(BF)
            a_bup[:, cols] += fold8(grad_hidden)
    grad_first = [None] * count
    for m in images:
        second = first[m] + (dot(act[pixels[m], :], wdown[...]) + row(V_BDOWN))
        low[m, 1:33, 8:40, :] = second.reshape(32, 32, 128)
        grad_normed = dot_nt(ghid[pixels[m], :], wup[...])
        a_gain2[...] += fold8(grad_normed * unit[m])
        a_bias2[...] += fold8(grad_normed)
        scaled_grad = grad_normed * row(V_GAIN2)
        grad_first[m] = grad_second[m] + scale[m] * (
            scaled_grad - lane_mean(scaled_grad) - unit[m] * lane_mean(scaled_grad * unit[m])
        )
        gfirst_ref[maps[m]] = grad_first[m]
        gbranch[pixels[m], :] = grad_first[m].astype(BF)
        a_bproj[...] += fold8(grad_first[m])
    here = pl.ds(step * count, count)
    a_up[...] += dot_tn(norm2[...], ghid[...])
    a_down[...] += dot_tn(gtail[...], act[...])
    for m in images:
        grad_mixed = dot_nt(gbranch[pixels[m], :], wproj[...])
        for k in range(3):
            share = fold8(grad_mixed * mixes[pixels[m], 128 * k : 128 * k + 128])
            dmix_ref[pl.ds(8 * k + maps[m], 1), :] = jnp.sum(share, axis=0, keepdims=True)
        gpad[m, :, 8:40, :] = grad_mixed.reshape(32, 32, 128)
        low_grad, image = grad_mixed.astype(BF), maps[m]
        gcat_ref[image, :, 0:128] = low_grad
        gcat_ref[image, 0:32, 128:256] = jnp.zeros((32, 128), BF)
        gcat_ref[image, 32:1024, 128:256] = low_grad[0:992]
        gcat_ref[image, 0:992, 256:384] = low_grad[32:1024]
        gcat_ref[image, 992:1024, 256:384] = jnp.zeros((32, 128), BF)
        gcat_ref[image, :, 384:512] = gpad[m, :, 7:39, :].reshape(1024, 128).astype(BF)
        gcat_ref[image, :, 512:640] = gpad[m, :, 9:41, :].reshape(1024, 128).astype(BF)
    a_proj[...] += dot_tn(mixed_s[...], gbranch[...])

    for at, tap in enumerate(TAPS):
        r, s = tap // 3, tap % 3
        for m in images:
            patch = low[m, pl.ds(r, 16, stride=2), pl.ds(7 + s, 16, stride=2), :]
            pm_ref[maps[m], :, 128 * at : 128 * at + 128] = patch.reshape(256, 128).astype(BF)
    a_conv[...] += dot_tn(pm_ref[here].reshape(256 * count, 1152), cot_here)

    @pl.when(step == steps - 1)
    def _():
        chip, core = place_of(placed)[0:2]
        vectors = jnp.concatenate(
            [jnp.sum(a_bconv[:, 128 * b : 128 * b + 128], axis=0, keepdims=True) for b in range(3)]
            + [jnp.sum(a_bup[:, 128 * b : 128 * b + 128], axis=0, keepdims=True) for b in range(4)]
            + [jnp.sum(ref[...], axis=0, keepdims=True) for ref in (a_bdown, a_bproj, a_gain2, a_bias2)]
            + [jnp.zeros((5, 128), F32)],
            axis=0,
        )
        vectors, vectors_low = split_low(vectors)
        down = [a_down[:, 128 * b : 128 * b + 128].T for b in range(4)]

        def piece(at, shard):
            rows = slice(16 * shard, 16 * shard + 16)
            if at < G1_EDGE:
                start = 128 * (at // 2) + 16 * shard
                return a_conv[start : start + 16, 128 * (at % 2) : 128 * (at % 2) + 128]
            if at < G1_UP:
                start = 256 * (at - G1_EDGE) + 16 * shard
                one = a_conv[start : start + 16, 256:320]
                if at == G1_UP - 1:
                    return jnp.concatenate([one, jnp.zeros((16, 64), F32)], axis=1)
                return jnp.concatenate([one, a_conv[start + 128 : start + 144, 256:320]], axis=1)
            if at < G1_DOWN:
                b = at - G1_UP
                return a_up[rows, 128 * b : 128 * b + 128]
            if at < G1_PROJ:
                start = 64 * (shard % 2) + 16 * (at - G1_DOWN)
                return down[shard // 2][start : start + 16, :]
            return a_proj[rows, :]

        for peer in range(4):
            to = lax.bitwise_xor(chip, peer)
            for at in range(G1_VEC):
                one, two = piece(at, 2 * peer), piece(at, 2 * peer + 1)
                keep_ref[to, 16 * at : 16 * at + 16, :] = jnp.where(core == 0, one, two)
                send_ref[to, 16 * at : 16 * at + 16, :] = jnp.where(core == 0, two, one).astype(BF)
            for at, values in ((G1_VEC, vectors), (G1_VEC_LOW, vectors_low)):
                keep_ref[to, 16 * at : 16 * at + 16, :] = values
                send_ref[to, 16 * at : 16 * at + 16, :] = values.astype(BF)


def branch_kernel(
    placed, valid, unit_ref, mix_ref, sums_ref, units_ref, gcat_ref, dmix_ref, vec_ref, pk_ref,
    spread_ref, keep_ref, send_ref,
    wcat, a_cat, a_edge, grads,
):
    step, steps, count = pl.program_id(0), pl.num_programs(0), unit_ref.shape[0]

    @pl.when(step == 0)
    def _():
        for k, weight in enumerate(branch_weights(pk_ref)):
            wcat[128 * k : 128 * k + 128, :] = weight.astype(F32)
        for ref in (a_cat, a_edge):
            ref[...] = jnp.zeros(ref.shape, ref.dtype)

    def row(at, width=128):
        return vec_ref[at : at + 1, 0:width]

    offsets = (iota((128, 128), 0) + 1) % 3 - 1
    for m in range(count):
        outer = dot_tn(unit_ref[m], gcat_ref[m])
        plain = outer[:, 0:128]
        parts = (
            jnp.where(offsets == 1, outer[:, 128:256], jnp.where(offsets == -1, outer[:, 256:384], plain)),
            jnp.where(offsets == 1, outer[:, 384:512], jnp.where(offsets == -1, outer[:, 512:640], plain)),
            plain,
        )
        maps = gcat_ref[m, :, 0:128].astype(F32).reshape(32, 32, 128)
        by_column = jnp.sum(maps, axis=0)
        total = jnp.sum(by_column, axis=0, keepdims=True)
        left, right = by_column[0:1], by_column[31:32]
        upper = jnp.sum(maps[0], axis=0, keepdims=True)
        lower = jnp.sum(maps[31], axis=0, keepdims=True)
        for k in range(3):
            at = 8 * k + step * count + m
            part = parts[k]
            mixing = mix_ref[pl.ds(at, 1), :]
            a_cat[128 * k : 128 * k + 128, :] += part * mixing
            a_edge[k : k + 1, :] += mixing * total
            if k == 0:
                a_edge[3:4, :] += mixing * lower
                a_edge[4:5, :] += mixing * upper
            if k == 1:
                a_edge[5:6, :] += mixing * right
                a_edge[6:7, :] += mixing * left

    @pl.when(step == steps - 1)
    def _():
        vec = vec_ref[...]
        head = head_weights(pk_ref, vec)
        counts = count_column(valid)
        sums = [sums_ref[8 * k : 8 * k + 8, :] for k in range(3)]
        pooled, hidden, slope, mixing = head_forward(sums, counts, wcat[...], head, vec)
        w_reduce, w_expand, _ = head
        grads_mix = [dmix_ref[8 * k : 8 * k + 8, :] for k in range(3)]
        mean = sum(m * g for m, g in zip(mixing, grads_mix))
        grad_logits = jnp.concatenate([m * (g - mean) for m, g in zip(mixing, grads_mix)], axis=1)
        grad_pre = dot_nt_high(grad_logits, w_expand) * slope
        grad_pooled = dot_nt_high(grad_pre, w_reduce)
        per_pixel = grad_pooled / counts
        spread = dot_nt_high(per_pixel, wcat[...])
        for k in range(3):
            spread_ref[8 * k : 8 * k + 8, :] = spread[:, 128 * k : 128 * k + 128]
        grads[:, 0:128] = dot_nt(dot_tn_high(pooled, grad_pre).astype(BF), spread_matrix())
        picks = jnp.concatenate([pick_matrix(k) for k in range(3)], axis=1)
        grads[:, 128:512] = dot_nt(dot_tn_high(hidden, grad_logits).astype(BF), picks)
        expand_bias = dot_nt_high(jnp.sum(grad_logits, axis=0, keepdims=True), picks.astype(F32))
        reduce_bias = jnp.sum(grad_pre, axis=0, keepdims=True)
        pooled_sum = jnp.sum(grad_pooled, axis=0, keepdims=True)
        gain, bias = column(row(V_GAIN1)), column(row(V_BIAS1))
        unit_sums = jnp.concatenate([units_ref[8 * k : 8 * k + 8, :] for k in range(3)], axis=1)
        unit_part = a_cat[...] + dot_tn_high(unit_sums, per_pixel)
        edge_part = dot_tn_high(jnp.concatenate(inside_counts(valid), axis=1), per_pixel)
        to_gain, to_bias = jnp.zeros((128, 128), F32), jnp.zeros((128, 128), F32)
        for k in range(3):
            here = slice(128 * k, 128 * k + 128)
            edges = edge_part[here] + a_edge[k : k + 1, :]
            if k < 2:
                edges = edges - jnp.where(offsets == 1, a_edge[2 * k + 3 : 2 * k + 4, :], 0.0)
                edges = edges - jnp.where(offsets == -1, a_edge[2 * k + 4 : 2 * k + 5, :], 0.0)
            to_gain = to_gain + unit_part[here] * wcat[here, :]
            to_bias = to_bias + edges * wcat[here, :]
            a_cat[here, :] = gain * unit_part[here] + bias * edges
        ones = jnp.ones((8, 128), F32)
        chip, core = place_of(placed)
        vectors = jnp.concatenate(
            [
                dot_nt_high(ones, to_gain)[0:1],
                dot_nt_high(ones, to_bias)[0:1],
                a_edge[0:1, :] + pooled_sum,
                a_edge[1:2, :] + pooled_sum,
                reduce_bias,
                expand_bias[:, 0:128],
                expand_bias[:, 128:256],
                expand_bias[:, 256:384],
            ],
            axis=0,
        )
        vectors = jnp.concatenate(split_low(vectors), axis=0)
        reduce_high, reduce_low = split_low(grads[:, 0:32])
        grads[:, 0:32] = reduce_high
        grads[:, 32:64] = reduce_low

        def piece(at, shard):
            rows = slice(16 * shard, 16 * shard + 16)
            if at < G2_REDUCE:
                return a_cat[128 * at + 16 * shard : 128 * at + 16 * shard + 16, :]
            if at == G2_REDUCE:
                return grads[rows, 0:128]
            return jnp.concatenate(
                [grads[16 * shard : 16 * shard + 4, 128 * b : 128 * b + 128] for b in range(1, 4)]
                + [jnp.zeros((4, 128), F32)],
                axis=0,
            )

        for peer in range(4):
            to = lax.bitwise_xor(chip, peer)
            for at in range(G2_VEC):
                one, two = piece(at, 2 * peer), piece(at, 2 * peer + 1)
                keep_ref[to, 16 * at : 16 * at + 16, :] = jnp.where(core == 0, one, two)
                send_ref[to, 16 * at : 16 * at + 16, :] = jnp.where(core == 0, two, one).astype(BF)
            keep_ref[to, 16 * G2_VEC : 16 * G2_VEC + 16, :] = vectors
            send_ref[to, 16 * G2_VEC : 16 * G2_VEC + 16, :] = vectors.astype(BF)


def input_kernel(
    valid, x_ref, mix_ref, spread, gcat_ref, gfirst_ref, vec_ref, pk_ref, after, grad_ref, wcat
):
    step, count = pl.program_id(0), x_ref.shape[0]

    @pl.when(step == 0)
    def _():
        offsets = (iota((128, 128), 0) + 1) % 3 - 1
        height, width, channel = [weight.astype(F32) for weight in branch_weights(pk_ref)]
        for at, (weight, offset) in enumerate(
            ((height, 0), (height, 1), (height, -1), (width, 0), (width, 1), (width, -1))
        ):
            wcat[:, 128 * at : 128 * at + 128] = jnp.where(offsets == offset, weight, 0.0)
        wcat[:, 768:896] = channel

    for m in range(count):
        image = step * count + m
        by_height, by_width, by_channel = [mix_ref[pl.ds(8 * k + image, 1), :] for k in range(3)]
        scaled = jnp.concatenate(
            [
                wcat[:, 0:128] * by_height + wcat[:, 384:512] * by_width + wcat[:, 768:896] * by_channel,
                wcat[:, 128:256] * by_height,
                wcat[:, 256:384] * by_height,
                wcat[:, 512:640] * by_width,
                wcat[:, 640:768] * by_width,
            ],
            axis=1,
        ).astype(BF)
        row, row_taker, col, col_taker = shifted_masks(valid, image)
        high, wide, plain = [spread[pl.ds(8 * k + image, 1), :].reshape(1, 1, 128) for k in range(3)]
        even = row * (col_taker * wide + col * plain) + row_taker * (col * high)
        grad_ref[m] = dot_nt(gcat_ref[m], scaled) + even.reshape(1024, 128)
    pixels = 1024 * count
    scaled_grad = grad_ref[...].reshape(pixels, 128) * vec_ref[V_GAIN1 : V_GAIN1 + 1, 0:128]
    values = x_ref[...].reshape(pixels, 128).astype(F32)
    centre = values - lane_mean(values)
    scale = lax.rsqrt(lane_mean(centre * centre) + EPS)
    unit = centre * scale
    grad = gfirst_ref[...].reshape(pixels, 128) + scale * (
        scaled_grad - lane_mean(scaled_grad) - unit * lane_mean(scaled_grad * unit)
    )
    grad_ref[...] = grad.reshape(count, 1024, 128)


def conv_kernel(pm_ref, vec_ref, pk_ref, after, map_ref, wconv):
    @pl.when(pl.program_id(0) == 0)
    def _():
        for at in range(9):
            for b in range(3):
                wconv[128 * at : 128 * at + 128, 128 * b : 128 * b + 128] = block(
                    pk_ref, B_CONV + 3 * at + b
                )

    count = pm_ref.shape[0]
    out = dot(pm_ref[...].reshape(256 * count, 1152), wconv[...])
    out = out + vec_ref[V_BCONV : V_BCONV + 1, 0:384]
    map_ref[...] = out[:, 0:320].astype(BF).reshape(count, 256, 320)


def sds(shape, dtype):
    return jax.ShapeDtypeStruct(shape, dtype)


def whole(shape):
    return pl.BlockSpec(shape, lambda s: (0,) * len(shape))


def params(mega):
    return pltpu.CompilerParams(vmem_limit_bytes=mega * 1024 * 1024)


def cost(microseconds):
    return pl.CostEstimate(
        flops=int(microseconds * 3e8), bytes_accessed=int(microseconds * 3e6), transcendentals=0
    )


VMEM_SPEC = pl.BlockSpec(memory_space=pltpu.VMEM)
ANY_SPEC = pl.BlockSpec(memory_space=pl.ANY)


def in_vmem(value):
    return pltpu.with_memory_space_constraint(value, pltpu.VMEM)


def in_hbm(value):
    return pltpu.with_memory_space_constraint(value, pltpu.HBM)


def per_step(shape, index):
    return pl.BlockSpec(shape, lambda s: (index(s),) + (0,) * (len(shape) - 1))


def same(step):
    return step


UNIT_IMAGES, NORM_IMAGES, MLP_IMAGES, BRANCH_IMAGES, INPUT_IMAGES, CONV_IMAGES = 2, 2, 2, 2, 2, 2
SMALL_MB, UNIT_MB, NORM_MB, MLP_MB, BRANCH_MB, INPUT_MB, CONV_MB = 8, 16, 16, 30, 16, 20, 16


def run_unit(valid, x):
    images, count = x.shape[0], UNIT_IMAGES
    return pl.pallas_call(
        unit_kernel,
        grid=(images // count,),
        in_specs=[VMEM_SPEC, per_step((count, 1024, 128), same)],
        out_specs=[VMEM_SPEC] * 3,
        out_shape=[
            pltpu.VMEM((images, 1024, 128), F32),
            pltpu.VMEM((images, 1024, 128), BF),
            sds((24, 128), F32),
        ],
        compiler_params=params(UNIT_MB),
        cost_estimate=cost(4),
        name="unit",
    )(valid, in_hbm(x))


def run_norm(placed, valid, unit, mine, other):
    images, count = unit.shape[0], NORM_IMAGES
    return pl.pallas_call(
        functools.partial(norm_kernel, placed),
        grid=(images // count,),
        in_specs=[VMEM_SPEC, per_step((count, 1024, 128), same), VMEM_SPEC, VMEM_SPEC],
        out_specs=[VMEM_SPEC] * 5,
        out_shape=[
            pltpu.VMEM((images, 1024, 128), BF),
            sds((24, 128), F32),
            sds((24, 128), F32),
            sds((16, 512), F32),
            pltpu.VMEM((SHARDS, ROWS, 128), BF),
        ],
        compiler_params=params(NORM_MB),
        cost_estimate=cost(5),
        name="norm",
    )(valid, in_vmem(unit), mine, other)


def run_mlp(placed, x, normed, mix, cot, vec, packed):
    images, count = x.shape[0], MLP_IMAGES
    pixels = 1024 * count
    g1 = (4, 16 * G1_BLOCKS, 128)
    shapes = [
        ((384, 128), BF), ((128, 128), BF), ((128, 512), BF), ((512, 128), BF), ((1152, 384), BF),
        ((32 * count, 32, 128), F32), ((count, 34, 48, 128), F32),
        ((pixels, 512), BF), ((pixels, 512), BF), ((pixels, 128), BF), ((pixels, 384), F32), ((pixels, 128), BF),
        ((pixels, 128), BF), ((pixels, 128), BF), ((count, 34, 48, 128), F32), ((count, 32, 48, 128), F32),
        ((count, 272, 384), BF), ((count, 272, 384), BF), ((264, 384), F32),
        ((1152, 384), F32), ((128, 512), F32), ((128, 512), F32), ((128, 128), F32),
        ((8, 384), F32), ((8, 512), F32), ((8, 128), F32), ((8, 128), F32), ((8, 128), F32), ((8, 128), F32),
    ]
    return pl.pallas_call(
        functools.partial(mlp_kernel, placed),
        grid=(images // count,),
        in_specs=[
            per_step((count, 1024, 128), same),
            VMEM_SPEC,
            VMEM_SPEC,
            per_step((count, 256, 320), same),
            VMEM_SPEC,
            VMEM_SPEC,
        ],
        out_specs=[VMEM_SPEC, VMEM_SPEC, VMEM_SPEC, VMEM_SPEC, whole(g1), whole(g1)],
        out_shape=[
            pltpu.VMEM((images, 256, 1152), BF),
            pltpu.VMEM((images, 1024, 128), F32),
            pltpu.VMEM((images, 1024, 640), BF),
            sds((24, 128), F32),
            sds(g1, F32),
            sds(g1, BF),
        ],
        scratch_shapes=[pltpu.VMEM(*shape) for shape in shapes],
        compiler_params=params(MLP_MB),
        cost_estimate=cost(35),
        name="mlp",
    )(in_hbm(x), in_vmem(normed), mix, cot, vec, in_vmem(packed))


def run_branches(placed, valid, unit, mix, sums, units, gcat, dmix, vec, packed):
    images, count = unit.shape[0], BRANCH_IMAGES
    g2 = (4, 16 * G2_BLOCKS, 128)
    shapes = [
        ((384, 128), F32), ((384, 128), F32), ((8, 128), F32), ((128, 512), F32),
    ]
    return pl.pallas_call(
        functools.partial(branch_kernel, placed),
        grid=(images // count,),
        in_specs=[
            VMEM_SPEC,
            per_step((count, 1024, 128), same),
            VMEM_SPEC,
            VMEM_SPEC,
            VMEM_SPEC,
            per_step((count, 1024, 640), same),
            VMEM_SPEC,
            VMEM_SPEC,
            VMEM_SPEC,
        ],
        out_specs=[whole((24, 128)), whole(g2), whole(g2)],
        out_shape=[sds((24, 128), F32), sds(g2, F32), sds(g2, BF)],
        scratch_shapes=[pltpu.VMEM(*shape) for shape in shapes],
        compiler_params=params(BRANCH_MB),
        cost_estimate=cost(8),
        name="branches",
    )(valid, in_vmem(unit), mix, sums, units, in_vmem(gcat), dmix, vec, in_vmem(packed))


def run_input(valid, x, mix, spread, gcat, gfirst, vec, packed, after):
    images, count = x.shape[0], INPUT_IMAGES
    maps = per_step((count, 1024, 128), same)
    return pl.pallas_call(
        input_kernel,
        grid=(images // count,),
        in_specs=[
            VMEM_SPEC, maps, VMEM_SPEC, VMEM_SPEC, per_step((count, 1024, 640), same), maps,
            VMEM_SPEC, VMEM_SPEC, ANY_SPEC,
        ],
        out_specs=maps,
        out_shape=sds((images, 1024, 128), F32),
        scratch_shapes=[pltpu.VMEM((128, 896), F32)],
        compiler_params=params(INPUT_MB),
        cost_estimate=cost(8),
        name="input_grad",
    )(valid, in_hbm(x), mix, spread, in_vmem(gcat), in_vmem(gfirst), vec, in_vmem(packed), after)


def run_conv(pm, vec, packed, after):
    images, count = pm.shape[0], CONV_IMAGES
    return pl.pallas_call(
        conv_kernel,
        grid=(images // count,),
        in_specs=[per_step((count, 256, 1152), same), VMEM_SPEC, VMEM_SPEC, ANY_SPEC],
        out_specs=per_step((count, 256, 320), same),
        out_shape=sds((images, 256, 320), BF),
        scratch_shapes=[pltpu.VMEM((1152, 384), BF)],
        compiler_params=params(CONV_MB),
        cost_estimate=cost(4),
        name="conv_out",
    )(in_vmem(pm), vec, in_vmem(packed), after)


def pack_weights(weights):
    return pl.pallas_call(
        pack_kernel,
        out_shape=sds((ROWS, 128), BF),
        in_specs=[VMEM_SPEC] * 21,
        out_specs=VMEM_SPEC,
        scratch_shapes=[pltpu.VMEM((16, 128), F32)],
        compiler_params=params(60),
        name="pack",
    )(*weights)


def join_kernel(own, one, two, three, after, out):
    for at, part in enumerate((own, one, two, three)):
        out[at] = part[...]


def join(own, near, after):
    return pl.pallas_call(
        join_kernel,
        out_shape=sds((4,) + own.shape, BF),
        in_specs=[VMEM_SPEC] * 4 + [ANY_SPEC],
        out_specs=VMEM_SPEC,
        compiler_params=params(SMALL_MB),
        cost_estimate=cost(1),
        name="join",
    )(own, *near, after)


def refine(ref, values):
    ref[...] = values.astype(BF)
    at = 16 * G1_VEC
    both = split_low(values[at : at + 16] + values[at + 16 : at + 32])
    ref[at : at + 32, :] = jnp.concatenate(both, axis=0).astype(BF)
    at = 16 * (G1_BLOCKS + G2_VEC)
    both = split_low(values[at : at + 8] + values[at + 8 : at + 16])
    ref[at : at + 16, :] = jnp.concatenate(both, axis=0).astype(BF)
    at = 16 * (G1_BLOCKS + G2_REDUCE)
    both = split_low(values[at : at + 16, 0:32] + values[at : at + 16, 32:64])
    ref[at : at + 16, 0:64] = jnp.concatenate(both, axis=1).astype(BF)


def sum_pair_kernel(keep1, got1, keep2, got2, own, *others):
    for peer in range(4):
        one = keep1[peer] + got1[peer].astype(F32)
        two = keep2[peer] + got2[peer].astype(F32)
        values = jnp.concatenate([one, two], axis=0)
        if peer == 0:
            own[...] = values
        else:
            refine(others[peer - 1], values)


def sum_four_kernel(own, one, two, three, total, low):
    value = own[...] + one[...].astype(F32) + two[...].astype(F32) + three[...].astype(F32)
    total[...] = value
    refine(low, value)


def sum_pair(keep1, got1, keep2, got2):
    rows = keep1.shape[1] + keep2.shape[1]
    return pl.pallas_call(
        sum_pair_kernel,
        out_shape=[sds((rows, 128), F32)] + [sds((rows, 128), BF)] * 3,
        in_specs=[VMEM_SPEC] * 4,
        out_specs=[VMEM_SPEC] * 4,
        compiler_params=params(SMALL_MB),
        cost_estimate=cost(2),
        name="sum_pair",
    )(keep1, got1, keep2, got2)


def sum_four(*values):
    shape = values[0].shape
    return pl.pallas_call(
        sum_four_kernel,
        out_shape=[sds(shape, F32), sds(shape, BF)],
        in_specs=[VMEM_SPEC] * 4,
        out_specs=[VMEM_SPEC] * 2,
        compiler_params=params(SMALL_MB),
        cost_estimate=cost(2),
        name="sum_four",
    )(*values)


def finish_kernel(*refs):
    (one0, one1, one2, one3,
     gain_one, bias_one, w_h, b_h, w_w, b_w, w_c, w_red, b_red, w_exp, b_exp, w_proj, b_proj,
     gain_two, bias_two, w_up, b_up, w_down, b_down, w_conv, b_conv) = refs
    shard = lax.axis_index("fsdp")

    def first(at, rows=16):
        here = slice(16 * at, 16 * at + rows)
        return (one0[here, :] + one1[here, :].astype(F32)) + (
            one2[here, :].astype(F32) + one3[here, :].astype(F32)
        )

    def second(at, rows=16):
        return first(G1_BLOCKS + at, rows)

    w_h[...] = second(G2_HEIGHT)
    w_w[...] = second(G2_WIDTH)
    w_c[...] = second(G2_CHANNEL)
    reduce = second(G2_REDUCE)
    w_red[...] = reduce[:, 0:32] + reduce[:, 32:64]
    expand = second(G2_EXPAND)
    for b in range(3):
        w_exp[:, 128 * b : 128 * b + 128] = expand[4 * b : 4 * b + 4, :]
    w_proj[...] = first(G1_PROJ)
    for b in range(4):
        w_up[:, 128 * b : 128 * b + 128] = first(G1_UP + b)
    w_down[...] = first(G1_DOWN, 64)
    for at, tap in enumerate(TAPS):
        kernel = w_conv.at[tap // 3, tap % 3]
        for b in range(2):
            kernel[:, 128 * b : 128 * b + 128] = first(G1_CONV + 2 * at + b)
        edge = 64 * (at % 2)
        kernel[:, 256:320] = first(G1_EDGE + at // 2)[:, edge : edge + 64]
    table_one, table_two = first(G1_VEC) + first(G1_VEC_LOW), second(G2_VEC)
    table_two = table_two[0:8, :] + table_two[8:16, :]

    def share(table, row, blocks, length, stride):
        total = jnp.zeros((1, 128), F32)
        for b in range(blocks):
            pick = iota((128, 128), 0) + 128 * b == iota((128, 128), 1) + shard * stride
            total = total + dot_high(table, pick.astype(F32))[row + b : row + b + 1, :]
        return total[:, 0:length].reshape(length)

    gain_one[...] = share(table_two, G2_GAIN1, 1, 16, 16)
    bias_one[...] = share(table_two, G2_BIAS1, 1, 16, 16)
    b_h[...] = share(table_two, G2_BH, 1, 16, 16)
    b_w[...] = share(table_two, G2_BW, 1, 16, 16)
    b_red[...] = share(table_two, G2_BR, 1, 4, 16)
    b_exp[...] = share(table_two, G2_BE, 3, 48, 48)
    b_proj[...] = share(table_one, G1_BPROJ, 1, 16, 16)
    gain_two[...] = share(table_one, G1_GAIN2, 1, 16, 16)
    bias_two[...] = share(table_one, G1_BIAS2, 1, 16, 16)
    b_up[...] = share(table_one, G1_BUP, 4, 64, 64)
    b_down[...] = share(table_one, G1_BDOWN, 1, 16, 16)
    b_conv[...] = share(table_one, G1_BCONV, 3, 40, 40)


def finish(sums, weights):
    return pl.pallas_call(
        finish_kernel,
        out_shape=[sds(w.shape, F32) for w in weights],
        in_specs=[VMEM_SPEC] * 4,
        out_specs=[VMEM_SPEC] * 21,
        compiler_params=params(SMALL_MB),
        name="finish",
    )(*sums)


def early(placed, input_map, valid_size, cotangent, gathered):
    images = input_map.shape[0]
    x = input_map.reshape(images, 1024, 128)
    cot = cotangent.reshape(images, 256, 320)
    unit, unit_low, units = run_unit(valid_size, x)
    normed, sums, mix, vec, packed = run_norm(placed, valid_size, unit, *gathered(units))
    pm, gfirst, gcat, dmix, keep1, send1 = run_mlp(placed, x, normed, mix, cot, vec, packed)
    spread, keep2, send2 = run_branches(
        placed, valid_size, unit_low, mix, sums, units, gcat, dmix, vec, packed
    )

    def late_map(after):
        return run_conv(pm, vec, packed, after).reshape(images, 16, 16, 320)

    def late_grad(after):
        grad = run_input(valid_size, x, mix, spread, gcat, gfirst, vec, packed, after)
        return grad.reshape(images, 32, 32, 128)

    return (keep1, send1, keep2, send2), late_map, late_grad


def compute(placed, input_map, valid_size, cotangent, packed):
    sums, late_map, late_grad = early(
        placed, input_map, valid_size, cotangent, lambda after: (packed[0::2], packed[1::2])
    )
    return late_map(sums[0]), late_grad(sums[0]), sums


def pack_whole(weights):
    (gain_one, bias_one, w_h, b_h, w_w, b_w, w_c, w_red, b_red, w_exp, b_exp, w_proj, b_proj,
     gain_two, bias_two, w_up, b_up, w_down, b_down, w_conv, b_conv) = weights

    def split(weight):
        weight = weight.reshape(SHARDS, weight.shape[0] // SHARDS, weight.shape[1])
        rows, cols = -weight.shape[1] % 16, -weight.shape[2] % 128
        weight = jnp.pad(weight, ((0, 0), (0, rows), (0, cols)))
        return [weight[:, :, at : at + 128] for at in range(0, weight.shape[2], 128)]

    pieces = split(w_h) + split(w_w) + split(w_c) + split(w_proj) + split(w_red) + split(w_exp)
    pieces = pieces + split(w_up) + split(w_down)
    for tap in TAPS:
        pieces = pieces + split(w_conv[tap // 3, tap % 3])
    vectors = (gain_one, bias_one, b_h, b_w, b_red, b_exp, b_proj, gain_two, bias_two, b_up, b_down, b_conv)
    rows = [
        jnp.pad(v.reshape(SHARDS, 1, v.shape[0] // SHARDS), ((0, 0), (0, 0), (0, 128 - v.shape[0] // SHARDS)))
        for v in vectors
    ]
    rows = rows + [jnp.zeros((SHARDS, 4, 128), BF)]
    return jnp.concatenate(pieces + [jnp.concatenate(rows, axis=1)], axis=1)


def unpack_whole(sums):
    one = jnp.stack([sums[0], sums[1].astype(F32)], axis=1).reshape(SHARDS, -1, 128)
    two = jnp.stack([sums[2], sums[3].astype(F32)], axis=1).reshape(SHARDS, -1, 128)

    def join(buffer, at, blocks, rows=16):
        parts = [buffer[:, 16 * (at + b) : 16 * (at + b) + rows, :] for b in range(blocks)]
        return jnp.concatenate(parts, axis=2).reshape(SHARDS * rows, 128 * blocks)

    def vector(buffer, at, row, blocks=1):
        start, rest = 16 * at + row, 16 if at == G1_VEC else 8
        both = buffer[0, start : start + blocks, :] + buffer[0, start + rest : start + rest + blocks, :]
        return both.reshape(128 * blocks)

    expand = two[:, 16 * G2_EXPAND : 16 * G2_EXPAND + 12, :].reshape(SHARDS, 3, 4, 128)
    taps = []
    for tap in range(9):
        at = TAPS.index(tap)
        edge = join(one, G1_EDGE + at // 2, 1)[:, 64 * (at % 2) : 64 * (at % 2) + 64]
        taps.append(jnp.concatenate([join(one, G1_CONV + 2 * at, 2), edge], axis=1))
    return (
        vector(two, G2_VEC, G2_GAIN1),
        vector(two, G2_VEC, G2_BIAS1),
        join(two, G2_HEIGHT, 1),
        vector(two, G2_VEC, G2_BH),
        join(two, G2_WIDTH, 1),
        vector(two, G2_VEC, G2_BW),
        join(two, G2_CHANNEL, 1),
        join(two, G2_REDUCE, 1)[:, 0:32] + join(two, G2_REDUCE, 1)[:, 32:64],
        vector(two, G2_VEC, G2_BR).reshape(SHARDS, 16)[:, 0:4].reshape(32),
        expand.transpose(0, 2, 1, 3).reshape(32, 384),
        vector(two, G2_VEC, G2_BE, 3),
        join(one, G1_PROJ, 1),
        vector(one, G1_VEC, G1_BPROJ),
        vector(one, G1_VEC, G1_GAIN2),
        vector(one, G1_VEC, G1_BIAS2),
        join(one, G1_UP, 4),
        vector(one, G1_VEC, G1_BUP, 4),
        one[:, 16 * G1_DOWN : 16 * G1_DOWN + 64, :].reshape(512, 128),
        vector(one, G1_VEC, G1_BDOWN),
        jnp.stack(taps).reshape(3, 3, 128, 320),
        vector(one, G1_VEC, G1_BCONV, 3)[0:320],
    )


def shards_of(mesh):
    shards, copies = mesh.shape["fsdp"], mesh.shape["rep"]

    def eight(input_map, valid_size, *rest):
        weights, cotangent = rest[:-1], rest[-1]
        sibling = [(i, i ^ 1) for i in range(shards)]
        own = pack_weights(weights)
        near = [
            lax.ppermute(own, "fsdp", [(i, i ^ (2 * peer)) for i in range(shards)])
            for peer in range(1, 4)
        ]

        def gathered(after):
            mine = join(own, near, after)
            return mine, lax.ppermute(mine, "fsdp", sibling)

        (keep1, send1, keep2, send2), late_map, late_grad = early(
            True, input_map, valid_size, cotangent, gathered
        )
        got1, got2 = lax.ppermute(send1, "fsdp", sibling), lax.ppermute(send2, "fsdp", sibling)
        own, *others = sum_pair(keep1, got1, keep2, got2)
        moved = [
            lax.ppermute(value, "fsdp", [(i, i ^ (2 * (peer + 1))) for i in range(shards)])
            for peer, value in enumerate(others)
        ]
        out = late_map(own)
        total, low = sum_four(own, *moved)
        far = [
            lax.ppermute(low, "rep", [(i, (i + k) % copies) for i in range(copies)])
            for k in range(1, copies)
        ]
        input_grad = late_grad(total)
        return (out, input_grad) + tuple(finish((total, *far), weights))

    def general(input_map, valid_size, *rest):
        weights, cotangent = rest[:-1], rest[-1]
        dims = [2 if w.ndim == 4 else 0 for w in weights]
        full = [lax.all_gather(w, "fsdp", axis=d, tiled=True) for w, d in zip(weights, dims)]
        packed = pack_whole(full)
        out, input_grad, sums = compute(False, input_map, valid_size, cotangent, packed)
        grads = [
            lax.psum_scatter(g, "fsdp", scatter_dimension=d, tiled=True)
            for g, d in zip(unpack_whole(sums), dims)
        ]
        return (out, input_grad) + tuple(lax.psum(grads, "rep"))

    return eight if shards == SHARDS and copies == 4 else general


def solution(mesh):
    maps = P(("rep", "fsdp"), None, None, None)
    vector, matrix = P("fsdp"), P("fsdp", None)
    weights = (
        vector, vector, matrix, vector, matrix, vector, matrix, matrix, vector, matrix, vector,
        matrix, vector, vector, vector, matrix, vector, matrix, vector,
        P(None, None, "fsdp", None), vector,
    )
    return jax.shard_map(
        shards_of(mesh),
        mesh=mesh,
        in_specs=(maps, P(("rep", "fsdp"), None)) + weights + (maps,),
        out_specs=(maps, maps) + weights,
        check_vma=False,
    )
```

```python
import functools

import jax
import jax.numpy as jnp
from jax import lax
from jax.experimental import pallas as pl
from jax.experimental.pallas import tpu as pltpu
from jax.sharding import PartitionSpec as P

BF = jnp.bfloat16
F32 = jnp.float32
HIGH = lax.Precision.HIGHEST
EPS = 1e-05

SHARDS = 8
B_HEIGHT, B_WIDTH, B_CHANNEL, B_PROJ, B_REDUCE = 0, 1, 2, 3, 4
B_EXPAND, B_UP, B_DOWN, B_VEC, BLOCKS = 5, 8, 12, 16, 17
C_PAIRS, C_EDGES, C_BLOCKS = 0, 18, 23
ROWS, CONV_ROWS = 16 * BLOCKS, 16 * C_BLOCKS
TAPS = (4, 5, 7, 8, 3, 6, 1, 2, 0)
(V_GAIN1, V_BIAS1, V_BH, V_BW, V_BR, V_BE, V_BP, V_GAIN2, V_BIAS2, V_BUP, V_BDOWN, V_BCONV) = range(12)
LENGTHS = (16, 16, 16, 16, 4, 48, 16, 16, 16, 64, 16, 40)
G1_CONV, G1_EDGE, G1_UP, G1_DOWN, G1_PROJ, G1_VEC, G1_VEC_LOW, G1_BLOCKS = 0, 18, 23, 27, 31, 32, 33, 34
G1_BCONV, G1_BUP, G1_BDOWN, G1_BPROJ, G1_GAIN2, G1_BIAS2 = 0, 3, 7, 8, 9, 10
G2_HEIGHT, G2_WIDTH, G2_CHANNEL, G2_REDUCE, G2_EXPAND, G2_VEC, G2_BLOCKS = 0, 1, 2, 3, 4, 5, 6
G2_GAIN1, G2_BIAS1, G2_BH, G2_BW, G2_BR, G2_BE = 0, 1, 2, 3, 4, 5


def iota(shape, axis):
    return lax.broadcasted_iota(jnp.int32, shape, axis)


def dot(left, right):
    return jnp.dot(left, right, preferred_element_type=F32)


def dot_nt(left, right):
    return lax.dot_general(left, right, (((1,), (1,)), ((), ())), preferred_element_type=F32)


def dot_tn(left, right):
    return lax.dot_general(left, right, (((0,), (0,)), ((), ())), preferred_element_type=F32)


def parts_of(values, count):
    parts = []
    for _ in range(count):
        parts.append(values.astype(BF))
        values = values - parts[-1].astype(F32)
    return parts


def dot_wide(left, right, product=dot):
    rows = left.shape[0]
    joined = product(jnp.concatenate(parts_of(left, 3), axis=0), right)
    return joined[0:rows] + (joined[rows : 2 * rows] + joined[2 * rows : 3 * rows])


def outer_wide(left, right):
    (left_high, left_low), (right_high, right_low) = parts_of(left, 2), parts_of(right, 2)
    return dot_tn(
        jnp.concatenate([left_high, left_high, left_low, left_low], axis=0),
        jnp.concatenate([right_high, right_low, right_high, right_low], axis=0),
    )


def fold8(values):
    rows, cols = values.shape
    return jnp.sum(values.reshape(rows // 8, 8, cols), axis=0)


def lane_mean(values):
    return jnp.mean(values, axis=-1, keepdims=True)


def gelu_both(values):
    cdf = 0.5 + 0.5 * lax.erf(values * 0.7071067811865476)
    slope = cdf + values * (jnp.exp(-0.5 * (values * values)) * 0.3989422804014327)
    return values * cdf, slope


def gelu_twice(values):
    cdf = 1.0 + lax.erf(values * 0.7071067811865476)
    density = (values * 0.7978845608028654) * jnp.exp2((values * values) * -0.7213475204444817)
    return values * cdf, cdf + density


def split_low(values):
    high = values.astype(BF).astype(F32)
    return high, (values - high).astype(BF).astype(F32)


def block(packed, at):
    return packed[:, 16 * at : 16 * at + 16, :].reshape(128, 128)


def branch_weights(packed):
    return [block(packed, at) for at in (B_HEIGHT, B_WIDTH, B_CHANNEL)]


def spread_matrix():
    unit, lane = iota((128, 128), 0), iota((128, 128), 1)
    return ((lane == 16 * (unit // 4) + unit % 4) & (unit < 32)).astype(BF)


def pick_matrix(k):
    return (iota((384, 128), 0) == 3 * iota((384, 128), 1) + k).astype(BF)


def head_weights(packed, vec):
    w_reduce = dot(block(packed, B_REDUCE), spread_matrix()).astype(BF)
    expand = jnp.concatenate([block(packed, B_EXPAND + b) for b in range(3)], axis=1)
    picks = jnp.concatenate([pick_matrix(k) for k in range(3)], axis=1)
    w_expand = dot(expand, picks).astype(BF)
    b_expand = dot(vec[:, 0:384].astype(BF), picks)[V_BE : V_BE + 1, :]
    return w_reduce, w_expand, b_expand


def head_forward(sums, counts, branches, head, vec):
    w_reduce, w_expand, b_expand = head
    pooled = dot_wide(jnp.concatenate(sums, axis=1), branches) / counts
    pooled = pooled + (vec[V_BH : V_BH + 1, 0:128] + vec[V_BW : V_BW + 1, 0:128])
    pre = dot_wide(pooled, w_reduce) + vec[V_BR : V_BR + 1, 0:128]
    hidden, slope = gelu_both(pre)
    joined = dot_wide(hidden, w_expand) + b_expand
    logits = [joined[:, 128 * k : 128 * k + 128] for k in range(3)]
    top = jnp.maximum(jnp.maximum(logits[0], logits[1]), logits[2])
    powers = [jnp.exp(v - top) for v in logits]
    total = powers[0] + powers[1] + powers[2]
    return pooled, hidden, slope, [v / total for v in powers]


def column(row_values):
    stacked = jnp.where(iota((8, 128), 0) == 0, row_values, 0.0)
    return dot_tn(stacked.astype(BF), jnp.ones((8, 128), BF))


def size_columns(valid_ref):
    sizes = valid_ref[...].astype(F32).astype(BF)
    kind = iota((2, 128), 0)
    return [dot_tn(sizes, (kind == axis).astype(BF)) for axis in range(2)]


def inside_counts(valid_ref):
    high, wide = size_columns(valid_ref)
    offsets = jnp.broadcast_to(channel_offsets()[0, 0:1, :], (8, 128))

    def kept(size):
        past = jnp.where(offsets == 1, jnp.where(size == 32.0, 1.0, 0.0), 0.0)
        return size - past - jnp.where(offsets == -1, 1.0, 0.0)

    return [kept(high) * wide, kept(wide) * high, high * wide]


def count_column(valid_ref):
    high, wide = size_columns(valid_ref)
    return high * wide


def channel_offsets():
    return (iota((1, 32, 128), 2) + 1) % 3 - 1


def shifted_masks(valid_ref, image):
    sizes = jnp.where(iota((2, 8), 1) == image, valid_ref[...].astype(F32), 0.0)
    size = jnp.sum(sizes, axis=1, keepdims=True)
    masks = []
    for axis, shape in ((0, (32, 1, 128)), (1, (1, 32, 128))):
        limit = size[axis : axis + 1, :].reshape(1, 1, 1)
        at = iota(shape, axis)
        taker = at - ((iota(shape, 2) + 1) % 3 - 1)
        masks.append((at.astype(F32) < limit).astype(F32))
        masks.append(((taker >= 0) & (taker.astype(F32) < limit)).astype(F32))
    return masks


def class_sums(maps, masks):
    row, row_taker, col, col_taker = masks

    def by_row(mask):
        return jnp.sum((maps * mask).reshape(32, 4, 8, 128), axis=1)

    plain, taken = by_row(col), by_row(col_taker)
    return [
        jnp.sum(jnp.sum(rows * mask, axis=0), axis=0, keepdims=True)
        for rows, mask in ((plain, row_taker), (taken, row), (plain, row))
    ]


def place_of(placed):
    if not placed:
        return 0, 0
    shard = lax.axis_index("fsdp")
    return shard // 2, lax.rem(shard, 2)


def pack_kernel(*refs):
    (gain_one, bias_one, w_h, b_h, w_w, b_w, w_c, w_red, b_red, w_exp, b_exp, w_proj, b_proj,
     gain_two, bias_two, w_up, b_up, w_down, b_down, w_conv, b_conv, out, vec) = refs
    conv = out.at[ROWS : ROWS + CONV_ROWS]

    def put(at, values):
        out[16 * at : 16 * at + values.shape[0], 0 : values.shape[1]] = values

    put(B_HEIGHT, w_h[...])
    put(B_WIDTH, w_w[...])
    put(B_CHANNEL, w_c[...])
    put(B_PROJ, w_proj[...])
    blank = jnp.zeros((16, 128), BF)
    put(B_REDUCE, blank)
    put(B_REDUCE, w_red[...])
    for b in range(3):
        vec[...] = jnp.zeros((16, 128), F32)
        vec[0:4, :] = w_exp[:, 128 * b : 128 * b + 128].astype(F32)
        put(B_EXPAND + b, vec[...].astype(BF))
    for b in range(4):
        put(B_UP + b, w_up[:, 128 * b : 128 * b + 128])
    put(B_DOWN, w_down[...])
    conv[16 * (C_BLOCKS - 1) : 16 * C_BLOCKS, :] = blank
    for at, tap in enumerate(TAPS):
        kernel = w_conv.at[tap // 3, tap % 3]
        for b in range(2):
            start = 16 * (C_PAIRS + 2 * at + b)
            conv[start : start + 16, :] = kernel[:, 128 * b : 128 * b + 128]
        start, lane = 16 * (C_EDGES + at // 2), 64 * (at % 2)
        conv[start : start + 16, lane : lane + 64] = kernel[:, 256:320]
    vec[...] = jnp.zeros((16, 128), F32)
    vectors = (gain_one, bias_one, b_h, b_w, b_red, b_exp, b_proj, gain_two, bias_two, b_up, b_down, b_conv)
    for row, (values, length) in enumerate(zip(vectors, LENGTHS)):
        vec[row : row + 1, 0:length] = values[...].astype(F32).reshape(1, length)
    put(B_VEC, vec[...].astype(BF))


def vector_table(packed):
    shards = packed[:, 16 * B_VEC : 16 * B_VEC + 16, :].reshape(128, 128)
    table = jnp.zeros((16, 512), F32)
    rows = iota((16, 512), 0)
    for length in (16, 4, 48, 64, 40):
        step = 16 if length == 4 else length
        lane = iota((128, 512), 1)
        source = iota((128, 512), 0)
        pick = ((source == lane % step) & (source < length)).astype(BF)
        spread = dot(shards, pick)
        mine = (source // 16) == (lane // step)
        whole = jnp.sum(jnp.where(mine, spread, 0.0).reshape(8, 16, 512), axis=0)
        held = functools.reduce(
            jnp.logical_or, [rows == v for v, size in enumerate(LENGTHS) if size == length]
        )
        table = jnp.where(held, whole, table)
    return table


def unit_kernel(valid, x_ref, unit_ref, low_ref, sums_ref):
    step, count = pl.program_id(0), x_ref.shape[0]
    low = x_ref[...].reshape(count * 1024, 128)
    centre = low.astype(F32) - dot(low, jnp.full((128, 128), 1.0 / 128.0, BF))
    scale = lax.rsqrt(lane_mean(centre * centre) + EPS)
    unit = centre * scale
    here = pl.ds(step * count, count)
    unit_ref[here] = unit.reshape(count, 1024, 128)
    low_ref[here] = unit.astype(BF).reshape(count, 1024, 128)
    for m in range(count):
        image = step * count + m
        maps = unit[1024 * m : 1024 * m + 1024].reshape(32, 32, 128)
        for k, total in enumerate(class_sums(maps, shifted_masks(valid, image))):
            sums_ref[pl.ds(8 * k + image, 1), :] = total


def norm_kernel(
    placed, valid, unit_ref, own, swapped, mine, other,
    norm_ref, head_ref, reduce_ref, expand_ref, mix_ref, vec_ref, pk_ref, sums_ref
):
    chip, core = place_of(placed)
    pk_ref[2 * chip + core] = own[0:ROWS, :]
    pk_ref[2 * chip + (1 - core)] = swapped[0:ROWS, :]
    for peer in range(1, 4):
        shard = 2 * lax.bitwise_xor(chip, peer)
        pk_ref[shard + core] = mine[peer - 1]
        pk_ref[shard + (1 - core)] = other[peer - 1]
    vec = vector_table(pk_ref)
    vec_ref[...] = vec
    head = head_weights(pk_ref, vec)
    gain = vec[V_GAIN1 : V_GAIN1 + 1, 0:128]
    bias = vec[V_BIAS1 : V_BIAS1 + 1, 0:128]
    for image in range(unit_ref.shape[0]):
        low = (unit_ref[image] * gain + bias).astype(BF)
        norm_ref[image] = low
        maps = low.astype(F32).reshape(32, 32, 128)
        for k, total in enumerate(class_sums(maps, shifted_masks(valid, image))):
            sums_ref[8 * k + image : 8 * k + image + 1, :] = total
    sums = [sums_ref[8 * k : 8 * k + 8, :] for k in range(3)]
    branches = jnp.concatenate(branch_weights(pk_ref), axis=0)
    pooled, hidden, slope, mixing = head_forward(sums, count_column(valid), branches, head, vec)
    for at, values in enumerate((pooled, hidden, slope)):
        head_ref[8 * at : 8 * at + 8, :] = values
    reduce_ref[...], expand_ref[...] = head[0], head[1]
    for k in range(3):
        mix_ref[8 * k : 8 * k + 8, :] = mixing[k]


def mlp_kernel(
    placed, x_ref, norm_ref, mix_ref, cot_ref, vec_ref, pk_ref, own, swapped, conv_mine, conv_other,
    pm_ref, gfirst_ref, gcat_ref, dmix_ref, wconv, keep_ref, send_ref,
    wcat, wproj, wup, wdown,
    gsec, low, act, ghid, norm2, mixes, mixed_s, gtail, gbranch, npad, gpad, cotp, cots, cotf,
    a_conv, a_up, a_down, a_proj, a_bconv, a_bup, a_bdown, a_bproj, a_gain2, a_bias2,
):
    step, steps, count = pl.program_id(0), pl.num_programs(0), x_ref.shape[0]

    @pl.when(step == 0)
    def _():
        for k, weight in enumerate(branch_weights(pk_ref)):
            wcat[128 * k : 128 * k + 128, :] = weight
        wproj[...] = block(pk_ref, B_PROJ)
        for b in range(4):
            wup[:, 128 * b : 128 * b + 128] = block(pk_ref, B_UP + b)
        wdown[...] = pk_ref[:, 16 * B_DOWN : 16 * B_DOWN + 64, :].reshape(512, 128) * jnp.bfloat16(0.5)
        chip, core = place_of(placed)
        blank = jnp.zeros((16, 64), BF)
        for peer in range(4):
            conv = slice(ROWS, ROWS + CONV_ROWS)
            pair = (own.at[conv], swapped.at[conv])
            if peer > 0:
                pair = (conv_mine.at[peer - 1], conv_other.at[peer - 1])
            for part, odd in zip(pair, (core, 1 - core)):
                shard = 2 * lax.bitwise_xor(chip, peer) + odd
                for at in range(9):
                    rows = pl.ds(pl.multiple_of(128 * at + 16 * shard, 16), 16)
                    for b in range(2):
                        start = 16 * (C_PAIRS + 2 * at + b)
                        wconv[rows, 128 * b : 128 * b + 128] = part[start : start + 16, :]
                    start, lane = 16 * (C_EDGES + at // 2), 64 * (at % 2)
                    edge = part[start : start + 16, :][:, lane : lane + 64]
                    wconv[rows, 256:384] = jnp.concatenate([edge, blank], axis=1)
        for ref in (low, npad):
            ref[:, 0:1] = jnp.zeros((count, 1, 48, 128), F32)
            ref[:, 33:34] = jnp.zeros((count, 1, 48, 128), F32)
        for ref in (low, npad, gpad):
            shape = ref.shape[0:2] + (8, 128)
            ref[:, :, 0:8, :] = jnp.zeros(shape, F32)
            ref[:, :, 40:48, :] = jnp.zeros(shape, F32)
        for ref in (cotp, cots, cotf, a_conv, a_up, a_down, a_proj, a_bconv, a_bup,
                    a_bdown, a_bproj, a_gain2, a_bias2):
            ref[...] = jnp.zeros(ref.shape, ref.dtype)

    def row(at, width=128):
        return vec_ref[at : at + 1, 0:width]

    images = range(count)
    maps = [step * count + m for m in images]
    pixels = [slice(1024 * m, 1024 * m + 1024) for m in images]

    offsets = channel_offsets()
    forth, back = offsets == 1, offsets == -1
    for m in images:
        mixing = [mix_ref[pl.ds(8 * k + maps[m], 1), :] for k in range(3)]
        biases = (row(V_BH), row(V_BW), 0.0)
        normed = norm_ref[maps[m]]
        here = normed.astype(F32).reshape(32, 32, 128)
        npad[m, 1:33, 8:40, :] = here
        high = jnp.where(
            forth, npad[m, 2:34, 8:40, :], jnp.where(back, npad[m, 0:32, 8:40, :], here)
        )
        wide = jnp.where(
            forth, npad[m, 1:33, 9:41, :], jnp.where(back, npad[m, 1:33, 7:39, :], here)
        )
        shifted = (high.reshape(1024, 128).astype(BF), wide.reshape(1024, 128).astype(BF), normed)
        mixed = 0.0
        for k in range(3):
            branch = dot(shifted[k], wcat[128 * k : 128 * k + 128, :]) + biases[k]
            mixes[pixels[m], 128 * k : 128 * k + 128] = branch
            mixed = mixed + branch * mixing[k]
        mixed_s[pixels[m], :] = mixed.astype(BF)
    first, unit, scale = [None] * count, [None] * count, [None] * count
    for m in images:
        added = dot(mixed_s[pixels[m], :], wproj[...]) + row(V_BP)
        first[m] = x_ref[m].astype(F32) + added
        centre = first[m] - lane_mean(first[m])
        scale[m] = lax.rsqrt(lane_mean(centre * centre) + EPS)
        unit[m] = centre * scale[m]
        norm2[pixels[m], :] = (unit[m] * row(V_GAIN2) + row(V_BIAS2)).astype(BF)

    for m in images:
        cot = cot_ref[m]
        cotp[m, 0:256, 0:320] = cot
        cotf[0:256, 0:320] = cot.astype(F32)
        ahead = cotf[1:257, :]
        ahead = jnp.where(iota(ahead.shape, 0) % 16 == 15, 0.0, ahead)
        cots[m, 0:256, :] = ahead.astype(BF)
        a_bconv[...] += fold8(cotf[0:256, :])
    flat = (count * 256, 384)
    cot_here, cot_right = cotp[:, 0:256, :].reshape(flat), cots[:, 0:256, :].reshape(flat)
    cot_below, cot_both = cotp[:, 16:272, :].reshape(flat), cots[:, 16:272, :].reshape(flat)
    pair_a = dot_nt(cot_here, wconv[0:256, :])
    pair_b = dot_nt(cot_here, wconv[256:512, :])
    pair_c = dot_nt(cot_right, wconv[512:768, :])
    pair_d = dot_nt(cot_below, wconv[768:1024, :])
    last = dot_nt(cot_both, wconv[1024:1152, :])
    planes = (
        (pair_a[:, 0:128], pair_a[:, 128:256] + pair_c[:, 0:128]),
        (
            pair_b[:, 0:128] + pair_d[:, 0:128],
            pair_b[:, 128:256] + pair_c[:, 128:256] + pair_d[:, 128:256] + last,
        ),
    )
    for p in range(2):
        for s in range(2):
            plane = planes[p][s]
            for i in range(16 * count):
                gsec[2 * i + p, pl.ds(s, 16, stride=2), :] = plane[16 * i : 16 * i + 16, :]

    grad_second = [gsec[32 * m : 32 * m + 32].reshape(1024, 128) for m in images]
    for m in images:
        tail = grad_second[m].astype(BF)
        gtail[pixels[m], :] = tail
        a_bdown[...] += fold8(grad_second[m])
        for b in range(2):
            cols = slice(256 * b, 256 * b + 256)
            hidden = dot(norm2[pixels[m], :], wup[:, cols]) + vec_ref[V_BUP : V_BUP + 1, cols]
            grad_act = dot_nt(tail, wdown[cols, :])
            value, slope = gelu_twice(hidden)
            act[pixels[m], cols] = value.astype(BF)
            grad_hidden = grad_act * slope
            ghid[pixels[m], cols] = grad_hidden.astype(BF)
            a_bup[:, cols] += fold8(grad_hidden)
    grad_first = [None] * count
    for m in images:
        second = first[m] + (dot(act[pixels[m], :], wdown[...]) + row(V_BDOWN))
        low[m, 1:33, 8:40, :] = second.reshape(32, 32, 128)
        grad_normed = dot_nt(ghid[pixels[m], :], wup[...])
        a_gain2[...] += fold8(grad_normed * unit[m])
        a_bias2[...] += fold8(grad_normed)
        scaled_grad = grad_normed * row(V_GAIN2)
        grad_first[m] = grad_second[m] + scale[m] * (
            scaled_grad - lane_mean(scaled_grad) - unit[m] * lane_mean(scaled_grad * unit[m])
        )
        gfirst_ref[maps[m]] = grad_first[m]
        gbranch[pixels[m], :] = grad_first[m].astype(BF)
        a_bproj[...] += fold8(grad_first[m])
    a_up[...] += dot_tn(norm2[...], ghid[...])
    a_down[...] += dot_tn(gtail[...], act[...])
    for m in images:
        grad_mixed = dot_nt(gbranch[pixels[m], :], wproj[...])
        for k in range(3):
            share = fold8(grad_mixed * mixes[pixels[m], 128 * k : 128 * k + 128])
            dmix_ref[pl.ds(8 * k + maps[m], 1), :] = jnp.sum(share, axis=0, keepdims=True)
        gpad[m, :, 8:40, :] = grad_mixed.reshape(32, 32, 128)
        low_grad, image = grad_mixed.astype(BF), maps[m]
        gcat_ref[image, :, 0:128] = low_grad
        gcat_ref[image, 0:32, 128:256] = jnp.zeros((32, 128), BF)
        gcat_ref[image, 32:1024, 128:256] = low_grad[0:992]
        gcat_ref[image, 0:992, 256:384] = low_grad[32:1024]
        gcat_ref[image, 992:1024, 256:384] = jnp.zeros((32, 128), BF)
        gcat_ref[image, :, 384:512] = gpad[m, :, 7:39, :].reshape(1024, 128).astype(BF)
        gcat_ref[image, :, 512:640] = gpad[m, :, 9:41, :].reshape(1024, 128).astype(BF)

    for at, tap in enumerate(TAPS):
        r, s = tap // 3, tap % 3
        for m in images:
            patch = low[m, pl.ds(r, 16, stride=2), pl.ds(7 + s, 16, stride=2), :]
            pm_ref[maps[m], :, 128 * at : 128 * at + 128] = patch.reshape(256, 128).astype(BF)

    a_proj[...] += dot_tn(mixed_s[...], gbranch[...])
    patches = pm_ref[pl.ds(step * count, count)].reshape(256 * count, 1152)
    a_conv[...] += dot_tn(patches, cot_here)

    @pl.when(step == steps - 1)
    def _():
        chip, core = place_of(placed)[0:2]
        vectors = jnp.concatenate(
            [jnp.sum(a_bconv[:, 128 * b : 128 * b + 128], axis=0, keepdims=True) for b in range(3)]
            + [jnp.sum(a_bup[:, 128 * b : 128 * b + 128], axis=0, keepdims=True) for b in range(4)]
            + [jnp.sum(ref[...], axis=0, keepdims=True) for ref in (a_bdown, a_bproj, a_gain2, a_bias2)]
            + [jnp.zeros((5, 128), F32)],
            axis=0,
        )
        vectors, vectors_low = split_low(vectors)
        down = [0.5 * a_down[:, 128 * b : 128 * b + 128].T for b in range(4)]

        def piece(at, shard):
            rows = slice(16 * shard, 16 * shard + 16)
            if at < G1_EDGE:
                start = 128 * (at // 2) + 16 * shard
                return a_conv[start : start + 16, 128 * (at % 2) : 128 * (at % 2) + 128]
            if at < G1_UP:
                start = 256 * (at - G1_EDGE) + 16 * shard
                one = a_conv[start : start + 16, 256:320]
                if at == G1_UP - 1:
                    return jnp.concatenate([one, jnp.zeros((16, 64), F32)], axis=1)
                return jnp.concatenate([one, a_conv[start + 128 : start + 144, 256:320]], axis=1)
            if at < G1_DOWN:
                b = at - G1_UP
                return a_up[rows, 128 * b : 128 * b + 128]
            if at < G1_PROJ:
                start = 64 * (shard % 2) + 16 * (at - G1_DOWN)
                return down[shard // 2][start : start + 16, :]
            return a_proj[rows, :]

        for peer in range(4):
            to = lax.bitwise_xor(chip, peer)
            for at in range(G1_VEC):
                one, two = piece(at, 2 * peer), piece(at, 2 * peer + 1)
                keep_ref[to, 16 * at : 16 * at + 16, :] = jnp.where(core == 0, one, two)
                send_ref[to, 16 * at : 16 * at + 16, :] = jnp.where(core == 0, two, one).astype(BF)
            for at, values in ((G1_VEC, vectors), (G1_VEC_LOW, vectors_low)):
                keep_ref[to, 16 * at : 16 * at + 16, :] = values
                send_ref[to, 16 * at : 16 * at + 16, :] = values.astype(BF)


def branch_kernel(
    placed, valid, unit_ref, mix_ref, head_ref, reduce_ref, expand_ref, units_ref, gcat_ref, dmix_ref,
    vec_ref, pk_ref,
    spread_ref, keep_ref, send_ref,
    wcat, a_cat, a_edge, grads,
):
    step, steps = pl.program_id(0), pl.num_programs(0)
    count = unit_ref.shape[0] // BRANCH_STEPS

    @pl.when(step == 0)
    def _():
        for k, weight in enumerate(branch_weights(pk_ref)):
            wcat[128 * k : 128 * k + 128, :] = weight.astype(F32)
        for ref in (a_cat, a_edge, grads):
            ref[...] = jnp.zeros(ref.shape, ref.dtype)

    def row(at, width=128):
        return vec_ref[at : at + 1, 0:width]

    offsets = (iota((128, 128), 0) + 1) % 3 - 1
    for m in range(count):
        image = step * count + m
        outer = dot_tn(unit_ref[image], gcat_ref[image])
        plain = outer[:, 0:128]
        parts = (
            jnp.where(offsets == 1, outer[:, 128:256], jnp.where(offsets == -1, outer[:, 256:384], plain)),
            jnp.where(offsets == 1, outer[:, 384:512], jnp.where(offsets == -1, outer[:, 512:640], plain)),
            plain,
        )
        maps = gcat_ref[image, :, 0:128].astype(F32).reshape(32, 32, 128)
        by_column = jnp.sum(maps, axis=0)
        total = jnp.sum(by_column, axis=0, keepdims=True)
        left, right = by_column[0:1], by_column[31:32]
        upper = jnp.sum(maps[0], axis=0, keepdims=True)
        lower = jnp.sum(maps[31], axis=0, keepdims=True)
        for k in range(3):
            at = 8 * k + image
            part = parts[k]
            mixing = mix_ref[pl.ds(at, 1), :]
            a_cat[128 * k : 128 * k + 128, :] += part * mixing
            a_edge[k : k + 1, :] += mixing * total
            if k == 0:
                a_edge[3:4, :] += mixing * lower
                a_edge[4:5, :] += mixing * upper
            if k == 1:
                a_edge[5:6, :] += mixing * right
                a_edge[6:7, :] += mixing * left

    @pl.when(step == steps - 1)
    def _():
        counts = count_column(valid)
        pooled, hidden, slope = [head_ref[8 * at : 8 * at + 8, :] for at in range(3)]
        mixing = [mix_ref[8 * k : 8 * k + 8, :] for k in range(3)]
        grads_mix = [dmix_ref[8 * k : 8 * k + 8, :] for k in range(3)]
        mean = sum(m * g for m, g in zip(mixing, grads_mix))
        grad_logits = jnp.concatenate([m * (g - mean) for m, g in zip(mixing, grads_mix)], axis=1)
        grad_pre = dot_wide(grad_logits, expand_ref[...], dot_nt) * slope
        grad_pooled = dot_wide(grad_pre, reduce_ref[...], dot_nt)
        per_pixel = grad_pooled / counts
        branches = jnp.concatenate(branch_weights(pk_ref), axis=0)
        spread = dot_wide(per_pixel, branches, dot_nt)
        for k in range(3):
            spread_ref[8 * k : 8 * k + 8, :] = spread[:, 128 * k : 128 * k + 128]
        for at, part in enumerate(parts_of(outer_wide(pooled, grad_pre), 2)):
            grads[:, 32 * at : 32 * at + 32] = dot_nt(part, spread_matrix())[:, 0:32]
        picks = jnp.concatenate([pick_matrix(k) for k in range(3)], axis=1)
        grads[:, 128:512] = dot_nt(outer_wide(hidden, grad_logits).astype(BF), picks)
        summed = jnp.broadcast_to(jnp.sum(grad_logits, axis=0, keepdims=True), (8, 384))
        expand_bias = dot_wide(summed, picks, dot_nt)[0:1]
        reduce_bias = jnp.sum(grad_pre, axis=0, keepdims=True)
        pooled_sum = jnp.sum(grad_pooled, axis=0, keepdims=True)
        gain, bias = column(row(V_GAIN1)), column(row(V_BIAS1))
        unit_sums = jnp.concatenate([units_ref[8 * k : 8 * k + 8, :] for k in range(3)], axis=1)
        unit_part = a_cat[...] + outer_wide(unit_sums, per_pixel)
        edge_part = outer_wide(jnp.concatenate(inside_counts(valid), axis=1), per_pixel)
        to_gain, to_bias = jnp.zeros((128, 128), F32), jnp.zeros((128, 128), F32)
        for k in range(3):
            here = slice(128 * k, 128 * k + 128)
            edges = edge_part[here] + a_edge[k : k + 1, :]
            if k < 2:
                edges = edges - jnp.where(offsets == 1, a_edge[2 * k + 3 : 2 * k + 4, :], 0.0)
                edges = edges - jnp.where(offsets == -1, a_edge[2 * k + 4 : 2 * k + 5, :], 0.0)
            to_gain = to_gain + unit_part[here] * wcat[here, :]
            to_bias = to_bias + edges * wcat[here, :]
            a_cat[here, :] = gain * unit_part[here] + bias * edges
        ones = jnp.ones((8, 384), BF)
        chip, core = place_of(placed)
        vectors = jnp.concatenate(
            [
                dot_nt(ones, jnp.concatenate(parts_of(to_gain, 3), axis=1))[0:1],
                dot_nt(ones, jnp.concatenate(parts_of(to_bias, 3), axis=1))[0:1],
                a_edge[0:1, :] + pooled_sum,
                a_edge[1:2, :] + pooled_sum,
                reduce_bias,
                expand_bias[:, 0:128],
                expand_bias[:, 128:256],
                expand_bias[:, 256:384],
            ],
            axis=0,
        )
        vectors = jnp.concatenate(split_low(vectors), axis=0)

        def piece(at, shard):
            rows = slice(16 * shard, 16 * shard + 16)
            if at < G2_REDUCE:
                return a_cat[128 * at + 16 * shard : 128 * at + 16 * shard + 16, :]
            if at == G2_REDUCE:
                return grads[rows, 0:128]
            return jnp.concatenate(
                [grads[16 * shard : 16 * shard + 4, 128 * b : 128 * b + 128] for b in range(1, 4)]
                + [jnp.zeros((4, 128), F32)],
                axis=0,
            )

        for peer in range(4):
            to = lax.bitwise_xor(chip, peer)
            for at in range(G2_VEC):
                one, two = piece(at, 2 * peer), piece(at, 2 * peer + 1)
                keep_ref[to, 16 * at : 16 * at + 16, :] = jnp.where(core == 0, one, two)
                send_ref[to, 16 * at : 16 * at + 16, :] = jnp.where(core == 0, two, one).astype(BF)
            keep_ref[to, 16 * G2_VEC : 16 * G2_VEC + 16, :] = vectors
            send_ref[to, 16 * G2_VEC : 16 * G2_VEC + 16, :] = vectors.astype(BF)


def input_kernel(
    valid, x_ref, mix_ref, spread, gcat_ref, gfirst_ref, vec_ref, pk_ref, after, grad_ref, wcat
):
    step, count = pl.program_id(0), x_ref.shape[0]

    @pl.when(step == 0)
    def _():
        offsets = (iota((128, 128), 0) + 1) % 3 - 1
        height, width, channel = [weight.astype(F32) for weight in branch_weights(pk_ref)]
        for at, (weight, offset) in enumerate(
            ((height, 0), (height, 1), (height, -1), (width, 0), (width, 1), (width, -1))
        ):
            wcat[:, 128 * at : 128 * at + 128] = jnp.where(offsets == offset, weight, 0.0)
        wcat[:, 768:896] = channel

    for m in range(count):
        image = step * count + m
        by_height, by_width, by_channel = [mix_ref[pl.ds(8 * k + image, 1), :] for k in range(3)]
        scaled = jnp.concatenate(
            [
                wcat[:, 0:128] * by_height + wcat[:, 384:512] * by_width + wcat[:, 768:896] * by_channel,
                wcat[:, 128:256] * by_height,
                wcat[:, 256:384] * by_height,
                wcat[:, 512:640] * by_width,
                wcat[:, 640:768] * by_width,
            ],
            axis=1,
        ).astype(BF)
        row, row_taker, col, col_taker = shifted_masks(valid, image)
        high, wide, plain = [spread[pl.ds(8 * k + image, 1), :].reshape(1, 1, 128) for k in range(3)]
        even = row * (col_taker * wide + col * plain) + row_taker * (col * high)
        grad_ref[m] = dot_nt(gcat_ref[image], scaled) + even.reshape(1024, 128)
    pixels = 1024 * count
    scaled_grad = grad_ref[...].reshape(pixels, 128) * vec_ref[V_GAIN1 : V_GAIN1 + 1, 0:128]
    values = x_ref[...].reshape(pixels, 128).astype(F32)
    centre = values - lane_mean(values)
    scale = lax.rsqrt(lane_mean(centre * centre) + EPS)
    unit = centre * scale
    grad = gfirst_ref[pl.ds(step * count, count)].reshape(pixels, 128) + scale * (
        scaled_grad - lane_mean(scaled_grad) - unit * lane_mean(scaled_grad * unit)
    )
    grad_ref[...] = grad.reshape(count, 1024, 128)


def conv_kernel(pm_ref, vec_ref, wconv, after, map_ref):
    count = map_ref.shape[0]
    here = pl.ds(pl.program_id(0) * count, count)
    out = dot(pm_ref[here].reshape(256 * count, 1152), wconv[...])
    out = out + vec_ref[V_BCONV : V_BCONV + 1, 0:384]
    map_ref[...] = out[:, 0:320].astype(BF).reshape(count, 256, 320)


def sds(shape, dtype):
    return jax.ShapeDtypeStruct(shape, dtype)


def whole(shape):
    return pl.BlockSpec(shape, lambda s: (0,) * len(shape))


def params(mega):
    return pltpu.CompilerParams(vmem_limit_bytes=mega * 1024 * 1024)


def cost(microseconds):
    return pl.CostEstimate(
        flops=int(microseconds * 3e8), bytes_accessed=int(microseconds * 3e6), transcendentals=0
    )


VMEM_SPEC = pl.BlockSpec(memory_space=pltpu.VMEM)
ANY_SPEC = pl.BlockSpec(memory_space=pl.ANY)


def in_vmem(value):
    return pltpu.with_memory_space_constraint(value, pltpu.VMEM)


def in_hbm(value):
    return pltpu.with_memory_space_constraint(value, pltpu.HBM)


def per_step(shape, index):
    return pl.BlockSpec(shape, lambda s: (index(s),) + (0,) * (len(shape) - 1))


def same(step):
    return step


UNIT_IMAGES, MLP_IMAGES, INPUT_IMAGES, CONV_IMAGES = 2, 2, 2, 2
BRANCH_STEPS = 2
SMALL_MB, UNIT_MB, NORM_MB, MLP_MB, BRANCH_MB, INPUT_MB, CONV_MB = 8, 16, 16, 30, 16, 20, 16


def run_unit(valid, x):
    images, count = x.shape[0], UNIT_IMAGES
    return pl.pallas_call(
        unit_kernel,
        grid=(images // count,),
        in_specs=[VMEM_SPEC, per_step((count, 1024, 128), same)],
        out_specs=[VMEM_SPEC] * 3,
        out_shape=[
            pltpu.VMEM((images, 1024, 128), F32),
            pltpu.VMEM((images, 1024, 128), BF),
            sds((24, 128), F32),
        ],
        compiler_params=params(UNIT_MB),
        cost_estimate=cost(4),
        name="unit",
    )(valid, in_hbm(x))


def run_norm(placed, valid, unit, *parts):
    images = unit.shape[0]
    return pl.pallas_call(
        functools.partial(norm_kernel, placed),
        in_specs=[VMEM_SPEC] * 6,
        out_specs=[VMEM_SPEC] * 7,
        out_shape=[
            pltpu.VMEM((images, 1024, 128), BF),
            sds((24, 128), F32),
            sds((128, 128), BF),
            sds((128, 384), BF),
            sds((24, 128), F32),
            sds((16, 512), F32),
            pltpu.VMEM((SHARDS, ROWS, 128), BF),
        ],
        scratch_shapes=[pltpu.VMEM((24, 128), F32)],
        compiler_params=params(NORM_MB),
        cost_estimate=cost(5),
        name="norm",
    )(valid, in_vmem(unit), *parts)


def run_mlp(placed, x, normed, mix, cot, vec, packed, *conv):
    images, count = x.shape[0], MLP_IMAGES
    pixels = 1024 * count
    g1 = (4, 16 * G1_BLOCKS, 128)
    shapes = [
        ((384, 128), BF), ((128, 128), BF), ((128, 512), BF), ((512, 128), BF),
        ((32 * count, 32, 128), F32), ((count, 34, 48, 128), F32),
        ((pixels, 512), BF), ((pixels, 512), BF), ((pixels, 128), BF), ((pixels, 384), F32), ((pixels, 128), BF),
        ((pixels, 128), BF), ((pixels, 128), BF), ((count, 34, 48, 128), F32), ((count, 32, 48, 128), F32),
        ((count, 272, 384), BF), ((count, 272, 384), BF), ((264, 384), F32),
        ((1152, 384), F32), ((128, 512), F32), ((128, 512), F32), ((128, 128), F32),
        ((8, 384), F32), ((8, 512), F32), ((8, 128), F32), ((8, 128), F32), ((8, 128), F32), ((8, 128), F32),
    ]
    return pl.pallas_call(
        functools.partial(mlp_kernel, placed),
        grid=(images // count,),
        in_specs=[
            per_step((count, 1024, 128), same),
            VMEM_SPEC,
            VMEM_SPEC,
            per_step((count, 256, 320), same),
            VMEM_SPEC,
            VMEM_SPEC,
            VMEM_SPEC,
            VMEM_SPEC,
            VMEM_SPEC,
            VMEM_SPEC,
        ],
        out_specs=[VMEM_SPEC] * 7,
        out_shape=[
            pltpu.VMEM((images, 256, 1152), BF),
            pltpu.VMEM((images, 1024, 128), F32),
            pltpu.VMEM((images, 1024, 640), BF),
            sds((24, 128), F32),
            pltpu.VMEM((1152, 384), BF),
            sds(g1, F32),
            sds(g1, BF),
        ],
        scratch_shapes=[pltpu.VMEM(*shape) for shape in shapes],
        compiler_params=params(MLP_MB),
        cost_estimate=cost(35),
        name="mlp",
    )(in_hbm(x), in_vmem(normed), mix, cot, vec, in_vmem(packed), *conv)


def run_branches(placed, valid, unit, mix, head, reduce, expand, units, gcat, dmix, vec, packed):
    g2 = (4, 16 * G2_BLOCKS, 128)
    shapes = [
        ((384, 128), F32), ((384, 128), F32), ((8, 128), F32), ((128, 512), F32),
    ]
    return pl.pallas_call(
        functools.partial(branch_kernel, placed),
        grid=(BRANCH_STEPS,),
        in_specs=[VMEM_SPEC] * 11,
        out_specs=[VMEM_SPEC] * 3,
        out_shape=[sds((24, 128), F32), sds(g2, F32), sds(g2, BF)],
        scratch_shapes=[pltpu.VMEM(*shape) for shape in shapes],
        compiler_params=params(BRANCH_MB),
        cost_estimate=cost(8),
        name="branches",
    )(valid, in_vmem(unit), mix, head, reduce, expand, units, in_vmem(gcat), dmix, vec, in_vmem(packed))


def run_input(valid, x, mix, spread, gcat, gfirst, vec, packed, after):
    images, count = x.shape[0], INPUT_IMAGES
    maps = per_step((count, 1024, 128), same)
    return pl.pallas_call(
        input_kernel,
        grid=(images // count,),
        in_specs=[
            VMEM_SPEC, maps, VMEM_SPEC, VMEM_SPEC, VMEM_SPEC, VMEM_SPEC, VMEM_SPEC, VMEM_SPEC, ANY_SPEC,
        ],
        out_specs=maps,
        out_shape=sds((images, 1024, 128), F32),
        scratch_shapes=[pltpu.VMEM((128, 896), F32)],
        compiler_params=params(INPUT_MB),
        cost_estimate=cost(8),
        name="input_grad",
    )(valid, in_hbm(x), mix, spread, in_vmem(gcat), in_vmem(gfirst), vec, in_vmem(packed), after)


def run_conv(pm, vec, wconv, after):
    images, count = pm.shape[0], CONV_IMAGES
    return pl.pallas_call(
        conv_kernel,
        grid=(images // count,),
        in_specs=[VMEM_SPEC, VMEM_SPEC, VMEM_SPEC, ANY_SPEC],
        out_specs=per_step((count, 256, 320), same),
        out_shape=sds((images, 256, 320), BF),
        compiler_params=params(CONV_MB),
        cost_estimate=cost(4),
        name="conv_out",
    )(in_vmem(pm), vec, in_vmem(wconv), after)


def pack_weights(weights):
    return pl.pallas_call(
        pack_kernel,
        out_shape=sds((ROWS + CONV_ROWS, 128), BF),
        in_specs=[VMEM_SPEC] * 21,
        out_specs=VMEM_SPEC,
        scratch_shapes=[pltpu.VMEM((16, 128), F32)],
        compiler_params=params(60),
        name="pack",
    )(*weights)


def join_kernel(one, two, three, after, small, conv):
    for at, part in enumerate((one, two, three)):
        small[at] = part[0:ROWS, :]
        conv[at] = part[ROWS : ROWS + CONV_ROWS, :]


def join(near, after):
    return pl.pallas_call(
        join_kernel,
        out_shape=[sds((3, ROWS, 128), BF), sds((3, CONV_ROWS, 128), BF)],
        in_specs=[VMEM_SPEC] * 3 + [ANY_SPEC],
        out_specs=[VMEM_SPEC] * 2,
        compiler_params=params(SMALL_MB),
        cost_estimate=cost(1),
        name="join",
    )(*near, after)


def refine(ref, values):
    ref[...] = values.astype(BF)
    at = 16 * G1_VEC
    both = split_low(values[at : at + 16] + values[at + 16 : at + 32])
    ref[at : at + 32, :] = jnp.concatenate(both, axis=0).astype(BF)
    at = 16 * (G1_BLOCKS + G2_VEC)
    both = split_low(values[at : at + 8] + values[at + 8 : at + 16])
    ref[at : at + 16, :] = jnp.concatenate(both, axis=0).astype(BF)
    at = 16 * (G1_BLOCKS + G2_REDUCE)
    both = split_low(values[at : at + 16, 0:32] + values[at : at + 16, 32:64])
    ref[at : at + 16, 0:64] = jnp.concatenate(both, axis=1).astype(BF)


def sum_pair_kernel(keep1, got1, keep2, got2, own, *others):
    for peer in range(4):
        one = keep1[peer] + got1[peer].astype(F32)
        two = keep2[peer] + got2[peer].astype(F32)
        values = jnp.concatenate([one, two], axis=0)
        if peer == 0:
            own[...] = values
        else:
            refine(others[peer - 1], values)


def sum_four_kernel(own, one, two, three, total, low):
    value = own[...] + one[...].astype(F32) + two[...].astype(F32) + three[...].astype(F32)
    total[...] = value
    refine(low, value)


def sum_pair(keep1, got1, keep2, got2):
    rows = keep1.shape[1] + keep2.shape[1]
    return pl.pallas_call(
        sum_pair_kernel,
        out_shape=[sds((rows, 128), F32)] + [sds((rows, 128), BF)] * 3,
        in_specs=[VMEM_SPEC] * 4,
        out_specs=[VMEM_SPEC] * 4,
        compiler_params=params(SMALL_MB),
        cost_estimate=cost(2),
        name="sum_pair",
    )(keep1, got1, keep2, got2)


def sum_four(*values):
    shape = values[0].shape
    return pl.pallas_call(
        sum_four_kernel,
        out_shape=[sds(shape, F32), sds(shape, BF)],
        in_specs=[VMEM_SPEC] * 4,
        out_specs=[VMEM_SPEC] * 2,
        compiler_params=params(SMALL_MB),
        cost_estimate=cost(2),
        name="sum_four",
    )(*values)


def finish_kernel(*refs):
    (one0, one1, one2, one3,
     gain_one, bias_one, w_h, b_h, w_w, b_w, w_c, w_red, b_red, w_exp, b_exp, w_proj, b_proj,
     gain_two, bias_two, w_up, b_up, w_down, b_down, w_conv, b_conv) = refs
    shard = lax.axis_index("fsdp")

    def first(at, rows=16):
        here = slice(16 * at, 16 * at + rows)
        return (one0[here, :] + one1[here, :].astype(F32)) + (
            one2[here, :].astype(F32) + one3[here, :].astype(F32)
        )

    def second(at, rows=16):
        return first(G1_BLOCKS + at, rows)

    w_h[...] = second(G2_HEIGHT)
    w_w[...] = second(G2_WIDTH)
    w_c[...] = second(G2_CHANNEL)
    reduce = second(G2_REDUCE)
    w_red[...] = reduce[:, 0:32] + reduce[:, 32:64]
    expand = second(G2_EXPAND)
    for b in range(3):
        w_exp[:, 128 * b : 128 * b + 128] = expand[4 * b : 4 * b + 4, :]
    w_proj[...] = first(G1_PROJ)
    for b in range(4):
        w_up[:, 128 * b : 128 * b + 128] = first(G1_UP + b)
    w_down[...] = first(G1_DOWN, 64)
    for at, tap in enumerate(TAPS):
        kernel = w_conv.at[tap // 3, tap % 3]
        for b in range(2):
            kernel[:, 128 * b : 128 * b + 128] = first(G1_CONV + 2 * at + b)
        edge = 64 * (at % 2)
        kernel[:, 256:320] = first(G1_EDGE + at // 2)[:, edge : edge + 64]
    table_one, table_two = first(G1_VEC) + first(G1_VEC_LOW), second(G2_VEC)
    table_two = table_two[0:8, :] + table_two[8:16, :]

    def share(table, row, blocks, length, stride):
        total = jnp.zeros((1, 128), F32)
        for b in range(blocks):
            pick = iota((128, 128), 0) + 128 * b == iota((128, 128), 1) + shard * stride
            total = total + dot_wide(table, pick.astype(BF))[row + b : row + b + 1, :]
        return total[:, 0:length].reshape(length)

    gain_one[...] = share(table_two, G2_GAIN1, 1, 16, 16)
    bias_one[...] = share(table_two, G2_BIAS1, 1, 16, 16)
    b_h[...] = share(table_two, G2_BH, 1, 16, 16)
    b_w[...] = share(table_two, G2_BW, 1, 16, 16)
    b_red[...] = share(table_two, G2_BR, 1, 4, 16)
    b_exp[...] = share(table_two, G2_BE, 3, 48, 48)
    b_proj[...] = share(table_one, G1_BPROJ, 1, 16, 16)
    gain_two[...] = share(table_one, G1_GAIN2, 1, 16, 16)
    bias_two[...] = share(table_one, G1_BIAS2, 1, 16, 16)
    b_up[...] = share(table_one, G1_BUP, 4, 64, 64)
    b_down[...] = share(table_one, G1_BDOWN, 1, 16, 16)
    b_conv[...] = share(table_one, G1_BCONV, 3, 40, 40)


def finish(sums, weights):
    return pl.pallas_call(
        finish_kernel,
        out_shape=[sds(w.shape, F32) for w in weights],
        in_specs=[VMEM_SPEC] * 4,
        out_specs=[VMEM_SPEC] * 21,
        compiler_params=params(SMALL_MB),
        name="finish",
    )(*sums)


def early(placed, input_map, valid_size, cotangent, gathered):
    images = input_map.shape[0]
    x = input_map.reshape(images, 1024, 128)
    valid_size = valid_size.T
    cot = cotangent.reshape(images, 256, 320)
    unit, unit_low, units = run_unit(valid_size, x)
    small, conv = gathered(units)
    normed, head, reduce, expand, mix, vec, packed = run_norm(placed, valid_size, unit, *small)
    pm, gfirst, gcat, dmix, wconv, keep1, send1 = run_mlp(
        placed, x, normed, mix, cot, vec, packed, *conv
    )
    spread, keep2, send2 = run_branches(
        placed, valid_size, unit_low, mix, head, reduce, expand, units, gcat, dmix, vec, packed
    )

    def late_map(after):
        return run_conv(pm, vec, wconv, after).reshape(images, 16, 16, 320)

    def late_grad(after):
        grad = run_input(valid_size, x, mix, spread, gcat, gfirst, vec, packed, after)
        return grad.reshape(images, 32, 32, 128)

    return (keep1, send1, keep2, send2), late_map, late_grad


def spread_out(packed):
    own = (packed[0], packed[1])
    return [
        own + (packed[2::2, rows], packed[3::2, rows]) for rows in (slice(0, ROWS), slice(ROWS, None))
    ]


def compute(placed, input_map, valid_size, cotangent, packed):
    sums, late_map, late_grad = early(
        placed,
        input_map,
        valid_size,
        cotangent,
        lambda after: spread_out(packed),
    )
    return late_map(sums[0]), late_grad(sums[0]), sums


def pack_whole(weights):
    (gain_one, bias_one, w_h, b_h, w_w, b_w, w_c, w_red, b_red, w_exp, b_exp, w_proj, b_proj,
     gain_two, bias_two, w_up, b_up, w_down, b_down, w_conv, b_conv) = weights

    def split(weight):
        weight = weight.reshape(SHARDS, weight.shape[0] // SHARDS, weight.shape[1])
        rows, cols = -weight.shape[1] % 16, -weight.shape[2] % 128
        weight = jnp.pad(weight, ((0, 0), (0, rows), (0, cols)))
        return [weight[:, :, at : at + 128] for at in range(0, weight.shape[2], 128)]

    pieces = split(w_h) + split(w_w) + split(w_c) + split(w_proj) + split(w_red) + split(w_exp)
    pieces = pieces + split(w_up) + split(w_down)
    taps = [split(w_conv[tap // 3, tap % 3]) for tap in TAPS]
    edges = [tap[2][:, :, 0:64] for tap in taps]
    edges.append(jnp.zeros_like(edges[0]))
    conv = [part for tap in taps for part in tap[0:2]]
    conv = conv + [jnp.concatenate(edges[at : at + 2], axis=2) for at in range(0, 10, 2)]
    vectors = (gain_one, bias_one, b_h, b_w, b_red, b_exp, b_proj, gain_two, bias_two, b_up, b_down, b_conv)
    rows = [
        jnp.pad(v.reshape(SHARDS, 1, v.shape[0] // SHARDS), ((0, 0), (0, 0), (0, 128 - v.shape[0] // SHARDS)))
        for v in vectors
    ]
    rows = rows + [jnp.zeros((SHARDS, 4, 128), BF)]
    return jnp.concatenate(pieces + [jnp.concatenate(rows, axis=1)] + conv, axis=1)


def unpack_whole(sums):
    one = jnp.stack([sums[0], sums[1].astype(F32)], axis=1).reshape(SHARDS, -1, 128)
    two = jnp.stack([sums[2], sums[3].astype(F32)], axis=1).reshape(SHARDS, -1, 128)

    def join(buffer, at, blocks, rows=16):
        parts = [buffer[:, 16 * (at + b) : 16 * (at + b) + rows, :] for b in range(blocks)]
        return jnp.concatenate(parts, axis=2).reshape(SHARDS * rows, 128 * blocks)

    def vector(buffer, at, row, blocks=1):
        start, rest = 16 * at + row, 16 if at == G1_VEC else 8
        both = buffer[0, start : start + blocks, :] + buffer[0, start + rest : start + rest + blocks, :]
        return both.reshape(128 * blocks)

    expand = two[:, 16 * G2_EXPAND : 16 * G2_EXPAND + 12, :].reshape(SHARDS, 3, 4, 128)
    taps = []
    for tap in range(9):
        at = TAPS.index(tap)
        edge = join(one, G1_EDGE + at // 2, 1)[:, 64 * (at % 2) : 64 * (at % 2) + 64]
        taps.append(jnp.concatenate([join(one, G1_CONV + 2 * at, 2), edge], axis=1))
    return (
        vector(two, G2_VEC, G2_GAIN1),
        vector(two, G2_VEC, G2_BIAS1),
        join(two, G2_HEIGHT, 1),
        vector(two, G2_VEC, G2_BH),
        join(two, G2_WIDTH, 1),
        vector(two, G2_VEC, G2_BW),
        join(two, G2_CHANNEL, 1),
        join(two, G2_REDUCE, 1)[:, 0:32] + join(two, G2_REDUCE, 1)[:, 32:64],
        vector(two, G2_VEC, G2_BR).reshape(SHARDS, 16)[:, 0:4].reshape(32),
        expand.transpose(0, 2, 1, 3).reshape(32, 384),
        vector(two, G2_VEC, G2_BE, 3),
        join(one, G1_PROJ, 1),
        vector(one, G1_VEC, G1_BPROJ),
        vector(one, G1_VEC, G1_GAIN2),
        vector(one, G1_VEC, G1_BIAS2),
        join(one, G1_UP, 4),
        vector(one, G1_VEC, G1_BUP, 4),
        one[:, 16 * G1_DOWN : 16 * G1_DOWN + 64, :].reshape(512, 128),
        vector(one, G1_VEC, G1_BDOWN),
        jnp.stack(taps).reshape(3, 3, 128, 320),
        vector(one, G1_VEC, G1_BCONV, 3)[0:320],
    )


def shards_of(mesh):
    shards, copies = mesh.shape["fsdp"], mesh.shape["rep"]

    def eight(input_map, valid_size, *rest):
        weights, cotangent = rest[:-1], rest[-1]
        sibling = [(i, i ^ 1) for i in range(shards)]
        packs = pack_weights(weights)
        swapped = lax.ppermute(packs, "fsdp", sibling)
        near = [
            lax.ppermute(packs, "fsdp", [(i, i ^ (2 * peer)) for i in range(shards)])
            for peer in range(1, 4)
        ]

        def gathered(after):
            small, conv = join(near, after)
            own = (packs, swapped)
            return own + (small, lax.ppermute(small, "fsdp", sibling)), (
                own + (conv, lax.ppermute(conv, "fsdp", sibling))
            )

        (keep1, send1, keep2, send2), late_map, late_grad = early(
            True, input_map, valid_size, cotangent, gathered
        )
        got1, got2 = lax.ppermute(send1, "fsdp", sibling), lax.ppermute(send2, "fsdp", sibling)
        own, *others = sum_pair(keep1, got1, keep2, got2)
        moved = [
            lax.ppermute(value, "fsdp", [(i, i ^ (2 * (peer + 1))) for i in range(shards)])
            for peer, value in enumerate(others)
        ]
        out = late_map(own)
        total, low = sum_four(own, *moved)
        far = [
            lax.ppermute(low, "rep", [(i, (i + k) % copies) for i in range(copies)])
            for k in range(1, copies)
        ]
        input_grad = late_grad(total)
        return (out, input_grad) + tuple(finish((total, *far), weights))

    def general(input_map, valid_size, *rest):
        weights, cotangent = rest[:-1], rest[-1]
        dims = [2 if w.ndim == 4 else 0 for w in weights]
        full = [lax.all_gather(w, "fsdp", axis=d, tiled=True) for w, d in zip(weights, dims)]
        packed = pack_whole(full)
        out, input_grad, sums = compute(False, input_map, valid_size, cotangent, packed)
        grads = [
            lax.psum_scatter(g, "fsdp", scatter_dimension=d, tiled=True)
            for g, d in zip(unpack_whole(sums), dims)
        ]
        return (out, input_grad) + tuple(lax.psum(grads, "rep"))

    return eight if shards == SHARDS and copies == 4 else general


def solution(mesh):
    maps = P(("rep", "fsdp"), None, None, None)
    vector, matrix = P("fsdp"), P("fsdp", None)
    weights = (
        vector, vector, matrix, vector, matrix, vector, matrix, matrix, vector, matrix, vector,
        matrix, vector, vector, vector, matrix, vector, matrix, vector,
        P(None, None, "fsdp", None), vector,
    )
    return jax.shard_map(
        shards_of(mesh),
        mesh=mesh,
        in_specs=(maps, P(("rep", "fsdp"), None)) + weights + (maps,),
        out_specs=(maps, maps) + weights,
        check_vma=False,
    )
```

```python
import functools

import jax
import jax.numpy as jnp
from jax import lax
from jax.experimental import pallas as pl
from jax.experimental.pallas import tpu as pltpu
from jax.sharding import PartitionSpec as P

BF = jnp.bfloat16
F32 = jnp.float32
HIGH = lax.Precision.HIGHEST
EPS = 1e-05

SHARDS = 8
B_HEIGHT, B_WIDTH, B_CHANNEL, B_PROJ, B_REDUCE = 0, 1, 2, 3, 4
B_EXPAND, B_UP, B_DOWN, B_VEC, BLOCKS = 5, 8, 12, 16, 17
C_PAIRS, C_EDGES, C_BLOCKS = 0, 18, 23
ROWS, CONV_ROWS = 16 * BLOCKS, 16 * C_BLOCKS
TAPS = (4, 5, 7, 8, 3, 6, 1, 2, 0)
(V_GAIN1, V_BIAS1, V_BH, V_BW, V_BR, V_BE, V_BP, V_GAIN2, V_BIAS2, V_BUP, V_BDOWN, V_BCONV) = range(12)
LENGTHS = (16, 16, 16, 16, 4, 48, 16, 16, 16, 64, 16, 40)
G1_CONV, G1_EDGE, G1_UP, G1_DOWN, G1_PROJ, G1_VEC, G1_VEC_LOW, G1_BLOCKS = 0, 18, 23, 27, 31, 32, 33, 34
G1_BCONV, G1_BUP, G1_BDOWN, G1_BPROJ, G1_GAIN2, G1_BIAS2 = 0, 3, 7, 8, 9, 10
G2_HEIGHT, G2_WIDTH, G2_CHANNEL, G2_REDUCE, G2_EXPAND, G2_VEC, G2_BLOCKS = 0, 1, 2, 3, 4, 5, 6
G2_GAIN1, G2_BIAS1, G2_BH, G2_BW, G2_BR, G2_BE = 0, 1, 2, 3, 4, 5


def iota(shape, axis):
    return lax.broadcasted_iota(jnp.int32, shape, axis)


def dot(left, right):
    return jnp.dot(left, right, preferred_element_type=F32)


def dot_nt(left, right):
    return lax.dot_general(left, right, (((1,), (1,)), ((), ())), preferred_element_type=F32)


def dot_tn(left, right):
    return lax.dot_general(left, right, (((0,), (0,)), ((), ())), preferred_element_type=F32)


def parts_of(values, count):
    parts = []
    for _ in range(count):
        parts.append(values.astype(BF))
        values = values - parts[-1].astype(F32)
    return parts


def dot_wide(left, right, product=dot):
    rows = left.shape[0]
    joined = product(jnp.concatenate(parts_of(left, 3), axis=0), right)
    return joined[0:rows] + (joined[rows : 2 * rows] + joined[2 * rows : 3 * rows])


def outer_wide(left, right):
    (left_high, left_low), (right_high, right_low) = parts_of(left, 2), parts_of(right, 2)
    return dot_tn(
        jnp.concatenate([left_high, left_high, left_low, left_low], axis=0),
        jnp.concatenate([right_high, right_low, right_high, right_low], axis=0),
    )


def fold8(values):
    rows, cols = values.shape
    return jnp.sum(values.reshape(rows // 8, 8, cols), axis=0)


def lane_mean(values):
    return jnp.mean(values, axis=-1, keepdims=True)


def gelu_both(values):
    cdf = 0.5 + 0.5 * lax.erf(values * 0.7071067811865476)
    slope = cdf + values * (jnp.exp(-0.5 * (values * values)) * 0.3989422804014327)
    return values * cdf, slope


def gelu_twice(values):
    cdf = 1.0 + lax.erf(values * 0.7071067811865476)
    density = (values * 0.7978845608028654) * jnp.exp2((values * values) * -0.7213475204444817)
    return values * cdf, cdf + density


def split_low(values):
    high = values.astype(BF).astype(F32)
    return high, (values - high).astype(BF).astype(F32)


def block(packed, at):
    return packed[:, 16 * at : 16 * at + 16, :].reshape(128, 128)


def branch_weights(packed):
    return [block(packed, at) for at in (B_HEIGHT, B_WIDTH, B_CHANNEL)]


def spread_matrix():
    unit, lane = iota((128, 128), 0), iota((128, 128), 1)
    return ((lane == 16 * (unit // 4) + unit % 4) & (unit < 32)).astype(BF)


def pick_matrix(k):
    return (iota((384, 128), 0) == 3 * iota((384, 128), 1) + k).astype(BF)


def head_weights(packed, vec):
    w_reduce = dot(block(packed, B_REDUCE), spread_matrix()).astype(BF)
    expand = jnp.concatenate([block(packed, B_EXPAND + b) for b in range(3)], axis=1)
    picks = jnp.concatenate([pick_matrix(k) for k in range(3)], axis=1)
    w_expand = dot(expand, picks).astype(BF)
    b_expand = dot(vec[:, 0:384].astype(BF), picks)[V_BE : V_BE + 1, :]
    return w_reduce, w_expand, b_expand


def head_forward(sums, counts, branches, head, vec):
    w_reduce, w_expand, b_expand = head
    pooled = dot_wide(jnp.concatenate(sums, axis=1), branches) / counts
    pooled = pooled + (vec[V_BH : V_BH + 1, 0:128] + vec[V_BW : V_BW + 1, 0:128])
    pre = dot_wide(pooled, w_reduce) + vec[V_BR : V_BR + 1, 0:128]
    hidden, slope = gelu_both(pre)
    joined = dot_wide(hidden, w_expand) + b_expand
    logits = [joined[:, 128 * k : 128 * k + 128] for k in range(3)]
    top = jnp.maximum(jnp.maximum(logits[0], logits[1]), logits[2])
    powers = [jnp.exp(v - top) for v in logits]
    total = powers[0] + powers[1] + powers[2]
    return pooled, hidden, slope, [v / total for v in powers]


def column(row_values):
    stacked = jnp.where(iota((8, 128), 0) == 0, row_values, 0.0)
    return dot_tn(stacked.astype(BF), jnp.ones((8, 128), BF))


def size_columns(valid_ref):
    sizes = valid_ref[...].astype(F32).astype(BF)
    kind = iota((2, 128), 0)
    return [dot_tn(sizes, (kind == axis).astype(BF)) for axis in range(2)]


def inside_counts(valid_ref):
    high, wide = size_columns(valid_ref)
    offsets = jnp.broadcast_to(channel_offsets()[0, 0:1, :], (8, 128))

    def kept(size):
        past = jnp.where(offsets == 1, jnp.where(size == 32.0, 1.0, 0.0), 0.0)
        return size - past - jnp.where(offsets == -1, 1.0, 0.0)

    return [kept(high) * wide, kept(wide) * high, high * wide]


def count_column(valid_ref):
    high, wide = size_columns(valid_ref)
    return high * wide


def channel_offsets():
    return (iota((1, 32, 128), 2) + 1) % 3 - 1


def shifted_masks(valid_ref, image):
    sizes = jnp.where(iota((2, 8), 1) == image, valid_ref[...].astype(F32), 0.0)
    size = jnp.sum(sizes, axis=1, keepdims=True)
    masks = []
    for axis, shape in ((0, (32, 1, 128)), (1, (1, 32, 128))):
        limit = size[axis : axis + 1, :].reshape(1, 1, 1)
        at = iota(shape, axis)
        taker = at - ((iota(shape, 2) + 1) % 3 - 1)
        masks.append((at.astype(F32) < limit).astype(F32))
        masks.append(((taker >= 0) & (taker.astype(F32) < limit)).astype(F32))
    return masks


def class_sums(maps, masks):
    row, row_taker, col, col_taker = masks

    def by_row(mask):
        return jnp.sum((maps * mask).reshape(32, 4, 8, 128), axis=1)

    plain, taken = by_row(col), by_row(col_taker)
    return [
        jnp.sum(jnp.sum(rows * mask, axis=0), axis=0, keepdims=True)
        for rows, mask in ((plain, row_taker), (taken, row), (plain, row))
    ]


def place_of(placed):
    if not placed:
        return 0, 0
    shard = lax.axis_index("fsdp")
    return shard // 2, lax.rem(shard, 2)


def pack_kernel(*refs):
    (gain_one, bias_one, w_h, b_h, w_w, b_w, w_c, w_red, b_red, w_exp, b_exp, w_proj, b_proj,
     gain_two, bias_two, w_up, b_up, w_down, b_down, w_conv, b_conv, out, vec) = refs
    conv = out.at[ROWS : ROWS + CONV_ROWS]

    def put(at, values):
        out[16 * at : 16 * at + values.shape[0], 0 : values.shape[1]] = values

    put(B_HEIGHT, w_h[...])
    put(B_WIDTH, w_w[...])
    put(B_CHANNEL, w_c[...])
    put(B_PROJ, w_proj[...])
    blank = jnp.zeros((16, 128), BF)
    put(B_REDUCE, blank)
    put(B_REDUCE, w_red[...])
    for b in range(3):
        vec[...] = jnp.zeros((16, 128), F32)
        vec[0:4, :] = w_exp[:, 128 * b : 128 * b + 128].astype(F32)
        put(B_EXPAND + b, vec[...].astype(BF))
    for b in range(4):
        put(B_UP + b, w_up[:, 128 * b : 128 * b + 128])
    put(B_DOWN, w_down[...])
    conv[16 * (C_BLOCKS - 1) : 16 * C_BLOCKS, :] = blank
    for at, tap in enumerate(TAPS):
        kernel = w_conv.at[tap // 3, tap % 3]
        for b in range(2):
            start = 16 * (C_PAIRS + 2 * at + b)
            conv[start : start + 16, :] = kernel[:, 128 * b : 128 * b + 128]
        start, lane = 16 * (C_EDGES + at // 2), 64 * (at % 2)
        conv[start : start + 16, lane : lane + 64] = kernel[:, 256:320]
    vec[...] = jnp.zeros((16, 128), F32)
    vectors = (gain_one, bias_one, b_h, b_w, b_red, b_exp, b_proj, gain_two, bias_two, b_up, b_down, b_conv)
    for row, (values, length) in enumerate(zip(vectors, LENGTHS)):
        vec[row : row + 1, 0:length] = values[...].astype(F32).reshape(1, length)
    put(B_VEC, vec[...].astype(BF))


def vector_table(packed):
    shards = packed[:, 16 * B_VEC : 16 * B_VEC + 16, :].reshape(128, 128)
    table = jnp.zeros((16, 512), F32)
    rows = iota((16, 512), 0)
    for length in (16, 4, 48, 64, 40):
        step = 16 if length == 4 else length
        lane = iota((128, 512), 1)
        source = iota((128, 512), 0)
        pick = ((source == lane % step) & (source < length)).astype(BF)
        spread = dot(shards, pick)
        mine = (source // 16) == (lane // step)
        whole = jnp.sum(jnp.where(mine, spread, 0.0).reshape(8, 16, 512), axis=0)
        held = functools.reduce(
            jnp.logical_or, [rows == v for v, size in enumerate(LENGTHS) if size == length]
        )
        table = jnp.where(held, whole, table)
    return table


def unit_kernel(
    valid, x_ref, cot_ref, unit_ref, low_ref, sums_ref, main_ref, right_ref, rest_ref, bias_ref, shift
):
    step, count = pl.program_id(0), x_ref.shape[0]

    @pl.when(step == 0)
    def _():
        shift[...] = jnp.zeros(shift.shape, F32)
        bias_ref[...] = jnp.zeros(bias_ref.shape, F32)

    lanes = iota((256, 128), 1) < 64
    blank, line = jnp.zeros((16, 256), BF), jnp.zeros((16, 128), F32)
    for m in range(count):
        cot = cot_ref[m].astype(F32)
        bias_ref[:, 0:320] += fold8(cot)
        shift[0:256, 0:320] = cot
        ahead = shift[1:257, :]
        ahead = jnp.where(iota((256, 384), 0) % 16 == 15, 0.0, ahead)
        main_ref[m, 0:256, :] = cot_ref[m, :, 0:256]
        main_ref[m, 256:272, :] = blank
        right_ref[m, 0:256, :] = ahead[:, 0:256].astype(BF)
        right_ref[m, 256:272, :] = blank
        both = jnp.where(lanes, shift[0:256, 256:384], pltpu.roll(ahead[:, 256:384], 64, 1))
        rest_ref[m, :, 0:128] = both.astype(BF)
        below = jnp.concatenate([both[16:256], line], axis=0)
        rest_ref[m, :, 128:256] = below.astype(BF)

    low = x_ref[...].reshape(count * 1024, 128)
    centre = low.astype(F32) - dot(low, jnp.full((128, 128), 1.0 / 128.0, BF))
    scale = lax.rsqrt(lane_mean(centre * centre) + EPS)
    unit = centre * scale
    here = pl.ds(step * count, count)
    unit_ref[here] = unit.reshape(count, 1024, 128)
    low_ref[here] = unit.astype(BF).reshape(count, 1024, 128)
    for m in range(count):
        image = step * count + m
        maps = unit[1024 * m : 1024 * m + 1024].reshape(32, 32, 128)
        for k, total in enumerate(class_sums(maps, shifted_masks(valid, image))):
            sums_ref[pl.ds(8 * k + image, 1), :] = total


def norm_kernel(
    placed, valid, unit_ref, own, swapped, mine, other,
    norm_ref, head_ref, reduce_ref, expand_ref, mix_ref, vec_ref, pk_ref, sums_ref
):
    chip, core = place_of(placed)
    pk_ref[2 * chip + core] = own[0:ROWS, :]
    pk_ref[2 * chip + (1 - core)] = swapped[0:ROWS, :]
    for peer in range(1, 4):
        shard = 2 * lax.bitwise_xor(chip, peer)
        pk_ref[shard + core] = mine[peer - 1]
        pk_ref[shard + (1 - core)] = other[peer - 1]
    vec = vector_table(pk_ref)
    vec_ref[...] = vec
    head = head_weights(pk_ref, vec)
    gain = vec[V_GAIN1 : V_GAIN1 + 1, 0:128]
    bias = vec[V_BIAS1 : V_BIAS1 + 1, 0:128]
    for image in range(unit_ref.shape[0]):
        low = (unit_ref[image] * gain + bias).astype(BF)
        norm_ref[image] = low
        maps = low.astype(F32).reshape(32, 32, 128)
        for k, total in enumerate(class_sums(maps, shifted_masks(valid, image))):
            sums_ref[8 * k + image : 8 * k + image + 1, :] = total
    sums = [sums_ref[8 * k : 8 * k + 8, :] for k in range(3)]
    branches = jnp.concatenate(branch_weights(pk_ref), axis=0)
    pooled, hidden, slope, mixing = head_forward(sums, count_column(valid), branches, head, vec)
    for at, values in enumerate((pooled, hidden, slope)):
        head_ref[8 * at : 8 * at + 8, :] = values
    reduce_ref[...], expand_ref[...] = head[0], head[1]
    for k in range(3):
        mix_ref[8 * k : 8 * k + 8, :] = mixing[k]


def mlp_kernel(
    placed, x_ref, norm_ref, mix_ref, main_ref, right_ref, rest_ref, bias_ref, vec_ref, pk_ref,
    own, swapped, conv_mine, conv_other,
    pm_ref, gfirst_ref, gcat_ref, dmix_ref, wconv, keep_ref, send_ref,
    wcat, wproj, wup, wdown, wrest,
    gsec, low, act, ghid, norm2, mixes, mixed_s, gtail, gbranch, npad,
    a_conv, a_rest, a_up, a_down, a_proj, a_bup, a_bdown, a_bproj, a_gain2, a_bias2,
):
    step, steps, count = pl.program_id(0), pl.num_programs(0), x_ref.shape[0]

    @pl.when(step == 0)
    def _():
        for k, weight in enumerate(branch_weights(pk_ref)):
            wcat[128 * k : 128 * k + 128, :] = weight
        wproj[...] = block(pk_ref, B_PROJ)
        for b in range(4):
            wup[:, 128 * b : 128 * b + 128] = block(pk_ref, B_UP + b)
        wdown[...] = pk_ref[:, 16 * B_DOWN : 16 * B_DOWN + 64, :].reshape(512, 128) * jnp.bfloat16(0.5)
        chip, core = place_of(placed)
        blank = jnp.zeros((16, 64), BF)
        for peer in range(4):
            conv = slice(ROWS, ROWS + CONV_ROWS)
            pair = (own.at[conv], swapped.at[conv])
            if peer > 0:
                pair = (conv_mine.at[peer - 1], conv_other.at[peer - 1])
            for part, odd in zip(pair, (core, 1 - core)):
                shard = 2 * lax.bitwise_xor(chip, peer) + odd
                for at in range(9):
                    rows = pl.ds(pl.multiple_of(128 * at + 16 * shard, 16), 16)
                    for b in range(2):
                        start = 16 * (C_PAIRS + 2 * at + b)
                        wconv[rows, 128 * b : 128 * b + 128] = part[start : start + 16, :]
                    start, lane = 16 * (C_EDGES + at // 2), 64 * (at % 2)
                    edge = part[start : start + 16, :][:, lane : lane + 64]
                    wconv[rows, 256:384] = jnp.concatenate([edge, blank], axis=1)
        none = jnp.zeros((128, 64), BF)
        for output, places in enumerate(((0, None, None, None), (1, 4, None, None), (2, None, 6, None), (3, 5, 7, 8))):
            ends = [none if at is None else wconv[128 * at : 128 * at + 128, 256:320] for at in places]
            rows = slice(128 * output, 128 * output + 128)
            wrest[rows, 0:128] = jnp.concatenate(ends[0:2], axis=1)
            wrest[rows, 128:256] = jnp.concatenate(ends[2:4], axis=1)
        for ref in (low, npad):
            ref[:, 0:1] = jnp.zeros((count, 1, 48, 128), F32)
            ref[:, 33:34] = jnp.zeros((count, 1, 48, 128), F32)
        for ref in (low, npad):
            shape = ref.shape[0:2] + (8, 128)
            ref[:, :, 0:8, :] = jnp.zeros(shape, F32)
            ref[:, :, 40:48, :] = jnp.zeros(shape, F32)
        for ref in (a_conv, a_rest, a_up, a_down, a_proj, a_bup, a_bdown, a_bproj, a_gain2, a_bias2):
            ref[...] = jnp.zeros(ref.shape, ref.dtype)

    def row(at, width=128):
        return vec_ref[at : at + 1, 0:width]

    images = range(count)
    maps = [step * count + m for m in images]
    pixels = [slice(1024 * m, 1024 * m + 1024) for m in images]

    offsets = channel_offsets()
    forth, back = offsets == 1, offsets == -1
    for m in images:
        mixing = [mix_ref[pl.ds(8 * k + maps[m], 1), :] for k in range(3)]
        biases = (row(V_BH), row(V_BW), 0.0)
        normed = norm_ref[maps[m]]
        here = normed.astype(F32).reshape(32, 32, 128)
        npad[m, 1:33, 8:40, :] = here
        high = jnp.where(
            forth, npad[m, 2:34, 8:40, :], jnp.where(back, npad[m, 0:32, 8:40, :], here)
        )
        wide = jnp.where(
            forth, npad[m, 1:33, 9:41, :], jnp.where(back, npad[m, 1:33, 7:39, :], here)
        )
        shifted = (high.reshape(1024, 128).astype(BF), wide.reshape(1024, 128).astype(BF), normed)
        mixed = 0.0
        for k in range(3):
            branch = dot(shifted[k], wcat[128 * k : 128 * k + 128, :]) + biases[k]
            mixes[pixels[m], 128 * k : 128 * k + 128] = branch
            mixed = mixed + branch * mixing[k]
        mixed_s[pixels[m], :] = mixed.astype(BF)
    first, unit, scale = [None] * count, [None] * count, [None] * count
    for m in images:
        added = dot(mixed_s[pixels[m], :], wproj[...]) + row(V_BP)
        first[m] = x_ref[m].astype(F32) + added
        centre = first[m] - lane_mean(first[m])
        scale[m] = lax.rsqrt(lane_mean(centre * centre) + EPS)
        unit[m] = centre * scale[m]
        norm2[pixels[m], :] = (unit[m] * row(V_GAIN2) + row(V_BIAS2)).astype(BF)

    flat = (count * 256, 256)
    cot_here, cot_right = main_ref[:, 0:256, :].reshape(flat), right_ref[:, 0:256, :].reshape(flat)
    cot_below, cot_both = main_ref[:, 16:272, :].reshape(flat), right_ref[:, 16:272, :].reshape(flat)
    cot_rest = rest_ref[...].reshape(flat)
    ends = dot_nt(cot_rest, wrest[...])
    from_here = dot_nt(cot_here, wconv[0:512, 0:256])
    from_right = dot_nt(cot_right, wconv[512:768, 0:256])
    from_below = dot_nt(cot_below, wconv[768:1024, 0:256])
    from_both = dot_nt(cot_both, wconv[1024:1152, 0:256])
    straight = from_here + ends
    planes = (
        (straight[:, 0:128], straight[:, 128:256] + from_right[:, 0:128]),
        (
            straight[:, 256:384] + from_below[:, 0:128],
            (straight[:, 384:512] + from_right[:, 128:256]) + (from_below[:, 128:256] + from_both),
        ),
    )
    for p in range(2):
        for s in range(2):
            plane = planes[p][s]
            for i in range(16 * count):
                gsec[2 * i + p, pl.ds(s, 16, stride=2), :] = plane[16 * i : 16 * i + 16, :]

    grad_second = [gsec[32 * m : 32 * m + 32].reshape(1024, 128) for m in images]
    for m in images:
        tail = grad_second[m].astype(BF)
        gtail[pixels[m], :] = tail
        a_bdown[...] += fold8(grad_second[m])
        for b in range(2):
            cols = slice(256 * b, 256 * b + 256)
            hidden = dot(norm2[pixels[m], :], wup[:, cols]) + vec_ref[V_BUP : V_BUP + 1, cols]
            grad_act = dot_nt(tail, wdown[cols, :])
            value, slope = gelu_twice(hidden)
            act[pixels[m], cols] = value.astype(BF)
            grad_hidden = grad_act * slope
            ghid[pixels[m], cols] = grad_hidden.astype(BF)
            a_bup[:, cols] += fold8(grad_hidden)
    grad_first = [None] * count
    for m in images:
        second = first[m] + (dot(act[pixels[m], :], wdown[...]) + row(V_BDOWN))
        low[m, 1:33, 8:40, :] = second.reshape(32, 32, 128)
        grad_normed = dot_nt(ghid[pixels[m], :], wup[...])
        a_gain2[...] += fold8(grad_normed * unit[m])
        a_bias2[...] += fold8(grad_normed)
        scaled_grad = grad_normed * row(V_GAIN2)
        grad_first[m] = grad_second[m] + scale[m] * (
            scaled_grad - lane_mean(scaled_grad) - unit[m] * lane_mean(scaled_grad * unit[m])
        )
        gfirst_ref[m] = grad_first[m]
        gbranch[pixels[m], :] = grad_first[m].astype(BF)
        a_bproj[...] += fold8(grad_first[m])
    a_up[...] += dot_tn(norm2[...], ghid[...])
    a_down[...] += dot_tn(gtail[...], act[...])
    for m in images:
        grad_mixed = dot_nt(gbranch[pixels[m], :], wproj[...])
        for k in range(3):
            share = fold8(grad_mixed * mixes[pixels[m], 128 * k : 128 * k + 128])
            dmix_ref[pl.ds(8 * k + maps[m], 1), :] = jnp.sum(share, axis=0, keepdims=True)
        npad[m, 1:33, 8:40, :] = grad_mixed.reshape(32, 32, 128)
        low_grad, image = grad_mixed.astype(BF), maps[m]
        gcat_ref[image, :, 0:128] = low_grad
        gcat_ref[image, 0:32, 128:256] = jnp.zeros((32, 128), BF)
        gcat_ref[image, 32:1024, 128:256] = low_grad[0:992]
        gcat_ref[image, 0:992, 256:384] = low_grad[32:1024]
        gcat_ref[image, 992:1024, 256:384] = jnp.zeros((32, 128), BF)
        gcat_ref[image, :, 384:512] = npad[m, 1:33, 7:39, :].reshape(1024, 128).astype(BF)
        gcat_ref[image, :, 512:640] = npad[m, 1:33, 9:41, :].reshape(1024, 128).astype(BF)

    for at, tap in enumerate(TAPS):
        r, s = tap // 3, tap % 3
        for m in images:
            patch = low[m, pl.ds(r, 16, stride=2), pl.ds(7 + s, 16, stride=2), :]
            pm_ref[maps[m], :, 128 * at : 128 * at + 128] = patch.reshape(256, 128).astype(BF)

    a_proj[...] += dot_tn(mixed_s[...], gbranch[...])
    patches = pm_ref[pl.ds(step * count, count)].reshape(256 * count, 1152)
    a_conv[...] += dot_tn(patches, cot_here)
    a_rest[...] += dot_tn(cot_rest[:, 0:64], patches)

    @pl.when(step == steps - 1)
    def _():
        chip, core = place_of(placed)[0:2]
        vectors = jnp.concatenate(
            [jnp.sum(bias_ref[:, 128 * b : 128 * b + 128], axis=0, keepdims=True) for b in range(3)]
            + [jnp.sum(a_bup[:, 128 * b : 128 * b + 128], axis=0, keepdims=True) for b in range(4)]
            + [jnp.sum(ref[...], axis=0, keepdims=True) for ref in (a_bdown, a_bproj, a_gain2, a_bias2)]
            + [jnp.zeros((5, 128), F32)],
            axis=0,
        )
        vectors, vectors_low = split_low(vectors)
        down = [0.5 * a_down[:, 128 * b : 128 * b + 128].T for b in range(4)]
        edges = [a_rest[:, 128 * t : 128 * t + 128].T for t in range(9)]

        def piece(at, shard):
            rows = slice(16 * shard, 16 * shard + 16)
            if at < G1_EDGE:
                start = 128 * (at // 2) + 16 * shard
                return a_conv[start : start + 16, 128 * (at % 2) : 128 * (at % 2) + 128]
            if at < G1_UP:
                one = edges[2 * (at - G1_EDGE)][rows]
                two = jnp.zeros((16, 64), F32)
                if at < G1_UP - 1:
                    two = edges[2 * (at - G1_EDGE) + 1][rows]
                return jnp.concatenate([one, two], axis=1)
            if at < G1_DOWN:
                b = at - G1_UP
                return a_up[rows, 128 * b : 128 * b + 128]
            if at < G1_PROJ:
                start = 64 * (shard % 2) + 16 * (at - G1_DOWN)
                return down[shard // 2][start : start + 16, :]
            return a_proj[rows, :]

        for peer in range(4):
            to = lax.bitwise_xor(chip, peer)
            for at in range(G1_VEC):
                one, two = piece(at, 2 * peer), piece(at, 2 * peer + 1)
                keep_ref[to, 16 * at : 16 * at + 16, :] = jnp.where(core == 0, one, two)
                send_ref[to, 16 * at : 16 * at + 16, :] = jnp.where(core == 0, two, one).astype(BF)
            for at, values in ((G1_VEC, vectors), (G1_VEC_LOW, vectors_low)):
                keep_ref[to, 16 * at : 16 * at + 16, :] = values
                send_ref[to, 16 * at : 16 * at + 16, :] = values.astype(BF)


def branch_kernel(
    placed, valid, unit_ref, mix_ref, head_ref, reduce_ref, expand_ref, units_ref, gcat_ref, dmix_ref,
    vec_ref, pk_ref,
    spread_ref, keep_ref, send_ref,
    wcat, a_cat, a_edge, grads,
):
    step, steps = pl.program_id(0), pl.num_programs(0)
    count = unit_ref.shape[0] // BRANCH_STEPS

    @pl.when(step == 0)
    def _():
        for k, weight in enumerate(branch_weights(pk_ref)):
            wcat[128 * k : 128 * k + 128, :] = weight.astype(F32)
        for ref in (a_cat, a_edge, grads):
            ref[...] = jnp.zeros(ref.shape, ref.dtype)

    def row(at, width=128):
        return vec_ref[at : at + 1, 0:width]

    offsets = (iota((128, 128), 0) + 1) % 3 - 1
    for m in range(count):
        image = step * count + m
        outer = dot_tn(unit_ref[image], gcat_ref[image])
        plain = outer[:, 0:128]
        parts = (
            jnp.where(offsets == 1, outer[:, 128:256], jnp.where(offsets == -1, outer[:, 256:384], plain)),
            jnp.where(offsets == 1, outer[:, 384:512], jnp.where(offsets == -1, outer[:, 512:640], plain)),
            plain,
        )
        maps = gcat_ref[image, :, 0:128].astype(F32).reshape(32, 32, 128)
        by_column = jnp.sum(maps, axis=0)
        total = jnp.sum(by_column, axis=0, keepdims=True)
        left, right = by_column[0:1], by_column[31:32]
        upper = jnp.sum(maps[0], axis=0, keepdims=True)
        lower = jnp.sum(maps[31], axis=0, keepdims=True)
        for k in range(3):
            at = 8 * k + image
            part = parts[k]
            mixing = mix_ref[pl.ds(at, 1), :]
            a_cat[128 * k : 128 * k + 128, :] += part * mixing
            a_edge[k : k + 1, :] += mixing * total
            if k == 0:
                a_edge[3:4, :] += mixing * lower
                a_edge[4:5, :] += mixing * upper
            if k == 1:
                a_edge[5:6, :] += mixing * right
                a_edge[6:7, :] += mixing * left

    @pl.when(step == steps - 1)
    def _():
        counts = count_column(valid)
        pooled, hidden, slope = [head_ref[8 * at : 8 * at + 8, :] for at in range(3)]
        mixing = [mix_ref[8 * k : 8 * k + 8, :] for k in range(3)]
        grads_mix = [dmix_ref[8 * k : 8 * k + 8, :] for k in range(3)]
        mean = sum(m * g for m, g in zip(mixing, grads_mix))
        grad_logits = jnp.concatenate([m * (g - mean) for m, g in zip(mixing, grads_mix)], axis=1)
        grad_pre = dot_wide(grad_logits, expand_ref[...], dot_nt) * slope
        grad_pooled = dot_wide(grad_pre, reduce_ref[...], dot_nt)
        per_pixel = grad_pooled / counts
        branches = jnp.concatenate(branch_weights(pk_ref), axis=0)
        spread = dot_wide(per_pixel, branches, dot_nt)
        for k in range(3):
            spread_ref[8 * k : 8 * k + 8, :] = spread[:, 128 * k : 128 * k + 128]
        for at, part in enumerate(parts_of(outer_wide(pooled, grad_pre), 2)):
            grads[:, 32 * at : 32 * at + 32] = dot_nt(part, spread_matrix())[:, 0:32]
        picks = jnp.concatenate([pick_matrix(k) for k in range(3)], axis=1)
        grads[:, 128:512] = dot_nt(outer_wide(hidden, grad_logits).astype(BF), picks)
        summed = jnp.broadcast_to(jnp.sum(grad_logits, axis=0, keepdims=True), (8, 384))
        expand_bias = dot_wide(summed, picks, dot_nt)[0:1]
        reduce_bias = jnp.sum(grad_pre, axis=0, keepdims=True)
        pooled_sum = jnp.sum(grad_pooled, axis=0, keepdims=True)
        gain, bias = column(row(V_GAIN1)), column(row(V_BIAS1))
        unit_sums = jnp.concatenate([units_ref[8 * k : 8 * k + 8, :] for k in range(3)], axis=1)
        unit_part = a_cat[...] + outer_wide(unit_sums, per_pixel)
        edge_part = outer_wide(jnp.concatenate(inside_counts(valid), axis=1), per_pixel)
        to_gain, to_bias = jnp.zeros((128, 128), F32), jnp.zeros((128, 128), F32)
        for k in range(3):
            here = slice(128 * k, 128 * k + 128)
            edges = edge_part[here] + a_edge[k : k + 1, :]
            if k < 2:
                edges = edges - jnp.where(offsets == 1, a_edge[2 * k + 3 : 2 * k + 4, :], 0.0)
                edges = edges - jnp.where(offsets == -1, a_edge[2 * k + 4 : 2 * k + 5, :], 0.0)
            to_gain = to_gain + unit_part[here] * wcat[here, :]
            to_bias = to_bias + edges * wcat[here, :]
            a_cat[here, :] = gain * unit_part[here] + bias * edges
        ones = jnp.ones((8, 384), BF)
        chip, core = place_of(placed)
        vectors = jnp.concatenate(
            [
                dot_nt(ones, jnp.concatenate(parts_of(to_gain, 3), axis=1))[0:1],
                dot_nt(ones, jnp.concatenate(parts_of(to_bias, 3), axis=1))[0:1],
                a_edge[0:1, :] + pooled_sum,
                a_edge[1:2, :] + pooled_sum,
                reduce_bias,
                expand_bias[:, 0:128],
                expand_bias[:, 128:256],
                expand_bias[:, 256:384],
            ],
            axis=0,
        )
        vectors = jnp.concatenate(split_low(vectors), axis=0)

        def piece(at, shard):
            rows = slice(16 * shard, 16 * shard + 16)
            if at < G2_REDUCE:
                return a_cat[128 * at + 16 * shard : 128 * at + 16 * shard + 16, :]
            if at == G2_REDUCE:
                return grads[rows, 0:128]
            return jnp.concatenate(
                [grads[16 * shard : 16 * shard + 4, 128 * b : 128 * b + 128] for b in range(1, 4)]
                + [jnp.zeros((4, 128), F32)],
                axis=0,
            )

        for peer in range(4):
            to = lax.bitwise_xor(chip, peer)
            for at in range(G2_VEC):
                one, two = piece(at, 2 * peer), piece(at, 2 * peer + 1)
                keep_ref[to, 16 * at : 16 * at + 16, :] = jnp.where(core == 0, one, two)
                send_ref[to, 16 * at : 16 * at + 16, :] = jnp.where(core == 0, two, one).astype(BF)
            keep_ref[to, 16 * G2_VEC : 16 * G2_VEC + 16, :] = vectors
            send_ref[to, 16 * G2_VEC : 16 * G2_VEC + 16, :] = vectors.astype(BF)


def input_kernel(base, valid, x_ref, mix_ref, spread, gcat_ref, gfirst_ref, vec_ref, pk_ref, *rest):
    grad_ref, token, wcat = rest[-3:]
    token[...] = jnp.zeros((8, 128), F32)
    step, count = pl.program_id(0), grad_ref.shape[0]

    @pl.when(step == 0)
    def _():
        offsets = (iota((128, 128), 0) + 1) % 3 - 1
        height, width, channel = [weight.astype(F32) for weight in branch_weights(pk_ref)]
        for at, (weight, offset) in enumerate(
            ((height, 0), (height, 1), (height, -1), (width, 0), (width, 1), (width, -1))
        ):
            wcat[:, 128 * at : 128 * at + 128] = jnp.where(offsets == offset, weight, 0.0)
        wcat[:, 768:896] = channel

    for m in range(count):
        image = base + step * count + m
        by_height, by_width, by_channel = [mix_ref[pl.ds(8 * k + image, 1), :] for k in range(3)]
        scaled = jnp.concatenate(
            [
                wcat[:, 0:128] * by_height + wcat[:, 384:512] * by_width + wcat[:, 768:896] * by_channel,
                wcat[:, 128:256] * by_height,
                wcat[:, 256:384] * by_height,
                wcat[:, 512:640] * by_width,
                wcat[:, 640:768] * by_width,
            ],
            axis=1,
        ).astype(BF)
        row, row_taker, col, col_taker = shifted_masks(valid, image)
        high, wide, plain = [spread[pl.ds(8 * k + image, 1), :].reshape(1, 1, 128) for k in range(3)]
        even = row * (col_taker * wide + col * plain) + row_taker * (col * high)
        grad_ref[m] = dot_nt(gcat_ref[image], scaled) + even.reshape(1024, 128)
    pixels = 1024 * count
    scaled_grad = grad_ref[...].reshape(pixels, 128) * vec_ref[V_GAIN1 : V_GAIN1 + 1, 0:128]
    here = pl.ds(base + step * count, count)
    values = x_ref[here].reshape(pixels, 128).astype(F32)
    centre = values - lane_mean(values)
    scale = lax.rsqrt(lane_mean(centre * centre) + EPS)
    unit = centre * scale
    grad = gfirst_ref[here].reshape(pixels, 128) + scale * (
        scaled_grad - lane_mean(scaled_grad) - unit * lane_mean(scaled_grad * unit)
    )
    grad_ref[...] = grad.reshape(count, 1024, 128)


def conv_kernel(pm_ref, vec_ref, wconv, after, map_ref, token):
    token[...] = jnp.zeros((8, 128), F32)
    count = map_ref.shape[0]
    here = pl.ds(pl.program_id(0) * count, count)
    out = dot(pm_ref[here].reshape(256 * count, 1152), wconv[...])
    out = out + vec_ref[V_BCONV : V_BCONV + 1, 0:384]
    map_ref[...] = out[:, 0:320].astype(BF).reshape(count, 256, 320)


def sds(shape, dtype):
    return jax.ShapeDtypeStruct(shape, dtype)


def whole(shape):
    return pl.BlockSpec(shape, lambda s: (0,) * len(shape))


def params(mega):
    return pltpu.CompilerParams(vmem_limit_bytes=mega * 1024 * 1024)


def cost(microseconds):
    return pl.CostEstimate(
        flops=int(microseconds * 3e8), bytes_accessed=int(microseconds * 3e6), transcendentals=0
    )


VMEM_SPEC = pl.BlockSpec(memory_space=pltpu.VMEM)
ANY_SPEC = pl.BlockSpec(memory_space=pl.ANY)


def in_vmem(value):
    return pltpu.with_memory_space_constraint(value, pltpu.VMEM)


def in_hbm(value):
    return pltpu.with_memory_space_constraint(value, pltpu.HBM)


def per_step(shape, index):
    return pl.BlockSpec(shape, lambda s: (index(s),) + (0,) * (len(shape) - 1))


def same(step):
    return step


UNIT_IMAGES, MLP_IMAGES, INPUT_IMAGES, CONV_IMAGES = 2, 2, 2, 4
BRANCH_STEPS = 2
SMALL_MB, UNIT_MB, NORM_MB, MLP_MB, BRANCH_MB, INPUT_MB, CONV_MB = 8, 16, 16, 35, 16, 20, 16


def cot_specs(count):
    return [per_step((count, rows, 256), same) for rows in (272, 272, 256)]


def run_unit(valid, x, cot):
    images, count = x.shape[0], UNIT_IMAGES
    return pl.pallas_call(
        unit_kernel,
        grid=(images // count,),
        in_specs=[VMEM_SPEC, per_step((count, 1024, 128), same), per_step((count, 256, 320), same)],
        out_specs=[VMEM_SPEC] * 3 + cot_specs(count) + [VMEM_SPEC],
        out_shape=[
            pltpu.VMEM((images, 1024, 128), F32),
            pltpu.VMEM((images, 1024, 128), BF),
            sds((24, 128), F32),
            sds((images, 272, 256), BF),
            sds((images, 272, 256), BF),
            sds((images, 256, 256), BF),
            sds((8, 384), F32),
        ],
        scratch_shapes=[pltpu.VMEM((264, 384), F32)],
        compiler_params=params(UNIT_MB),
        cost_estimate=cost(4),
        name="unit",
    )(valid, in_hbm(x), in_hbm(cot))


def run_norm(placed, valid, unit, *parts):
    images = unit.shape[0]
    return pl.pallas_call(
        functools.partial(norm_kernel, placed),
        in_specs=[VMEM_SPEC] * 6,
        out_specs=[VMEM_SPEC] * 7,
        out_shape=[
            pltpu.VMEM((images, 1024, 128), BF),
            sds((24, 128), F32),
            sds((128, 128), BF),
            sds((128, 384), BF),
            sds((24, 128), F32),
            sds((16, 512), F32),
            pltpu.VMEM((SHARDS, ROWS, 128), BF),
        ],
        scratch_shapes=[pltpu.VMEM((24, 128), F32)],
        compiler_params=params(NORM_MB),
        cost_estimate=cost(5),
        name="norm",
    )(valid, in_vmem(unit), *parts)


def run_mlp(placed, x, normed, mix, cot, vec, packed, *conv):
    images, count = x.shape[0], MLP_IMAGES
    pixels = 1024 * count
    g1 = (4, 16 * G1_BLOCKS, 128)
    shapes = [
        ((384, 128), BF), ((128, 128), BF), ((128, 512), BF), ((512, 128), BF), ((512, 256), BF),
        ((32 * count, 32, 128), F32), ((count, 34, 48, 128), F32),
        ((pixels, 512), BF), ((pixels, 512), BF), ((pixels, 128), BF), ((pixels, 384), F32), ((pixels, 128), BF),
        ((pixels, 128), BF), ((pixels, 128), BF), ((count, 34, 48, 128), F32),
        ((1152, 256), F32), ((64, 1152), F32), ((128, 512), F32), ((128, 512), F32), ((128, 128), F32),
        ((8, 512), F32), ((8, 128), F32), ((8, 128), F32), ((8, 128), F32), ((8, 128), F32),
    ]
    return pl.pallas_call(
        functools.partial(mlp_kernel, placed),
        grid=(images // count,),
        in_specs=[
            per_step((count, 1024, 128), same),
        ]
        + [VMEM_SPEC] * 2
        + cot_specs(count)
        + [VMEM_SPEC] * 7,
        out_specs=[VMEM_SPEC, per_step((count, 1024, 128), same)] + [VMEM_SPEC] * 5,
        out_shape=[
            pltpu.VMEM((images, 256, 1152), BF),
            sds((images, 1024, 128), F32),
            pltpu.VMEM((images, 1024, 640), BF),
            sds((24, 128), F32),
            pltpu.VMEM((1152, 384), BF),
            sds(g1, F32),
            sds(g1, BF),
        ],
        scratch_shapes=[pltpu.VMEM(*shape) for shape in shapes],
        compiler_params=params(MLP_MB),
        cost_estimate=cost(35),
        name="mlp",
    )(in_hbm(x), in_vmem(normed), mix, *[in_hbm(part) for part in cot[0:3]], cot[3], vec, in_vmem(packed), *conv)


def run_branches(placed, valid, unit, mix, head, reduce, expand, units, gcat, dmix, vec, packed):
    g2 = (4, 16 * G2_BLOCKS, 128)
    shapes = [
        ((384, 128), F32), ((384, 128), F32), ((8, 128), F32), ((128, 512), F32),
    ]
    return pl.pallas_call(
        functools.partial(branch_kernel, placed),
        grid=(BRANCH_STEPS,),
        in_specs=[VMEM_SPEC] * 11,
        out_specs=[VMEM_SPEC] * 3,
        out_shape=[sds((24, 128), F32), sds(g2, F32), sds(g2, BF)],
        scratch_shapes=[pltpu.VMEM(*shape) for shape in shapes],
        compiler_params=params(BRANCH_MB),
        cost_estimate=cost(8),
        name="branches",
    )(valid, in_vmem(unit), mix, head, reduce, expand, units, in_vmem(gcat), dmix, vec, in_vmem(packed))


def run_input(base, held, valid, x, mix, spread, gcat, gfirst, vec, packed, after):
    images, count = x.shape[0], INPUT_IMAGES
    maps = per_step((count, 1024, 128), lambda s: s + base // count)
    more = [] if held is None else [held]
    return pl.pallas_call(
        functools.partial(input_kernel, base),
        grid=(images // count // 2,),
        in_specs=[
            VMEM_SPEC, VMEM_SPEC, VMEM_SPEC, VMEM_SPEC, VMEM_SPEC, VMEM_SPEC, VMEM_SPEC, VMEM_SPEC, ANY_SPEC,
        ]
        + [ANY_SPEC] * len(more),
        out_specs=[maps, whole((8, 128))],
        out_shape=[sds((images, 1024, 128), F32), sds((8, 128), F32)],
        scratch_shapes=[pltpu.VMEM((128, 896), F32)],
        compiler_params=params(INPUT_MB),
        input_output_aliases={9: 0} if more else {},
        cost_estimate=cost(4),
        name="input_grad",
    )(valid, in_vmem(x), mix, spread, in_vmem(gcat), in_vmem(gfirst), vec, in_vmem(packed), after, *more)


def run_conv(pm, vec, wconv, after):
    images, count = pm.shape[0], CONV_IMAGES
    return pl.pallas_call(
        conv_kernel,
        grid=(images // count,),
        in_specs=[VMEM_SPEC, VMEM_SPEC, VMEM_SPEC, ANY_SPEC],
        out_specs=[per_step((count, 256, 320), same), whole((8, 128))],
        out_shape=[sds((images, 256, 320), BF), sds((8, 128), F32)],
        compiler_params=params(CONV_MB),
        cost_estimate=cost(4),
        name="conv_out",
    )(in_vmem(pm), vec, in_vmem(wconv), after)


def pack_weights(weights):
    return pl.pallas_call(
        pack_kernel,
        out_shape=sds((ROWS + CONV_ROWS, 128), BF),
        in_specs=[VMEM_SPEC] * 21,
        out_specs=VMEM_SPEC,
        scratch_shapes=[pltpu.VMEM((16, 128), F32)],
        compiler_params=params(60),
        name="pack",
    )(*weights)


def join_kernel(one, two, three, after, small, conv):
    for at, part in enumerate((one, two, three)):
        small[at] = part[0:ROWS, :]
        conv[at] = part[ROWS : ROWS + CONV_ROWS, :]


def join(near, after):
    return pl.pallas_call(
        join_kernel,
        out_shape=[sds((3, ROWS, 128), BF), sds((3, CONV_ROWS, 128), BF)],
        in_specs=[VMEM_SPEC] * 3 + [ANY_SPEC],
        out_specs=[VMEM_SPEC] * 2,
        compiler_params=params(SMALL_MB),
        cost_estimate=cost(1),
        name="join",
    )(*near, after)


def refine(ref, values):
    ref[...] = values.astype(BF)
    at = 16 * G1_VEC
    both = split_low(values[at : at + 16] + values[at + 16 : at + 32])
    ref[at : at + 32, :] = jnp.concatenate(both, axis=0).astype(BF)
    at = 16 * (G1_BLOCKS + G2_VEC)
    both = split_low(values[at : at + 8] + values[at + 8 : at + 16])
    ref[at : at + 16, :] = jnp.concatenate(both, axis=0).astype(BF)
    at = 16 * (G1_BLOCKS + G2_REDUCE)
    both = split_low(values[at : at + 16, 0:32] + values[at : at + 16, 32:64])
    ref[at : at + 16, 0:64] = jnp.concatenate(both, axis=1).astype(BF)


def sum_pair_kernel(keep1, got1, keep2, got2, own, *others):
    for peer in range(4):
        one = keep1[peer] + got1[peer].astype(F32)
        two = keep2[peer] + got2[peer].astype(F32)
        values = jnp.concatenate([one, two], axis=0)
        if peer == 0:
            own[...] = values
        else:
            refine(others[peer - 1], values)


def sum_four_kernel(own, one, two, three, after, total, low):
    value = own[...] + one[...].astype(F32) + two[...].astype(F32) + three[...].astype(F32)
    total[...] = value
    refine(low, value)


def sum_two_kernel(own, one, after, total, low):
    value = own[...] + one[...].astype(F32)
    total[...] = value
    refine(low, value)


def sum_two(*values):
    shape = values[0].shape
    return pl.pallas_call(
        sum_two_kernel,
        out_shape=[sds(shape, F32), sds(shape, BF)],
        in_specs=[VMEM_SPEC] * 2 + [ANY_SPEC],
        out_specs=[VMEM_SPEC] * 2,
        compiler_params=params(SMALL_MB),
        cost_estimate=cost(1),
        name="sum_two",
    )(*values)


def sum_pair(keep1, got1, keep2, got2):
    rows = keep1.shape[1] + keep2.shape[1]
    return pl.pallas_call(
        sum_pair_kernel,
        out_shape=[sds((rows, 128), F32)] + [sds((rows, 128), BF)] * 3,
        in_specs=[VMEM_SPEC] * 4,
        out_specs=[VMEM_SPEC] * 4,
        compiler_params=params(SMALL_MB),
        cost_estimate=cost(2),
        name="sum_pair",
    )(keep1, got1, keep2, got2)


def sum_four(*values):
    shape = values[0].shape
    return pl.pallas_call(
        sum_four_kernel,
        out_shape=[sds(shape, F32), sds(shape, BF)],
        in_specs=[VMEM_SPEC] * 4 + [ANY_SPEC],
        out_specs=[VMEM_SPEC] * 2,
        compiler_params=params(SMALL_MB),
        cost_estimate=cost(2),
        name="sum_four",
    )(*values)


def finish_kernel(*refs):
    (own, far,
     gain_one, bias_one, w_h, b_h, w_w, b_w, w_c, w_red, b_red, w_exp, b_exp, w_proj, b_proj,
     gain_two, bias_two, w_up, b_up, w_down, b_down, w_conv, b_conv) = refs
    shard = lax.axis_index("fsdp")

    def first(at, rows=16):
        here = slice(16 * at, 16 * at + rows)
        return own[here, :] + far[here, :].astype(F32)

    def second(at, rows=16):
        return first(G1_BLOCKS + at, rows)

    w_h[...] = second(G2_HEIGHT)
    w_w[...] = second(G2_WIDTH)
    w_c[...] = second(G2_CHANNEL)
    reduce = second(G2_REDUCE)
    w_red[...] = reduce[:, 0:32] + reduce[:, 32:64]
    expand = second(G2_EXPAND)
    for b in range(3):
        w_exp[:, 128 * b : 128 * b + 128] = expand[4 * b : 4 * b + 4, :]
    w_proj[...] = first(G1_PROJ)
    for b in range(4):
        w_up[:, 128 * b : 128 * b + 128] = first(G1_UP + b)
    w_down[...] = first(G1_DOWN, 64)
    for at, tap in enumerate(TAPS):
        kernel = w_conv.at[tap // 3, tap % 3]
        for b in range(2):
            kernel[:, 128 * b : 128 * b + 128] = first(G1_CONV + 2 * at + b)
        edge = 64 * (at % 2)
        kernel[:, 256:320] = first(G1_EDGE + at // 2)[:, edge : edge + 64]
    table_one, table_two = first(G1_VEC) + first(G1_VEC_LOW), second(G2_VEC)
    table_two = table_two[0:8, :] + table_two[8:16, :]

    def share(table, row, blocks, length, stride):
        total = jnp.zeros((1, 128), F32)
        for b in range(blocks):
            pick = iota((128, 128), 0) + 128 * b == iota((128, 128), 1) + shard * stride
            total = total + dot_wide(table, pick.astype(BF))[row + b : row + b + 1, :]
        return total[:, 0:length].reshape(length)

    gain_one[...] = share(table_two, G2_GAIN1, 1, 16, 16)
    bias_one[...] = share(table_two, G2_BIAS1, 1, 16, 16)
    b_h[...] = share(table_two, G2_BH, 1, 16, 16)
    b_w[...] = share(table_two, G2_BW, 1, 16, 16)
    b_red[...] = share(table_two, G2_BR, 1, 4, 16)
    b_exp[...] = share(table_two, G2_BE, 3, 48, 48)
    b_proj[...] = share(table_one, G1_BPROJ, 1, 16, 16)
    gain_two[...] = share(table_one, G1_GAIN2, 1, 16, 16)
    bias_two[...] = share(table_one, G1_BIAS2, 1, 16, 16)
    b_up[...] = share(table_one, G1_BUP, 4, 64, 64)
    b_down[...] = share(table_one, G1_BDOWN, 1, 16, 16)
    b_conv[...] = share(table_one, G1_BCONV, 3, 40, 40)


def finish(sums, weights):
    return pl.pallas_call(
        finish_kernel,
        out_shape=[sds(w.shape, F32) for w in weights],
        in_specs=[VMEM_SPEC] * 2,
        out_specs=[VMEM_SPEC] * 21,
        compiler_params=params(SMALL_MB),
        name="finish",
    )(*sums)


def early(placed, input_map, valid_size, cotangent, gathered):
    images = input_map.shape[0]
    x = input_map.reshape(images, 1024, 128)
    valid_size = valid_size.T
    cot = cotangent.reshape(images, 256, 320)
    unit, unit_low, units, main, right, rest, bias = run_unit(valid_size, x, cot)
    small, conv = gathered(units)
    normed, head, reduce, expand, mix, vec, packed = run_norm(placed, valid_size, unit, *small)
    pm, gfirst, gcat, dmix, wconv, keep1, send1 = run_mlp(
        placed, x, normed, mix, (main, right, rest, bias), vec, packed, *conv
    )
    spread, keep2, send2 = run_branches(
        placed, valid_size, unit_low, mix, head, reduce, expand, units, gcat, dmix, vec, packed
    )

    def late_map(after):
        out, token = run_conv(pm, vec, wconv, after)
        return out.reshape(images, 16, 16, 320), token

    def late_grad(after, held=None):
        base = 0 if held is None else images // 2
        return run_input(base, held, valid_size, x, mix, spread, gcat, gfirst, vec, packed, after)

    return (keep1, send1, keep2, send2), late_map, late_grad


def spread_out(packed):
    own = (packed[0], packed[1])
    return [
        own + (packed[2::2, rows], packed[3::2, rows]) for rows in (slice(0, ROWS), slice(ROWS, None))
    ]


def compute(placed, input_map, valid_size, cotangent, packed):
    sums, late_map, late_grad = early(
        placed,
        input_map,
        valid_size,
        cotangent,
        lambda after: spread_out(packed),
    )
    input_grad = late_grad(sums[0], late_grad(sums[0])[0])[0]
    return late_map(sums[0])[0], input_grad.reshape(input_map.shape), sums


def pack_whole(weights):
    (gain_one, bias_one, w_h, b_h, w_w, b_w, w_c, w_red, b_red, w_exp, b_exp, w_proj, b_proj,
     gain_two, bias_two, w_up, b_up, w_down, b_down, w_conv, b_conv) = weights

    def split(weight):
        weight = weight.reshape(SHARDS, weight.shape[0] // SHARDS, weight.shape[1])
        rows, cols = -weight.shape[1] % 16, -weight.shape[2] % 128
        weight = jnp.pad(weight, ((0, 0), (0, rows), (0, cols)))
        return [weight[:, :, at : at + 128] for at in range(0, weight.shape[2], 128)]

    pieces = split(w_h) + split(w_w) + split(w_c) + split(w_proj) + split(w_red) + split(w_exp)
    pieces = pieces + split(w_up) + split(w_down)
    taps = [split(w_conv[tap // 3, tap % 3]) for tap in TAPS]
    edges = [tap[2][:, :, 0:64] for tap in taps]
    edges.append(jnp.zeros_like(edges[0]))
    conv = [part for tap in taps for part in tap[0:2]]
    conv = conv + [jnp.concatenate(edges[at : at + 2], axis=2) for at in range(0, 10, 2)]
    vectors = (gain_one, bias_one, b_h, b_w, b_red, b_exp, b_proj, gain_two, bias_two, b_up, b_down, b_conv)
    rows = [
        jnp.pad(v.reshape(SHARDS, 1, v.shape[0] // SHARDS), ((0, 0), (0, 0), (0, 128 - v.shape[0] // SHARDS)))
        for v in vectors
    ]
    rows = rows + [jnp.zeros((SHARDS, 4, 128), BF)]
    return jnp.concatenate(pieces + [jnp.concatenate(rows, axis=1)] + conv, axis=1)


def unpack_whole(sums):
    one = jnp.stack([sums[0], sums[1].astype(F32)], axis=1).reshape(SHARDS, -1, 128)
    two = jnp.stack([sums[2], sums[3].astype(F32)], axis=1).reshape(SHARDS, -1, 128)

    def join(buffer, at, blocks, rows=16):
        parts = [buffer[:, 16 * (at + b) : 16 * (at + b) + rows, :] for b in range(blocks)]
        return jnp.concatenate(parts, axis=2).reshape(SHARDS * rows, 128 * blocks)

    def vector(buffer, at, row, blocks=1):
        start, rest = 16 * at + row, 16 if at == G1_VEC else 8
        both = buffer[0, start : start + blocks, :] + buffer[0, start + rest : start + rest + blocks, :]
        return both.reshape(128 * blocks)

    expand = two[:, 16 * G2_EXPAND : 16 * G2_EXPAND + 12, :].reshape(SHARDS, 3, 4, 128)
    taps = []
    for tap in range(9):
        at = TAPS.index(tap)
        edge = join(one, G1_EDGE + at // 2, 1)[:, 64 * (at % 2) : 64 * (at % 2) + 64]
        taps.append(jnp.concatenate([join(one, G1_CONV + 2 * at, 2), edge], axis=1))
    return (
        vector(two, G2_VEC, G2_GAIN1),
        vector(two, G2_VEC, G2_BIAS1),
        join(two, G2_HEIGHT, 1),
        vector(two, G2_VEC, G2_BH),
        join(two, G2_WIDTH, 1),
        vector(two, G2_VEC, G2_BW),
        join(two, G2_CHANNEL, 1),
        join(two, G2_REDUCE, 1)[:, 0:32] + join(two, G2_REDUCE, 1)[:, 32:64],
        vector(two, G2_VEC, G2_BR).reshape(SHARDS, 16)[:, 0:4].reshape(32),
        expand.transpose(0, 2, 1, 3).reshape(32, 384),
        vector(two, G2_VEC, G2_BE, 3),
        join(one, G1_PROJ, 1),
        vector(one, G1_VEC, G1_BPROJ),
        vector(one, G1_VEC, G1_GAIN2),
        vector(one, G1_VEC, G1_BIAS2),
        join(one, G1_UP, 4),
        vector(one, G1_VEC, G1_BUP, 4),
        one[:, 16 * G1_DOWN : 16 * G1_DOWN + 64, :].reshape(512, 128),
        vector(one, G1_VEC, G1_BDOWN),
        jnp.stack(taps).reshape(3, 3, 128, 320),
        vector(one, G1_VEC, G1_BCONV, 3)[0:320],
    )


def shards_of(mesh):
    shards, copies = mesh.shape["fsdp"], mesh.shape["rep"]

    def eight(input_map, valid_size, *rest):
        weights, cotangent = rest[:-1], rest[-1]
        sibling = [(i, i ^ 1) for i in range(shards)]
        packs = pack_weights(weights)
        swapped = lax.ppermute(packs, "fsdp", sibling)
        near = [
            lax.ppermute(packs, "fsdp", [(i, i ^ (2 * peer)) for i in range(shards)])
            for peer in range(1, 4)
        ]

        def gathered(after):
            small, conv = join(near, after)
            own = (packs, swapped)
            return own + (small, lax.ppermute(small, "fsdp", sibling)), (
                own + (conv, lax.ppermute(conv, "fsdp", sibling))
            )

        (keep1, send1, keep2, send2), late_map, late_grad = early(
            True, input_map, valid_size, cotangent, gathered
        )
        got1, got2 = lax.ppermute(send1, "fsdp", sibling), lax.ppermute(send2, "fsdp", sibling)
        own, *others = sum_pair(keep1, got1, keep2, got2)
        moved = [
            lax.ppermute(value, "fsdp", [(i, i ^ (2 * (peer + 1))) for i in range(shards)])
            for peer, value in enumerate(others)
        ]
        out, token = late_map(own)
        total, low = sum_four(own, *moved, token)
        both = [(copy, shard) for copy in range(copies) for shard in range(shards)]
        steps = [
            [(z * shards + f, (z ^ (1 + (f + at) % 2)) * shards + f) for z, f in both] for at in range(2)
        ]
        far = lax.ppermute(low, ("rep", "fsdp"), steps[0])
        held, token = late_grad(total)
        total, low = sum_two(total, far, token)
        far = lax.ppermute(low, ("rep", "fsdp"), steps[1])
        input_grad = late_grad(total, held)[0].reshape(input_map.shape)
        return (out, input_grad) + tuple(finish((total, far), weights))

    def general(input_map, valid_size, *rest):
        weights, cotangent = rest[:-1], rest[-1]
        dims = [2 if w.ndim == 4 else 0 for w in weights]
        full = [lax.all_gather(w, "fsdp", axis=d, tiled=True) for w, d in zip(weights, dims)]
        packed = pack_whole(full)
        out, input_grad, sums = compute(False, input_map, valid_size, cotangent, packed)
        grads = [
            lax.psum_scatter(g, "fsdp", scatter_dimension=d, tiled=True)
            for g, d in zip(unpack_whole(sums), dims)
        ]
        return (out, input_grad) + tuple(lax.psum(grads, "rep"))

    return eight if shards == SHARDS and copies == 4 else general


def solution(mesh):
    maps = P(("rep", "fsdp"), None, None, None)
    vector, matrix = P("fsdp"), P("fsdp", None)
    weights = (
        vector, vector, matrix, vector, matrix, vector, matrix, matrix, vector, matrix, vector,
        matrix, vector, vector, vector, matrix, vector, matrix, vector,
        P(None, None, "fsdp", None), vector,
    )
    return jax.shard_map(
        shards_of(mesh),
        mesh=mesh,
        in_specs=(maps, P(("rep", "fsdp"), None)) + weights + (maps,),
        out_specs=(maps, maps) + weights,
        check_vma=False,
    )
```

```python
import functools

import jax
import jax.numpy as jnp
from jax import lax
from jax.experimental import pallas as pl
from jax.experimental.pallas import tpu as pltpu
from jax.sharding import PartitionSpec as P

BF = jnp.bfloat16
F32 = jnp.float32
HIGH = lax.Precision.HIGHEST
EPS = 1e-05

SHARDS = 8
B_HEIGHT, B_WIDTH, B_CHANNEL, B_PROJ, B_REDUCE = 0, 1, 2, 3, 4
B_EXPAND, B_UP, B_DOWN, B_VEC, BLOCKS = 5, 8, 12, 16, 17
C_PAIRS, C_EDGES, C_BLOCKS = 0, 18, 23
ROWS, CONV_ROWS = 16 * BLOCKS, 16 * C_BLOCKS
TAPS = (4, 5, 7, 8, 3, 6, 1, 2, 0)
(V_GAIN1, V_BIAS1, V_BH, V_BW, V_BR, V_BE, V_BP, V_GAIN2, V_BIAS2, V_BUP, V_BDOWN, V_BCONV) = range(12)
LENGTHS = (16, 16, 16, 16, 4, 48, 16, 16, 16, 64, 16, 40)
G1_CONV, G1_EDGE, G1_UP, G1_DOWN, G1_PROJ, G1_VEC, G1_VEC_LOW, G1_BLOCKS = 0, 18, 23, 27, 31, 32, 33, 34
G1_BCONV, G1_BUP, G1_BDOWN, G1_BPROJ, G1_GAIN2, G1_BIAS2 = 0, 3, 7, 8, 9, 10
G2_HEIGHT, G2_WIDTH, G2_CHANNEL, G2_REDUCE, G2_EXPAND, G2_VEC, G2_BLOCKS = 0, 1, 2, 3, 4, 5, 6
G2_GAIN1, G2_BIAS1, G2_BH, G2_BW, G2_BR, G2_BE = 0, 1, 2, 3, 4, 5


def iota(shape, axis):
    return lax.broadcasted_iota(jnp.int32, shape, axis)


def dot(left, right):
    return jnp.dot(left, right, preferred_element_type=F32)


def dot_nt(left, right):
    return lax.dot_general(left, right, (((1,), (1,)), ((), ())), preferred_element_type=F32)


def dot_tn(left, right):
    return lax.dot_general(left, right, (((0,), (0,)), ((), ())), preferred_element_type=F32)


def parts_of(values, count):
    parts = []
    for _ in range(count):
        parts.append(values.astype(BF))
        values = values - parts[-1].astype(F32)
    return parts


def dot_wide(left, right, product=dot):
    rows = left.shape[0]
    joined = product(jnp.concatenate(parts_of(left, 3), axis=0), right)
    return joined[0:rows] + (joined[rows : 2 * rows] + joined[2 * rows : 3 * rows])


def outer_wide(left, right):
    (left_high, left_low), (right_high, right_low) = parts_of(left, 2), parts_of(right, 2)
    return dot_tn(
        jnp.concatenate([left_high, left_high, left_low, left_low], axis=0),
        jnp.concatenate([right_high, right_low, right_high, right_low], axis=0),
    )


def fold8(values):
    rows, cols = values.shape
    return jnp.sum(values.reshape(rows // 8, 8, cols), axis=0)


def lane_mean(values):
    return jnp.mean(values, axis=-1, keepdims=True)


def gelu_both(values):
    cdf = 0.5 + 0.5 * lax.erf(values * 0.7071067811865476)
    slope = cdf + values * (jnp.exp(-0.5 * (values * values)) * 0.3989422804014327)
    return values * cdf, slope


def gelu_twice(values):
    cdf = 1.0 + lax.erf(values * 0.7071067811865476)
    density = (values * 0.7978845608028654) * jnp.exp2((values * values) * -0.7213475204444817)
    return values * cdf, cdf + density


def split_low(values):
    high = values.astype(BF).astype(F32)
    return high, (values - high).astype(BF).astype(F32)


def block(packed, at):
    return packed[:, 16 * at : 16 * at + 16, :].reshape(128, 128)


def branch_weights(packed):
    return [block(packed, at) for at in (B_HEIGHT, B_WIDTH, B_CHANNEL)]


def spread_matrix():
    unit, lane = iota((128, 128), 0), iota((128, 128), 1)
    return ((lane == 16 * (unit // 4) + unit % 4) & (unit < 32)).astype(BF)


def pick_matrix(k):
    return (iota((384, 128), 0) == 3 * iota((384, 128), 1) + k).astype(BF)


def head_weights(packed, vec):
    w_reduce = dot(block(packed, B_REDUCE), spread_matrix()).astype(BF)
    expand = jnp.concatenate([block(packed, B_EXPAND + b) for b in range(3)], axis=1)
    picks = jnp.concatenate([pick_matrix(k) for k in range(3)], axis=1)
    w_expand = dot(expand, picks).astype(BF)
    b_expand = dot(vec[:, 0:384].astype(BF), picks)[V_BE : V_BE + 1, :]
    return w_reduce, w_expand, b_expand


def head_forward(sums, counts, branches, head, vec):
    w_reduce, w_expand, b_expand = head
    pooled = dot_wide(jnp.concatenate(sums, axis=1), branches) / counts
    pooled = pooled + (vec[V_BH : V_BH + 1, 0:128] + vec[V_BW : V_BW + 1, 0:128])
    pre = dot_wide(pooled, w_reduce) + vec[V_BR : V_BR + 1, 0:128]
    hidden, slope = gelu_both(pre)
    joined = dot_wide(hidden, w_expand) + b_expand
    logits = [joined[:, 128 * k : 128 * k + 128] for k in range(3)]
    top = jnp.maximum(jnp.maximum(logits[0], logits[1]), logits[2])
    powers = [jnp.exp(v - top) for v in logits]
    total = powers[0] + powers[1] + powers[2]
    return pooled, hidden, slope, [v / total for v in powers]


def column(row_values):
    stacked = jnp.where(iota((8, 128), 0) == 0, row_values, 0.0)
    return dot_tn(stacked.astype(BF), jnp.ones((8, 128), BF))


def size_columns(valid_ref):
    sizes = valid_ref[...].astype(F32).astype(BF)
    kind = iota((2, 128), 0)
    return [dot_tn(sizes, (kind == axis).astype(BF)) for axis in range(2)]


def inside_counts(valid_ref):
    high, wide = size_columns(valid_ref)
    offsets = jnp.broadcast_to(channel_offsets()[0, 0:1, :], (8, 128))

    def kept(size):
        past = jnp.where(offsets == 1, jnp.where(size == 32.0, 1.0, 0.0), 0.0)
        return size - past - jnp.where(offsets == -1, 1.0, 0.0)

    return [kept(high) * wide, kept(wide) * high, high * wide]


def count_column(valid_ref):
    high, wide = size_columns(valid_ref)
    return high * wide


def channel_offsets():
    return jnp.broadcast_to(((iota((1, 128), 1) + 1) % 3 - 1).reshape(1, 1, 128), (1, 32, 128))


def shifted_masks(valid_ref, image):
    sizes = jnp.where(iota((2, 8), 1) == image, valid_ref[...].astype(F32), 0.0)
    size = jnp.sum(sizes, axis=1, keepdims=True)
    masks = []
    for axis, shape in ((0, (32, 1, 128)), (1, (1, 32, 128))):
        limit = size[axis : axis + 1, :].reshape(1, 1, 1)
        at = iota(shape, axis)
        taker = at - channel_offsets()[:, 0:1, :]
        masks.append((at.astype(F32) < limit).astype(F32))
        masks.append(((taker >= 0) & (taker.astype(F32) < limit)).astype(F32))
    return masks


def class_sums(maps, masks):
    row, row_taker, col, col_taker = masks

    def by_row(mask):
        return jnp.sum((maps * mask).reshape(32, 4, 8, 128), axis=1)

    plain, taken = by_row(col), by_row(col_taker)
    return [
        jnp.sum(jnp.sum(rows * mask, axis=0), axis=0, keepdims=True)
        for rows, mask in ((plain, row_taker), (taken, row), (plain, row))
    ]


def pixel_masks(valid_ref, image):
    sizes = jnp.where(iota((2, 8), 1) == image, valid_ref[...].astype(F32), 0.0)
    size = jnp.sum(sizes, axis=1, keepdims=True)
    pixel, kind = iota((8, 1024), 1), iota((8, 1024), 0)

    def taker(at, one):
        back, forth = (kind == one).astype(jnp.int32), (kind == one + 1).astype(jnp.int32)
        return (at - back + forth).astype(F32)

    row, column = taker(pixel // 32, 1), taker(pixel % 32, 3)
    inside = (row >= 0.0) & (row < size[0:1]) & (column >= 0.0) & (column < size[1:2])
    return inside.astype(F32).astype(BF)


def place_of(placed):
    if not placed:
        return 0, 0
    shard = lax.axis_index("fsdp")
    return shard // 2, lax.rem(shard, 2)


def pack_kernel(*refs):
    (gain_one, bias_one, w_h, b_h, w_w, b_w, w_c, w_red, b_red, w_exp, b_exp, w_proj, b_proj,
     gain_two, bias_two, w_up, b_up, w_down, b_down, w_conv, b_conv, out, vec) = refs
    conv = out.at[ROWS : ROWS + CONV_ROWS]

    def put(at, values):
        out[16 * at : 16 * at + values.shape[0], 0 : values.shape[1]] = values

    put(B_HEIGHT, w_h[...])
    put(B_WIDTH, w_w[...])
    put(B_CHANNEL, w_c[...])
    put(B_PROJ, w_proj[...])
    blank = jnp.zeros((16, 128), BF)
    put(B_REDUCE, blank)
    put(B_REDUCE, w_red[...])
    for b in range(3):
        vec[...] = jnp.zeros((16, 128), F32)
        vec[0:4, :] = w_exp[:, 128 * b : 128 * b + 128].astype(F32)
        put(B_EXPAND + b, vec[...].astype(BF))
    for b in range(4):
        put(B_UP + b, w_up[:, 128 * b : 128 * b + 128])
    put(B_DOWN, w_down[...])
    conv[16 * (C_BLOCKS - 1) : 16 * C_BLOCKS, :] = blank
    for at, tap in enumerate(TAPS):
        kernel = w_conv.at[tap // 3, tap % 3]
        for b in range(2):
            start = 16 * (C_PAIRS + 2 * at + b)
            conv[start : start + 16, :] = kernel[:, 128 * b : 128 * b + 128]
        start, lane = 16 * (C_EDGES + at // 2), 64 * (at % 2)
        conv[start : start + 16, lane : lane + 64] = kernel[:, 256:320]
    vec[...] = jnp.zeros((16, 128), F32)
    vectors = (gain_one, bias_one, b_h, b_w, b_red, b_exp, b_proj, gain_two, bias_two, b_up, b_down, b_conv)
    for row, (values, length) in enumerate(zip(vectors, LENGTHS)):
        vec[row : row + 1, 0:length] = values[...].astype(F32).reshape(1, length)
    put(B_VEC, vec[...].astype(BF))


def vector_table(packed):
    shards = packed[:, 16 * B_VEC : 16 * B_VEC + 16, :].reshape(128, 128)
    table = jnp.zeros((16, 512), F32)
    rows = iota((16, 512), 0)
    for length in (16, 4, 48, 64, 40):
        step = 16 if length == 4 else length
        lane = iota((1, 512), 1)
        source = iota((128, 512), 0)
        pick = (source == jnp.where(lane % step < length, lane % step, -1)).astype(BF)
        spread = dot(shards, pick)
        mine = (source // 16) == (lane // step)
        whole = jnp.sum(jnp.where(mine, spread, 0.0).reshape(8, 16, 512), axis=0)
        held = functools.reduce(
            jnp.logical_or, [rows == v for v, size in enumerate(LENGTHS) if size == length]
        )
        table = jnp.where(held, whole, table)
    return table


def unit_kernel(
    valid, x_ref, cot_ref, unit_ref, low_ref, sums_ref, main_ref, right_ref, rest_ref, bias_ref, shift
):
    step, count = pl.program_id(0), x_ref.shape[0]

    @pl.when(step == 0)
    def _():
        shift[...] = jnp.zeros(shift.shape, F32)
        bias_ref[...] = jnp.zeros(bias_ref.shape, F32)

    lanes = iota((256, 128), 1) < 64
    blank, line = jnp.zeros((16, 256), BF), jnp.zeros((16, 128), F32)
    for m in range(count):
        cot = cot_ref[m].astype(F32)
        bias_ref[:, 0:320] += fold8(cot)
        shift[0:256, 0:320] = cot
        ahead = shift[1:257, :]
        ahead = jnp.where(iota((256, 384), 0) % 16 == 15, 0.0, ahead)
        main_ref[m, 0:256, :] = cot_ref[m, :, 0:256]
        main_ref[m, 256:272, :] = blank
        right_ref[m, 0:256, :] = ahead[:, 0:256].astype(BF)
        right_ref[m, 256:272, :] = blank
        both = jnp.where(lanes, shift[0:256, 256:384], pltpu.roll(ahead[:, 256:384], 64, 1))
        rest_ref[m, :, 0:128] = both.astype(BF)
        below = jnp.concatenate([both[16:256], line], axis=0)
        rest_ref[m, :, 128:256] = below.astype(BF)

    low = x_ref[...].reshape(count * 1024, 128)
    centre = low.astype(F32) - dot(low, jnp.full((128, 128), 1.0 / 128.0, BF))
    scale = lax.rsqrt(lane_mean(centre * centre) + EPS)
    unit = centre * scale
    here = pl.ds(step * count, count)
    unit_ref[here] = unit.reshape(count, 1024, 128)
    low_ref[here] = unit.astype(BF).reshape(count, 1024, 128)
    for m in range(count):
        image = step * count + m
        maps = unit[1024 * m : 1024 * m + 1024].reshape(32, 32, 128)
        for k, total in enumerate(class_sums(maps, shifted_masks(valid, image))):
            sums_ref[pl.ds(8 * k + image, 1), :] = total


def norm_kernel(
    placed, valid, unit_ref, own, swapped, mine, other,
    norm_ref, head_ref, reduce_ref, expand_ref, mix_ref, vec_ref, pk_ref, sums_ref
):
    chip, core = place_of(placed)
    pk_ref[2 * chip + core] = own[0:ROWS, :]
    pk_ref[2 * chip + (1 - core)] = swapped[0:ROWS, :]
    for peer in range(1, 4):
        shard = 2 * lax.bitwise_xor(chip, peer)
        pk_ref[shard + core] = mine[peer - 1]
        pk_ref[shard + (1 - core)] = other[peer - 1]
    vec = vector_table(pk_ref)
    vec_ref[...] = vec
    head = head_weights(pk_ref, vec)
    gain = vec[V_GAIN1 : V_GAIN1 + 1, 0:128]
    bias = vec[V_BIAS1 : V_BIAS1 + 1, 0:128]
    offsets = channel_offsets()[0, 0:1, :]
    for image in range(unit_ref.shape[0]):
        low = (unit_ref[image] * gain + bias).astype(BF)
        norm_ref[image] = low
        totals = dot(pixel_masks(valid, image), low)
        for k in range(2):
            forth, back = totals[2 * k + 1 : 2 * k + 2], totals[2 * k + 2 : 2 * k + 3]
            total = jnp.where(offsets == 1, forth, jnp.where(offsets == -1, back, totals[0:1]))
            sums_ref[8 * k + image : 8 * k + image + 1, :] = total
        sums_ref[16 + image : 17 + image, :] = totals[0:1]
    sums = [sums_ref[8 * k : 8 * k + 8, :] for k in range(3)]
    branches = jnp.concatenate(branch_weights(pk_ref), axis=0)
    pooled, hidden, slope, mixing = head_forward(sums, count_column(valid), branches, head, vec)
    for at, values in enumerate((pooled, hidden, slope)):
        head_ref[8 * at : 8 * at + 8, :] = values
    reduce_ref[...], expand_ref[...] = head[0], head[1]
    for k in range(3):
        mix_ref[8 * k : 8 * k + 8, :] = mixing[k]


def mlp_kernel(
    placed, x_ref, norm_ref, mix_ref, main_ref, right_ref, rest_ref, bias_ref, vec_ref, pk_ref,
    own, swapped, conv_mine, conv_other,
    pm_ref, gfirst_ref, gcat_ref, dmix_ref, wconv, keep_ref, send_ref,
    wcat, wproj, wup, wdown, wrest,
    gsec, low, act, ghid, norm2, mixes, mixed_s, gtail, gbranch, npad,
    a_conv, a_rest, a_up, a_down, a_proj, a_bup, a_bdown, a_bproj, a_gain2, a_bias2,
):
    step, steps = pl.program_id(0), pl.num_programs(0)
    count = x_ref.shape[0] // steps

    @pl.when(step == 0)
    def _():
        for k, weight in enumerate(branch_weights(pk_ref)):
            wcat[128 * k : 128 * k + 128, :] = weight
        wproj[...] = block(pk_ref, B_PROJ)
        for b in range(4):
            wup[:, 128 * b : 128 * b + 128] = block(pk_ref, B_UP + b)
        wdown[...] = pk_ref[:, 16 * B_DOWN : 16 * B_DOWN + 64, :].reshape(512, 128) * jnp.bfloat16(0.5)
        chip, core = place_of(placed)
        blank = jnp.zeros((16, 64), BF)
        for peer in range(4):
            conv = slice(ROWS, ROWS + CONV_ROWS)
            pair = (own.at[conv], swapped.at[conv])
            if peer > 0:
                pair = (conv_mine.at[peer - 1], conv_other.at[peer - 1])
            for part, odd in zip(pair, (core, 1 - core)):
                shard = 2 * lax.bitwise_xor(chip, peer) + odd
                for at in range(9):
                    rows = pl.ds(pl.multiple_of(128 * at + 16 * shard, 16), 16)
                    for b in range(2):
                        start = 16 * (C_PAIRS + 2 * at + b)
                        wconv[rows, 128 * b : 128 * b + 128] = part[start : start + 16, :]
                    start, lane = 16 * (C_EDGES + at // 2), 64 * (at % 2)
                    edge = part[start : start + 16, :][:, lane : lane + 64]
                    wconv[rows, 256:384] = jnp.concatenate([edge, blank], axis=1)
        none = jnp.zeros((128, 64), BF)
        for output, places in enumerate(((0, None, None, None), (1, 4, None, None), (2, None, 6, None), (3, 5, 7, 8))):
            ends = [none if at is None else wconv[128 * at : 128 * at + 128, 256:320] for at in places]
            rows = slice(128 * output, 128 * output + 128)
            wrest[rows, 0:128] = jnp.concatenate(ends[0:2], axis=1)
            wrest[rows, 128:256] = jnp.concatenate(ends[2:4], axis=1)
        for ref in (low, npad):
            ref[:, 0:1] = jnp.zeros((count, 1, 48, 128), F32)
            ref[:, 33:34] = jnp.zeros((count, 1, 48, 128), F32)
        for ref in (low, npad):
            shape = ref.shape[0:2] + (8, 128)
            ref[:, :, 0:8, :] = jnp.zeros(shape, F32)
            ref[:, :, 40:48, :] = jnp.zeros(shape, F32)
        for ref in (a_conv, a_rest, a_up, a_down, a_proj, a_bup, a_bdown, a_bproj, a_gain2, a_bias2):
            ref[...] = jnp.zeros(ref.shape, ref.dtype)

    def row(at, width=128):
        return vec_ref[at : at + 1, 0:width]

    images = range(count)
    maps = [step * count + m for m in images]
    pixels = [slice(1024 * m, 1024 * m + 1024) for m in images]

    offsets = channel_offsets()
    forth, back = offsets == 1, offsets == -1
    for m in images:
        mixing = [mix_ref[pl.ds(8 * k + maps[m], 1), :] for k in range(3)]
        biases = (row(V_BH), row(V_BW), 0.0)
        normed = norm_ref[maps[m]]
        here = normed.astype(F32).reshape(32, 32, 128)
        npad[m, 1:33, 8:40, :] = here
        high = jnp.where(
            forth, npad[m, 2:34, 8:40, :], jnp.where(back, npad[m, 0:32, 8:40, :], here)
        )
        wide = jnp.where(
            forth, npad[m, 1:33, 9:41, :], jnp.where(back, npad[m, 1:33, 7:39, :], here)
        )
        shifted = (high.reshape(1024, 128).astype(BF), wide.reshape(1024, 128).astype(BF), normed)
        mixed = 0.0
        for k in range(3):
            branch = dot(shifted[k], wcat[128 * k : 128 * k + 128, :]) + biases[k]
            mixes[pixels[m], 128 * k : 128 * k + 128] = branch
            mixed = mixed + branch * mixing[k]
        mixed_s[pixels[m], :] = mixed.astype(BF)
    first, unit, scale = [None] * count, [None] * count, [None] * count
    for m in images:
        added = dot(mixed_s[pixels[m], :], wproj[...]) + row(V_BP)
        first[m] = x_ref[maps[m]].astype(F32) + added
        centre = first[m] - lane_mean(first[m])
        scale[m] = lax.rsqrt(lane_mean(centre * centre) + EPS)
        unit[m] = centre * scale[m]
        norm2[pixels[m], :] = (unit[m] * row(V_GAIN2) + row(V_BIAS2)).astype(BF)

    flat = (count * 256, 256)
    cot_here, cot_right = main_ref[:, 0:256, :].reshape(flat), right_ref[:, 0:256, :].reshape(flat)
    cot_below, cot_both = main_ref[:, 16:272, :].reshape(flat), right_ref[:, 16:272, :].reshape(flat)
    cot_rest = rest_ref[...].reshape(flat)
    ends = dot_nt(cot_rest, wrest[...])
    from_here = dot_nt(cot_here, wconv[0:512, 0:256])
    from_right = dot_nt(cot_right, wconv[512:768, 0:256])
    from_below = dot_nt(cot_below, wconv[768:1024, 0:256])
    from_both = dot_nt(cot_both, wconv[1024:1152, 0:256])
    straight = from_here + ends
    planes = (
        (straight[:, 0:128], straight[:, 128:256] + from_right[:, 0:128]),
        (
            straight[:, 256:384] + from_below[:, 0:128],
            (straight[:, 384:512] + from_right[:, 128:256]) + (from_below[:, 128:256] + from_both),
        ),
    )
    for p in range(2):
        for s in range(2):
            plane = planes[p][s]
            for i in range(16 * count):
                gsec[2 * i + p, pl.ds(s, 16, stride=2), :] = plane[16 * i : 16 * i + 16, :]

    grad_second = [gsec[32 * m : 32 * m + 32].reshape(1024, 128) for m in images]
    for m in images:
        tail = grad_second[m].astype(BF)
        gtail[pixels[m], :] = tail
        a_bdown[...] += fold8(grad_second[m])
        for b in range(2):
            cols = slice(256 * b, 256 * b + 256)
            hidden = dot(norm2[pixels[m], :], wup[:, cols]) + vec_ref[V_BUP : V_BUP + 1, cols]
            grad_act = dot_nt(tail, wdown[cols, :])
            value, slope = gelu_twice(hidden)
            act[pixels[m], cols] = value.astype(BF)
            grad_hidden = grad_act * slope
            ghid[pixels[m], cols] = grad_hidden.astype(BF)
            a_bup[:, cols] += fold8(grad_hidden)
    grad_first = [None] * count
    for m in images:
        second = first[m] + (dot(act[pixels[m], :], wdown[...]) + row(V_BDOWN))
        low[m, 1:33, 8:40, :] = second.reshape(32, 32, 128)
        grad_normed = dot_nt(ghid[pixels[m], :], wup[...])
        a_gain2[...] += fold8(grad_normed * unit[m])
        a_bias2[...] += fold8(grad_normed)
        scaled_grad = grad_normed * row(V_GAIN2)
        grad_first[m] = grad_second[m] + scale[m] * (
            scaled_grad - lane_mean(scaled_grad) - unit[m] * lane_mean(scaled_grad * unit[m])
        )
        gfirst_ref[m] = grad_first[m]
        gbranch[pixels[m], :] = grad_first[m].astype(BF)
        a_bproj[...] += fold8(grad_first[m])
    a_up[...] += dot_tn(norm2[...], ghid[...])
    a_down[...] += dot_tn(gtail[...], act[...])
    for m in images:
        grad_mixed = dot_nt(gbranch[pixels[m], :], wproj[...])
        for k in range(3):
            share = fold8(grad_mixed * mixes[pixels[m], 128 * k : 128 * k + 128])
            dmix_ref[pl.ds(8 * k + maps[m], 1), :] = jnp.sum(share, axis=0, keepdims=True)
        npad[m, 1:33, 8:40, :] = grad_mixed.reshape(32, 32, 128)
        low_grad, image = grad_mixed.astype(BF), maps[m]
        gcat_ref[image, :, 0:128] = low_grad
        gcat_ref[image, 0:32, 128:256] = jnp.zeros((32, 128), BF)
        gcat_ref[image, 32:1024, 128:256] = low_grad[0:992]
        gcat_ref[image, 0:992, 256:384] = low_grad[32:1024]
        gcat_ref[image, 992:1024, 256:384] = jnp.zeros((32, 128), BF)
        gcat_ref[image, :, 384:512] = npad[m, 1:33, 7:39, :].reshape(1024, 128).astype(BF)
        gcat_ref[image, :, 512:640] = npad[m, 1:33, 9:41, :].reshape(1024, 128).astype(BF)

    for at, tap in enumerate(TAPS):
        r, s = tap // 3, tap % 3
        for m in images:
            patch = low[m, pl.ds(r, 16, stride=2), pl.ds(7 + s, 16, stride=2), :]
            pm_ref[m, :, 128 * at : 128 * at + 128] = patch.reshape(256, 128).astype(BF)

    a_proj[...] += dot_tn(mixed_s[...], gbranch[...])
    patches = pm_ref[...].reshape(256 * count, 1152)
    a_conv[...] += dot_tn(patches, cot_here)
    a_rest[...] += dot_tn(patches[:, 0:512], cot_rest)

    @pl.when(step == steps - 1)
    def _():
        chip, core = place_of(placed)[0:2]
        vectors = jnp.concatenate(
            [jnp.sum(bias_ref[:, 128 * b : 128 * b + 128], axis=0, keepdims=True) for b in range(3)]
            + [jnp.sum(a_bup[:, 128 * b : 128 * b + 128], axis=0, keepdims=True) for b in range(4)]
            + [jnp.sum(ref[...], axis=0, keepdims=True) for ref in (a_bdown, a_bproj, a_gain2, a_bias2)]
            + [jnp.zeros((5, 128), F32)],
            axis=0,
        )
        vectors, vectors_low = split_low(vectors)
        down = [0.5 * a_down[:, 128 * b : 128 * b + 128].T for b in range(4)]
        spots = ((0, 0), (1, 0), (2, 0), (3, 0), (1, 1), (3, 1), (2, 2), (3, 2), (3, 3))

        def edge(at, rows):
            patch, place = spots[at]
            rows = slice(128 * patch + rows.start, 128 * patch + rows.stop)
            return a_rest[rows, 64 * place : 64 * place + 64]


        def piece(at, shard):
            rows = slice(16 * shard, 16 * shard + 16)
            if at < G1_EDGE:
                start = 128 * (at // 2) + 16 * shard
                return a_conv[start : start + 16, 128 * (at % 2) : 128 * (at % 2) + 128]
            if at < G1_UP:
                one = edge(2 * (at - G1_EDGE), rows)
                two = jnp.zeros((16, 64), F32)
                if at < G1_UP - 1:
                    two = edge(2 * (at - G1_EDGE) + 1, rows)
                return jnp.concatenate([one, two], axis=1)
            if at < G1_DOWN:
                b = at - G1_UP
                return a_up[rows, 128 * b : 128 * b + 128]
            if at < G1_PROJ:
                start = 64 * (shard % 2) + 16 * (at - G1_DOWN)
                return down[shard // 2][start : start + 16, :]
            return a_proj[rows, :]

        for peer in range(4):
            to = lax.bitwise_xor(chip, peer)
            for at in range(G1_VEC):
                one, two = piece(at, 2 * peer), piece(at, 2 * peer + 1)
                keep_ref[to, 16 * at : 16 * at + 16, :] = jnp.where(core == 0, one, two)
                send_ref[to, 16 * at : 16 * at + 16, :] = jnp.where(core == 0, two, one).astype(BF)
            for at, values in ((G1_VEC, vectors), (G1_VEC_LOW, vectors_low)):
                keep_ref[to, 16 * at : 16 * at + 16, :] = values
                send_ref[to, 16 * at : 16 * at + 16, :] = values.astype(BF)


def branch_kernel(
    placed, valid, unit_ref, mix_ref, head_ref, reduce_ref, expand_ref, units_ref, gcat_ref, dmix_ref,
    vec_ref, pk_ref,
    spread_ref, keep_ref, send_ref,
    wcat, a_cat, a_edge, grads,
):
    step, steps = pl.program_id(0), pl.num_programs(0)
    count = unit_ref.shape[0] // BRANCH_STEPS

    @pl.when(step == 0)
    def _():
        for k, weight in enumerate(branch_weights(pk_ref)):
            wcat[128 * k : 128 * k + 128, :] = weight.astype(F32)
        for ref in (a_cat, a_edge, grads):
            ref[...] = jnp.zeros(ref.shape, ref.dtype)

    def row(at, width=128):
        return vec_ref[at : at + 1, 0:width]

    offsets = (iota((128, 128), 0) + 1) % 3 - 1
    for m in range(count):
        image = step * count + m
        outer = dot_tn(unit_ref[image], gcat_ref[image])
        plain = outer[:, 0:128]
        parts = (
            jnp.where(offsets == 1, outer[:, 128:256], jnp.where(offsets == -1, outer[:, 256:384], plain)),
            jnp.where(offsets == 1, outer[:, 384:512], jnp.where(offsets == -1, outer[:, 512:640], plain)),
            plain,
        )
        maps = gcat_ref[image, :, 0:128].astype(F32).reshape(32, 32, 128)
        by_column = jnp.sum(maps, axis=0)
        total = jnp.sum(by_column, axis=0, keepdims=True)
        left, right = by_column[0:1], by_column[31:32]
        upper = jnp.sum(maps[0], axis=0, keepdims=True)
        lower = jnp.sum(maps[31], axis=0, keepdims=True)
        for k in range(3):
            at = 8 * k + image
            part = parts[k]
            mixing = mix_ref[pl.ds(at, 1), :]
            a_cat[128 * k : 128 * k + 128, :] += part * mixing
            a_edge[k : k + 1, :] += mixing * total
            if k == 0:
                a_edge[3:4, :] += mixing * lower
                a_edge[4:5, :] += mixing * upper
            if k == 1:
                a_edge[5:6, :] += mixing * right
                a_edge[6:7, :] += mixing * left

    @pl.when(step == steps - 1)
    def _():
        counts = count_column(valid)
        pooled, hidden, slope = [head_ref[8 * at : 8 * at + 8, :] for at in range(3)]
        mixing = [mix_ref[8 * k : 8 * k + 8, :] for k in range(3)]
        grads_mix = [dmix_ref[8 * k : 8 * k + 8, :] for k in range(3)]
        mean = sum(m * g for m, g in zip(mixing, grads_mix))
        grad_logits = jnp.concatenate([m * (g - mean) for m, g in zip(mixing, grads_mix)], axis=1)
        grad_pre = dot_wide(grad_logits, expand_ref[...], dot_nt) * slope
        grad_pooled = dot_wide(grad_pre, reduce_ref[...], dot_nt)
        per_pixel = grad_pooled / counts
        branches = jnp.concatenate(branch_weights(pk_ref), axis=0)
        spread = dot_wide(per_pixel, branches, dot_nt)
        for k in range(3):
            spread_ref[8 * k : 8 * k + 8, :] = spread[:, 128 * k : 128 * k + 128]
        for at, part in enumerate(parts_of(outer_wide(pooled, grad_pre), 2)):
            grads[:, 32 * at : 32 * at + 32] = dot_nt(part, spread_matrix())[:, 0:32]
        picks = jnp.concatenate([pick_matrix(k) for k in range(3)], axis=1)
        grads[:, 128:512] = dot_nt(outer_wide(hidden, grad_logits).astype(BF), picks)
        summed = jnp.broadcast_to(jnp.sum(grad_logits, axis=0, keepdims=True), (8, 384))
        expand_bias = dot_wide(summed, picks, dot_nt)[0:1]
        reduce_bias = jnp.sum(grad_pre, axis=0, keepdims=True)
        pooled_sum = jnp.sum(grad_pooled, axis=0, keepdims=True)
        gain, bias = column(row(V_GAIN1)), column(row(V_BIAS1))
        unit_sums = jnp.concatenate([units_ref[8 * k : 8 * k + 8, :] for k in range(3)], axis=1)
        unit_part = a_cat[...] + outer_wide(unit_sums, per_pixel)
        edge_part = outer_wide(jnp.concatenate(inside_counts(valid), axis=1), per_pixel)
        to_gain, to_bias = jnp.zeros((128, 128), F32), jnp.zeros((128, 128), F32)
        for k in range(3):
            here = slice(128 * k, 128 * k + 128)
            edges = edge_part[here] + a_edge[k : k + 1, :]
            if k < 2:
                edges = edges - jnp.where(offsets == 1, a_edge[2 * k + 3 : 2 * k + 4, :], 0.0)
                edges = edges - jnp.where(offsets == -1, a_edge[2 * k + 4 : 2 * k + 5, :], 0.0)
            to_gain = to_gain + unit_part[here] * wcat[here, :]
            to_bias = to_bias + edges * wcat[here, :]
            a_cat[here, :] = gain * unit_part[here] + bias * edges
        ones = jnp.ones((8, 384), BF)
        chip, core = place_of(placed)
        vectors = jnp.concatenate(
            [
                dot_nt(ones, jnp.concatenate(parts_of(to_gain, 3), axis=1))[0:1],
                dot_nt(ones, jnp.concatenate(parts_of(to_bias, 3), axis=1))[0:1],
                a_edge[0:1, :] + pooled_sum,
                a_edge[1:2, :] + pooled_sum,
                reduce_bias,
                expand_bias[:, 0:128],
                expand_bias[:, 128:256],
                expand_bias[:, 256:384],
            ],
            axis=0,
        )
        vectors = jnp.concatenate(split_low(vectors), axis=0)

        def piece(at, shard):
            rows = slice(16 * shard, 16 * shard + 16)
            if at < G2_REDUCE:
                return a_cat[128 * at + 16 * shard : 128 * at + 16 * shard + 16, :]
            if at == G2_REDUCE:
                return grads[rows, 0:128]
            return jnp.concatenate(
                [grads[16 * shard : 16 * shard + 4, 128 * b : 128 * b + 128] for b in range(1, 4)]
                + [jnp.zeros((4, 128), F32)],
                axis=0,
            )

        for peer in range(4):
            to = lax.bitwise_xor(chip, peer)
            for at in range(G2_VEC):
                one, two = piece(at, 2 * peer), piece(at, 2 * peer + 1)
                keep_ref[to, 16 * at : 16 * at + 16, :] = jnp.where(core == 0, one, two)
                send_ref[to, 16 * at : 16 * at + 16, :] = jnp.where(core == 0, two, one).astype(BF)
            keep_ref[to, 16 * G2_VEC : 16 * G2_VEC + 16, :] = vectors
            send_ref[to, 16 * G2_VEC : 16 * G2_VEC + 16, :] = vectors.astype(BF)


def input_kernel(base, valid, x_ref, mix_ref, spread, gcat_ref, gfirst_ref, vec_ref, pk_ref, *rest):
    grad_ref, token, wcat = rest[-3:]
    token[...] = jnp.zeros((8, 128), F32)
    step, count = pl.program_id(0), grad_ref.shape[0]

    @pl.when(step == 0)
    def _():
        offsets = (iota((128, 128), 0) + 1) % 3 - 1
        height, width, channel = [weight.astype(F32) for weight in branch_weights(pk_ref)]
        for at, (weight, offset) in enumerate(
            ((height, 0), (height, 1), (height, -1), (width, 0), (width, 1), (width, -1))
        ):
            wcat[:, 128 * at : 128 * at + 128] = jnp.where(offsets == offset, weight, 0.0)
        wcat[:, 768:896] = channel

    for m in range(count):
        image = base + step * count + m
        by_height, by_width, by_channel = [mix_ref[pl.ds(8 * k + image, 1), :] for k in range(3)]
        scaled = jnp.concatenate(
            [
                wcat[:, 0:128] * by_height + wcat[:, 384:512] * by_width + wcat[:, 768:896] * by_channel,
                wcat[:, 128:256] * by_height,
                wcat[:, 256:384] * by_height,
                wcat[:, 512:640] * by_width,
                wcat[:, 640:768] * by_width,
            ],
            axis=1,
        ).astype(BF)
        row, row_taker, col, col_taker = shifted_masks(valid, image)
        high, wide, plain = [spread[pl.ds(8 * k + image, 1), :].reshape(1, 1, 128) for k in range(3)]
        even = row * (col_taker * wide + col * plain) + row_taker * (col * high)
        grad_ref[m] = dot_nt(gcat_ref[image], scaled) + even.reshape(1024, 128)
    pixels = 1024 * count
    scaled_grad = grad_ref[...].reshape(pixels, 128) * vec_ref[V_GAIN1 : V_GAIN1 + 1, 0:128]
    here = pl.ds(base + step * count, count)
    values = x_ref[here].reshape(pixels, 128).astype(F32)
    centre = values - lane_mean(values)
    scale = lax.rsqrt(lane_mean(centre * centre) + EPS)
    unit = centre * scale
    grad = gfirst_ref[here].reshape(pixels, 128) + scale * (
        scaled_grad - lane_mean(scaled_grad) - unit * lane_mean(scaled_grad * unit)
    )
    grad_ref[...] = grad.reshape(count, 1024, 128)


def conv_kernel(pm_ref, vec_ref, wconv, after, map_ref, token):
    token[...] = jnp.zeros((8, 128), F32)
    count = map_ref.shape[0]
    out = dot(pm_ref[...].reshape(256 * count, 1152), wconv[...])
    out = out + vec_ref[V_BCONV : V_BCONV + 1, 0:384]
    map_ref[...] = out[:, 0:320].astype(BF).reshape(count, 256, 320)


def sds(shape, dtype):
    return jax.ShapeDtypeStruct(shape, dtype)


def whole(shape):
    return pl.BlockSpec(shape, lambda s: (0,) * len(shape))


def params(mega):
    return pltpu.CompilerParams(vmem_limit_bytes=mega * 1024 * 1024)


def cost(microseconds):
    return pl.CostEstimate(
        flops=int(microseconds * 3e8), bytes_accessed=int(microseconds * 3e6), transcendentals=0
    )


VMEM_SPEC = pl.BlockSpec(memory_space=pltpu.VMEM)
ANY_SPEC = pl.BlockSpec(memory_space=pl.ANY)


def in_vmem(value):
    return pltpu.with_memory_space_constraint(value, pltpu.VMEM)


def in_hbm(value):
    return pltpu.with_memory_space_constraint(value, pltpu.HBM)


def per_step(shape, index):
    return pl.BlockSpec(shape, lambda s: (index(s),) + (0,) * (len(shape) - 1))


def same(step):
    return step


UNIT_IMAGES, MLP_IMAGES, INPUT_IMAGES, CONV_IMAGES = 2, 2, 2, 4
BRANCH_STEPS = 2
SMALL_MB, UNIT_MB, NORM_MB, MLP_MB, BRANCH_MB, INPUT_MB, CONV_MB = 8, 16, 16, 35, 16, 20, 16


def cot_specs(count):
    return [per_step((count, rows, 256), same) for rows in (272, 272, 256)]


def run_unit(valid, x, cot):
    images, count = x.shape[0], UNIT_IMAGES
    return pl.pallas_call(
        unit_kernel,
        grid=(images // count,),
        in_specs=[VMEM_SPEC, per_step((count, 1024, 128), same), per_step((count, 256, 320), same)],
        out_specs=[VMEM_SPEC] * 3 + cot_specs(count) + [VMEM_SPEC],
        out_shape=[
            pltpu.VMEM((images, 1024, 128), F32),
            pltpu.VMEM((images, 1024, 128), BF),
            sds((24, 128), F32),
            sds((images, 272, 256), BF),
            sds((images, 272, 256), BF),
            sds((images, 256, 256), BF),
            sds((8, 384), F32),
        ],
        scratch_shapes=[pltpu.VMEM((264, 384), F32)],
        compiler_params=params(UNIT_MB),
        cost_estimate=cost(4),
        name="unit",
    )(valid, in_hbm(x), in_hbm(cot))


def run_norm(placed, valid, unit, *parts):
    images = unit.shape[0]
    return pl.pallas_call(
        functools.partial(norm_kernel, placed),
        in_specs=[VMEM_SPEC] * 6,
        out_specs=[VMEM_SPEC] * 7,
        out_shape=[
            pltpu.VMEM((images, 1024, 128), BF),
            sds((24, 128), F32),
            sds((128, 128), BF),
            sds((128, 384), BF),
            sds((24, 128), F32),
            sds((16, 512), F32),
            pltpu.VMEM((SHARDS, ROWS, 128), BF),
        ],
        scratch_shapes=[pltpu.VMEM((24, 128), F32)],
        compiler_params=params(NORM_MB),
        cost_estimate=cost(5),
        name="norm",
    )(valid, in_vmem(unit), *parts)


def run_mlp(placed, x, normed, mix, cot, vec, packed, *conv):
    images, count = x.shape[0], MLP_IMAGES
    pixels = 1024 * count
    g1 = (4, 16 * G1_BLOCKS, 128)
    shapes = [
        ((384, 128), BF), ((128, 128), BF), ((128, 512), BF), ((512, 128), BF), ((512, 256), BF),
        ((32 * count, 32, 128), F32), ((count, 34, 48, 128), F32),
        ((pixels, 512), BF), ((pixels, 512), BF), ((pixels, 128), BF), ((pixels, 384), F32), ((pixels, 128), BF),
        ((pixels, 128), BF), ((pixels, 128), BF), ((count, 34, 48, 128), F32),
        ((1152, 256), F32), ((512, 256), F32), ((128, 512), F32), ((128, 512), F32), ((128, 128), F32),
        ((8, 512), F32), ((8, 128), F32), ((8, 128), F32), ((8, 128), F32), ((8, 128), F32),
    ]
    return pl.pallas_call(
        functools.partial(mlp_kernel, placed),
        grid=(images // count,),
        in_specs=[VMEM_SPEC]
        + [VMEM_SPEC] * 2
        + cot_specs(count)
        + [VMEM_SPEC] * 7,
        out_specs=[per_step((count, 256, 1152), same), per_step((count, 1024, 128), same)] + [VMEM_SPEC] * 5,
        out_shape=[
            sds((images, 256, 1152), BF),
            sds((images, 1024, 128), F32),
            pltpu.VMEM((images, 1024, 640), BF),
            sds((24, 128), F32),
            pltpu.VMEM((1152, 384), BF),
            pltpu.VMEM(g1, F32),
            pltpu.VMEM(g1, BF),
        ],
        scratch_shapes=[pltpu.VMEM(*shape) for shape in shapes],
        compiler_params=params(MLP_MB),
        cost_estimate=cost(35),
        name="mlp",
    )(in_vmem(x), in_vmem(normed), mix, *[in_hbm(part) for part in cot[0:3]], cot[3], vec, in_vmem(packed), *conv)


def run_branches(placed, valid, unit, mix, head, reduce, expand, units, gcat, dmix, vec, packed):
    g2 = (4, 16 * G2_BLOCKS, 128)
    shapes = [
        ((384, 128), F32), ((384, 128), F32), ((8, 128), F32), ((128, 512), F32),
    ]
    return pl.pallas_call(
        functools.partial(branch_kernel, placed),
        grid=(BRANCH_STEPS,),
        in_specs=[VMEM_SPEC] * 11,
        out_specs=[VMEM_SPEC] * 3,
        out_shape=[sds((24, 128), F32), sds(g2, F32), sds(g2, BF)],
        scratch_shapes=[pltpu.VMEM(*shape) for shape in shapes],
        compiler_params=params(BRANCH_MB),
        cost_estimate=cost(8),
        name="branches",
    )(valid, in_vmem(unit), mix, head, reduce, expand, units, in_vmem(gcat), dmix, vec, in_vmem(packed))


def run_input(base, held, valid, x, mix, spread, gcat, gfirst, vec, packed, after):
    images, count = x.shape[0], INPUT_IMAGES
    maps = per_step((count, 1024, 128), lambda s: s + base // count)
    more = [] if held is None else [held]
    return pl.pallas_call(
        functools.partial(input_kernel, base),
        grid=(images // count // 2,),
        in_specs=[
            VMEM_SPEC, VMEM_SPEC, VMEM_SPEC, VMEM_SPEC, VMEM_SPEC, VMEM_SPEC, VMEM_SPEC, VMEM_SPEC, ANY_SPEC,
        ]
        + [ANY_SPEC] * len(more),
        out_specs=[maps, whole((8, 128))],
        out_shape=[sds((images, 1024, 128), F32), sds((8, 128), F32)],
        scratch_shapes=[pltpu.VMEM((128, 896), F32)],
        compiler_params=params(INPUT_MB),
        input_output_aliases={9: 0} if more else {},
        cost_estimate=cost(4),
        name="input_grad",
    )(valid, in_vmem(x), mix, spread, in_vmem(gcat), in_vmem(gfirst), vec, in_vmem(packed), after, *more)


def run_conv(pm, vec, wconv, after):
    images, count = pm.shape[0], CONV_IMAGES
    return pl.pallas_call(
        conv_kernel,
        grid=(images // count,),
        in_specs=[per_step((count, 256, 1152), same), VMEM_SPEC, VMEM_SPEC, ANY_SPEC],
        out_specs=[per_step((count, 256, 320), same), whole((8, 128))],
        out_shape=[sds((images, 256, 320), BF), sds((8, 128), F32)],
        compiler_params=params(CONV_MB),
        cost_estimate=cost(4),
        name="conv_out",
    )(in_hbm(pm), vec, in_vmem(wconv), after)


def pack_weights(weights):
    return pl.pallas_call(
        pack_kernel,
        out_shape=pltpu.VMEM((ROWS + CONV_ROWS, 128), BF),
        in_specs=[VMEM_SPEC] * 21,
        out_specs=VMEM_SPEC,
        scratch_shapes=[pltpu.VMEM((16, 128), F32)],
        compiler_params=params(60),
        name="pack",
    )(*weights)


def join_kernel(one, two, three, after, small, conv):
    for at, part in enumerate((one, two, three)):
        small[at] = part[0:ROWS, :]
        conv[at] = part[ROWS : ROWS + CONV_ROWS, :]


def join(near, after):
    return pl.pallas_call(
        join_kernel,
        out_shape=[sds((3, ROWS, 128), BF), sds((3, CONV_ROWS, 128), BF)],
        in_specs=[VMEM_SPEC] * 3 + [ANY_SPEC],
        out_specs=[VMEM_SPEC] * 2,
        compiler_params=params(SMALL_MB),
        cost_estimate=cost(1),
        name="join",
    )(*near, after)


def refine(ref, values):
    ref[...] = values.astype(BF)
    at = 16 * G1_VEC
    both = split_low(values[at : at + 16] + values[at + 16 : at + 32])
    ref[at : at + 32, :] = jnp.concatenate(both, axis=0).astype(BF)
    at = 16 * (G1_BLOCKS + G2_VEC)
    both = split_low(values[at : at + 8] + values[at + 8 : at + 16])
    ref[at : at + 16, :] = jnp.concatenate(both, axis=0).astype(BF)
    at = 16 * (G1_BLOCKS + G2_REDUCE)
    both = split_low(values[at : at + 16, 0:32] + values[at : at + 16, 32:64])
    ref[at : at + 16, 0:64] = jnp.concatenate(both, axis=1).astype(BF)


def sum_pair_kernel(keep1, got1, keep2, got2, own, *others):
    for peer in range(4):
        one = keep1[peer] + got1[peer].astype(F32)
        two = keep2[peer] + got2[peer].astype(F32)
        values = jnp.concatenate([one, two], axis=0)
        if peer == 0:
            own[...] = values
        else:
            refine(others[peer - 1], values)


def sum_four_kernel(own, one, two, three, after, total, low):
    value = own[...] + one[...].astype(F32) + two[...].astype(F32) + three[...].astype(F32)
    total[...] = value
    refine(low, value)


def sum_two_kernel(own, one, after, total, low):
    value = own[...] + one[...].astype(F32)
    total[...] = value
    refine(low, value)


def sum_two(*values):
    shape = values[0].shape
    return pl.pallas_call(
        sum_two_kernel,
        out_shape=[sds(shape, F32), sds(shape, BF)],
        in_specs=[VMEM_SPEC] * 2 + [ANY_SPEC],
        out_specs=[VMEM_SPEC] * 2,
        compiler_params=params(SMALL_MB),
        cost_estimate=cost(1),
        name="sum_two",
    )(*values)


def sum_pair(keep1, got1, keep2, got2):
    rows = keep1.shape[1] + keep2.shape[1]
    return pl.pallas_call(
        sum_pair_kernel,
        out_shape=[sds((rows, 128), F32)] + [sds((rows, 128), BF)] * 3,
        in_specs=[VMEM_SPEC] * 4,
        out_specs=[VMEM_SPEC] * 4,
        compiler_params=params(SMALL_MB),
        cost_estimate=cost(2),
        name="sum_pair",
    )(keep1, got1, keep2, got2)


def sum_four(*values):
    shape = values[0].shape
    return pl.pallas_call(
        sum_four_kernel,
        out_shape=[sds(shape, F32), sds(shape, BF)],
        in_specs=[VMEM_SPEC] * 4 + [ANY_SPEC],
        out_specs=[VMEM_SPEC] * 2,
        compiler_params=params(SMALL_MB),
        cost_estimate=cost(2),
        name="sum_four",
    )(*values)


def finish_kernel(*refs):
    (own, far,
     gain_one, bias_one, w_h, b_h, w_w, b_w, w_c, w_red, b_red, w_exp, b_exp, w_proj, b_proj,
     gain_two, bias_two, w_up, b_up, w_down, b_down, w_conv, b_conv) = refs
    shard = lax.axis_index("fsdp")

    def first(at, rows=16):
        here = slice(16 * at, 16 * at + rows)
        return own[here, :] + far[here, :].astype(F32)

    def second(at, rows=16):
        return first(G1_BLOCKS + at, rows)

    w_h[...] = second(G2_HEIGHT)
    w_w[...] = second(G2_WIDTH)
    w_c[...] = second(G2_CHANNEL)
    reduce = second(G2_REDUCE)
    w_red[...] = reduce[:, 0:32] + reduce[:, 32:64]
    expand = second(G2_EXPAND)
    for b in range(3):
        w_exp[:, 128 * b : 128 * b + 128] = expand[4 * b : 4 * b + 4, :]
    w_proj[...] = first(G1_PROJ)
    for b in range(4):
        w_up[:, 128 * b : 128 * b + 128] = first(G1_UP + b)
    w_down[...] = first(G1_DOWN, 64)
    for at, tap in enumerate(TAPS):
        kernel = w_conv.at[tap // 3, tap % 3]
        for b in range(2):
            kernel[:, 128 * b : 128 * b + 128] = first(G1_CONV + 2 * at + b)
        edge = 64 * (at % 2)
        kernel[:, 256:320] = first(G1_EDGE + at // 2)[:, edge : edge + 64]
    table_one, table_two = first(G1_VEC) + first(G1_VEC_LOW), second(G2_VEC)
    table_two = table_two[0:8, :] + table_two[8:16, :]

    def share(table, row, blocks, length, stride):
        total = jnp.zeros((1, 128), F32)
        for b in range(blocks):
            pick = iota((128, 128), 0) + 128 * b == iota((128, 128), 1) + shard * stride
            total = total + dot_wide(table, pick.astype(BF))[row + b : row + b + 1, :]
        return total[:, 0:length].reshape(length)

    gain_one[...] = share(table_two, G2_GAIN1, 1, 16, 16)
    bias_one[...] = share(table_two, G2_BIAS1, 1, 16, 16)
    b_h[...] = share(table_two, G2_BH, 1, 16, 16)
    b_w[...] = share(table_two, G2_BW, 1, 16, 16)
    b_red[...] = share(table_two, G2_BR, 1, 4, 16)
    b_exp[...] = share(table_two, G2_BE, 3, 48, 48)
    b_proj[...] = share(table_one, G1_BPROJ, 1, 16, 16)
    gain_two[...] = share(table_one, G1_GAIN2, 1, 16, 16)
    bias_two[...] = share(table_one, G1_BIAS2, 1, 16, 16)
    b_up[...] = share(table_one, G1_BUP, 4, 64, 64)
    b_down[...] = share(table_one, G1_BDOWN, 1, 16, 16)
    b_conv[...] = share(table_one, G1_BCONV, 3, 40, 40)


def finish(sums, weights):
    return pl.pallas_call(
        finish_kernel,
        out_shape=[sds(w.shape, F32) for w in weights],
        in_specs=[VMEM_SPEC] * 2,
        out_specs=[VMEM_SPEC] * 21,
        compiler_params=params(SMALL_MB),
        name="finish",
    )(*sums)


def early(placed, input_map, valid_size, cotangent, gathered):
    images = input_map.shape[0]
    x = input_map.reshape(images, 1024, 128)
    valid_size = valid_size.T
    cot = cotangent.reshape(images, 256, 320)
    unit, unit_low, units, main, right, rest, bias = run_unit(valid_size, x, cot)
    small, conv = gathered(units)
    normed, head, reduce, expand, mix, vec, packed = run_norm(placed, valid_size, unit, *small)
    pm, gfirst, gcat, dmix, wconv, keep1, send1 = run_mlp(
        placed, x, normed, mix, (main, right, rest, bias), vec, packed, *conv
    )
    spread, keep2, send2 = run_branches(
        placed, valid_size, unit_low, mix, head, reduce, expand, units, gcat, dmix, vec, packed
    )

    def late_map(after):
        out, token = run_conv(pm, vec, wconv, after)
        return out.reshape(images, 16, 16, 320), token

    def late_grad(after, held=None):
        base = 0 if held is None else images // 2
        return run_input(base, held, valid_size, x, mix, spread, gcat, gfirst, vec, packed, after)

    return (keep1, send1, keep2, send2), late_map, late_grad


def spread_out(packed):
    own = (packed[0], packed[1])
    return [
        own + (packed[2::2, rows], packed[3::2, rows]) for rows in (slice(0, ROWS), slice(ROWS, None))
    ]


def compute(placed, input_map, valid_size, cotangent, packed):
    sums, late_map, late_grad = early(
        placed,
        input_map,
        valid_size,
        cotangent,
        lambda after: spread_out(packed),
    )
    input_grad = late_grad(sums[0], late_grad(sums[0])[0])[0]
    return late_map(sums[0])[0], input_grad.reshape(input_map.shape), sums


def pack_whole(weights):
    (gain_one, bias_one, w_h, b_h, w_w, b_w, w_c, w_red, b_red, w_exp, b_exp, w_proj, b_proj,
     gain_two, bias_two, w_up, b_up, w_down, b_down, w_conv, b_conv) = weights

    def split(weight):
        weight = weight.reshape(SHARDS, weight.shape[0] // SHARDS, weight.shape[1])
        rows, cols = -weight.shape[1] % 16, -weight.shape[2] % 128
        weight = jnp.pad(weight, ((0, 0), (0, rows), (0, cols)))
        return [weight[:, :, at : at + 128] for at in range(0, weight.shape[2], 128)]

    pieces = split(w_h) + split(w_w) + split(w_c) + split(w_proj) + split(w_red) + split(w_exp)
    pieces = pieces + split(w_up) + split(w_down)
    taps = [split(w_conv[tap // 3, tap % 3]) for tap in TAPS]
    edges = [tap[2][:, :, 0:64] for tap in taps]
    edges.append(jnp.zeros_like(edges[0]))
    conv = [part for tap in taps for part in tap[0:2]]
    conv = conv + [jnp.concatenate(edges[at : at + 2], axis=2) for at in range(0, 10, 2)]
    vectors = (gain_one, bias_one, b_h, b_w, b_red, b_exp, b_proj, gain_two, bias_two, b_up, b_down, b_conv)
    rows = [
        jnp.pad(v.reshape(SHARDS, 1, v.shape[0] // SHARDS), ((0, 0), (0, 0), (0, 128 - v.shape[0] // SHARDS)))
        for v in vectors
    ]
    rows = rows + [jnp.zeros((SHARDS, 4, 128), BF)]
    return jnp.concatenate(pieces + [jnp.concatenate(rows, axis=1)] + conv, axis=1)


def unpack_whole(sums):
    one = jnp.stack([sums[0], sums[1].astype(F32)], axis=1).reshape(SHARDS, -1, 128)
    two = jnp.stack([sums[2], sums[3].astype(F32)], axis=1).reshape(SHARDS, -1, 128)

    def join(buffer, at, blocks, rows=16):
        parts = [buffer[:, 16 * (at + b) : 16 * (at + b) + rows, :] for b in range(blocks)]
        return jnp.concatenate(parts, axis=2).reshape(SHARDS * rows, 128 * blocks)

    def vector(buffer, at, row, blocks=1):
        start, rest = 16 * at + row, 16 if at == G1_VEC else 8
        both = buffer[0, start : start + blocks, :] + buffer[0, start + rest : start + rest + blocks, :]
        return both.reshape(128 * blocks)

    expand = two[:, 16 * G2_EXPAND : 16 * G2_EXPAND + 12, :].reshape(SHARDS, 3, 4, 128)
    taps = []
    for tap in range(9):
        at = TAPS.index(tap)
        edge = join(one, G1_EDGE + at // 2, 1)[:, 64 * (at % 2) : 64 * (at % 2) + 64]
        taps.append(jnp.concatenate([join(one, G1_CONV + 2 * at, 2), edge], axis=1))
    return (
        vector(two, G2_VEC, G2_GAIN1),
        vector(two, G2_VEC, G2_BIAS1),
        join(two, G2_HEIGHT, 1),
        vector(two, G2_VEC, G2_BH),
        join(two, G2_WIDTH, 1),
        vector(two, G2_VEC, G2_BW),
        join(two, G2_CHANNEL, 1),
        join(two, G2_REDUCE, 1)[:, 0:32] + join(two, G2_REDUCE, 1)[:, 32:64],
        vector(two, G2_VEC, G2_BR).reshape(SHARDS, 16)[:, 0:4].reshape(32),
        expand.transpose(0, 2, 1, 3).reshape(32, 384),
        vector(two, G2_VEC, G2_BE, 3),
        join(one, G1_PROJ, 1),
        vector(one, G1_VEC, G1_BPROJ),
        vector(one, G1_VEC, G1_GAIN2),
        vector(one, G1_VEC, G1_BIAS2),
        join(one, G1_UP, 4),
        vector(one, G1_VEC, G1_BUP, 4),
        one[:, 16 * G1_DOWN : 16 * G1_DOWN + 64, :].reshape(512, 128),
        vector(one, G1_VEC, G1_BDOWN),
        jnp.stack(taps).reshape(3, 3, 128, 320),
        vector(one, G1_VEC, G1_BCONV, 3)[0:320],
    )


def shards_of(mesh):
    shards, copies = mesh.shape["fsdp"], mesh.shape["rep"]

    def eight(input_map, valid_size, *rest):
        weights, cotangent = rest[:-1], rest[-1]
        sibling = [(i, i ^ 1) for i in range(shards)]
        packs = pack_weights(weights)
        swapped = lax.ppermute(packs, "fsdp", sibling)
        near = [
            lax.ppermute(packs, "fsdp", [(i, i ^ (2 * peer)) for i in range(shards)])
            for peer in range(1, 4)
        ]

        def gathered(after):
            small, conv = join(near, after)
            own = (packs, swapped)
            return own + (small, lax.ppermute(small, "fsdp", sibling)), (
                own + (conv, lax.ppermute(conv, "fsdp", sibling))
            )

        (keep1, send1, keep2, send2), late_map, late_grad = early(
            True, input_map, valid_size, cotangent, gathered
        )
        got1, got2 = lax.ppermute(send1, "fsdp", sibling), lax.ppermute(send2, "fsdp", sibling)
        own, *others = sum_pair(keep1, got1, keep2, got2)
        moved = [
            lax.ppermute(value, "fsdp", [(i, i ^ (2 * (peer + 1))) for i in range(shards)])
            for peer, value in enumerate(others)
        ]
        out, token = late_map(own)
        total, low = sum_four(own, *moved, token)
        both = [(copy, shard) for copy in range(copies) for shard in range(shards)]
        steps = [
            [(z * shards + f, (z ^ (1 + (f + at) % 2)) * shards + f) for z, f in both] for at in range(2)
        ]
        far = lax.ppermute(low, ("rep", "fsdp"), steps[0])
        held, token = late_grad(total)
        total, low = sum_two(total, far, token)
        far = lax.ppermute(low, ("rep", "fsdp"), steps[1])
        input_grad = late_grad(total, held)[0].reshape(input_map.shape)
        return (out, input_grad) + tuple(finish((total, far), weights))

    def general(input_map, valid_size, *rest):
        weights, cotangent = rest[:-1], rest[-1]
        dims = [2 if w.ndim == 4 else 0 for w in weights]
        full = [lax.all_gather(w, "fsdp", axis=d, tiled=True) for w, d in zip(weights, dims)]
        packed = pack_whole(full)
        out, input_grad, sums = compute(False, input_map, valid_size, cotangent, packed)
        grads = [
            lax.psum_scatter(g, "fsdp", scatter_dimension=d, tiled=True)
            for g, d in zip(unpack_whole(sums), dims)
        ]
        return (out, input_grad) + tuple(lax.psum(grads, "rep"))

    return eight if shards == SHARDS and copies == 4 else general


def solution(mesh):
    maps = P(("rep", "fsdp"), None, None, None)
    vector, matrix = P("fsdp"), P("fsdp", None)
    weights = (
        vector, vector, matrix, vector, matrix, vector, matrix, matrix, vector, matrix, vector,
        matrix, vector, vector, vector, matrix, vector, matrix, vector,
        P(None, None, "fsdp", None), vector,
    )
    return jax.shard_map(
        shards_of(mesh),
        mesh=mesh,
        in_specs=(maps, P(("rep", "fsdp"), None)) + weights + (maps,),
        out_specs=(maps, maps) + weights,
        check_vma=False,
    )
```

```python
import functools

import jax
import jax.numpy as jnp
from jax import lax
from jax.experimental import pallas as pl
from jax.experimental.pallas import tpu as pltpu
from jax.sharding import PartitionSpec as P

BF = jnp.bfloat16
F32 = jnp.float32
HIGH = lax.Precision.HIGHEST
EPS = 1e-05

SHARDS = 8
B_HEIGHT, B_WIDTH, B_CHANNEL, B_PROJ, B_REDUCE = 0, 1, 2, 3, 4
B_EXPAND, B_UP, B_DOWN, B_VEC, BLOCKS = 5, 8, 12, 16, 17
C_PAIRS, C_EDGES, C_BLOCKS = 0, 18, 23
ROWS, CONV_ROWS = 16 * BLOCKS, 16 * C_BLOCKS
TAPS = (4, 5, 7, 8, 3, 6, 1, 2, 0)
(V_GAIN1, V_BIAS1, V_BH, V_BW, V_BR, V_BE, V_BP, V_GAIN2, V_BIAS2, V_BUP, V_BDOWN, V_BCONV) = range(12)
LENGTHS = (16, 16, 16, 16, 4, 48, 16, 16, 16, 64, 16, 40)
G1_CONV, G1_EDGE, G1_UP, G1_DOWN, G1_PROJ, G1_VEC, G1_VEC_LOW, G1_BLOCKS = 0, 18, 23, 27, 31, 32, 33, 34
G1_BCONV, G1_BUP, G1_BDOWN, G1_BPROJ, G1_GAIN2, G1_BIAS2 = 0, 3, 7, 8, 9, 10
G2_HEIGHT, G2_WIDTH, G2_CHANNEL, G2_REDUCE, G2_EXPAND, G2_VEC, G2_BLOCKS = 0, 1, 2, 3, 4, 5, 6
G2_GAIN1, G2_BIAS1, G2_BH, G2_BW, G2_BR, G2_BE = 0, 1, 2, 3, 4, 5


def iota(shape, axis):
    return lax.broadcasted_iota(jnp.int32, shape, axis)


def dot(left, right):
    return jnp.dot(left, right, preferred_element_type=F32)


def dot_nt(left, right):
    return lax.dot_general(left, right, (((1,), (1,)), ((), ())), preferred_element_type=F32)


def dot_tn(left, right):
    return lax.dot_general(left, right, (((0,), (0,)), ((), ())), preferred_element_type=F32)


def parts_of(values, count):
    parts = []
    for _ in range(count):
        parts.append(values.astype(BF))
        values = values - parts[-1].astype(F32)
    return parts


def dot_wide(left, right, product=dot):
    rows = left.shape[0]
    joined = product(jnp.concatenate(parts_of(left, 3), axis=0), right)
    return joined[0:rows] + (joined[rows : 2 * rows] + joined[2 * rows : 3 * rows])


def outer_wide(left, right):
    (left_high, left_low), (right_high, right_low) = parts_of(left, 2), parts_of(right, 2)
    return dot_tn(
        jnp.concatenate([left_high, left_high, left_low, left_low], axis=0),
        jnp.concatenate([right_high, right_low, right_high, right_low], axis=0),
    )


def fold8(values):
    rows, cols = values.shape
    return jnp.sum(values.reshape(rows // 8, 8, cols), axis=0)


def lane_mean(values):
    return jnp.mean(values, axis=-1, keepdims=True)


def gelu_both(values):
    cdf = 0.5 + 0.5 * lax.erf(values * 0.7071067811865476)
    slope = cdf + values * (jnp.exp(-0.5 * (values * values)) * 0.3989422804014327)
    return values * cdf, slope


def gelu_twice(values):
    cdf = 1.0 + lax.erf(values * 0.7071067811865476)
    density = (values * 0.7978845608028654) * jnp.exp2((values * values) * -0.7213475204444817)
    return values * cdf, cdf + density


def split_low(values):
    high = values.astype(BF).astype(F32)
    return high, (values - high).astype(BF).astype(F32)


def block(packed, at):
    return packed[:, 16 * at : 16 * at + 16, :].reshape(128, 128)


def branch_weights(packed):
    return [block(packed, at) for at in (B_HEIGHT, B_WIDTH, B_CHANNEL)]


def spread_matrix():
    unit, lane = iota((128, 128), 0), iota((128, 128), 1)
    return ((lane == 16 * (unit // 4) + unit % 4) & (unit < 32)).astype(BF)


def pick_matrix(k):
    return (iota((384, 128), 0) == 3 * iota((384, 128), 1) + k).astype(BF)


def head_weights(packed, vec):
    w_reduce = dot(block(packed, B_REDUCE), spread_matrix()).astype(BF)
    expand = jnp.concatenate([block(packed, B_EXPAND + b) for b in range(3)], axis=1)
    picks = jnp.concatenate([pick_matrix(k) for k in range(3)], axis=1)
    w_expand = dot(expand, picks).astype(BF)
    b_expand = dot(vec[:, 0:384].astype(BF), picks)[V_BE : V_BE + 1, :]
    return w_reduce, w_expand, b_expand


def head_forward(sums, counts, branches, head, vec):
    w_reduce, w_expand, b_expand = head
    pooled = dot_wide(jnp.concatenate(sums, axis=1), branches) / counts
    pooled = pooled + (vec[V_BH : V_BH + 1, 0:128] + vec[V_BW : V_BW + 1, 0:128])
    pre = dot_wide(pooled, w_reduce) + vec[V_BR : V_BR + 1, 0:128]
    hidden, slope = gelu_both(pre)
    joined = dot_wide(hidden, w_expand) + b_expand
    logits = [joined[:, 128 * k : 128 * k + 128] for k in range(3)]
    top = jnp.maximum(jnp.maximum(logits[0], logits[1]), logits[2])
    powers = [jnp.exp(v - top) for v in logits]
    total = powers[0] + powers[1] + powers[2]
    return pooled, hidden, slope, [v / total for v in powers]


def column(row_values):
    stacked = jnp.where(iota((8, 128), 0) == 0, row_values, 0.0)
    return dot_tn(stacked.astype(BF), jnp.ones((8, 128), BF))


def size_columns(valid_ref):
    sizes = valid_ref[...].astype(F32).astype(BF)
    kind = iota((2, 128), 0)
    return [dot_tn(sizes, (kind == axis).astype(BF)) for axis in range(2)]


def inside_counts(valid_ref):
    high, wide = size_columns(valid_ref)
    offsets = jnp.broadcast_to(channel_offsets()[0, 0:1, :], (8, 128))

    def kept(size):
        past = jnp.where(offsets == 1, jnp.where(size == 32.0, 1.0, 0.0), 0.0)
        return size - past - jnp.where(offsets == -1, 1.0, 0.0)

    return [kept(high) * wide, kept(wide) * high, high * wide]


def count_column(valid_ref):
    high, wide = size_columns(valid_ref)
    return high * wide


def channel_offsets():
    return jnp.broadcast_to(((iota((1, 128), 1) + 1) % 3 - 1).reshape(1, 1, 128), (1, 32, 128))


def shifted_masks(valid_ref, image):
    sizes = jnp.where(iota((2, 8), 1) == image, valid_ref[...].astype(F32), 0.0)
    size = jnp.sum(sizes, axis=1, keepdims=True)
    masks = []
    for axis, shape in ((0, (32, 1, 128)), (1, (1, 32, 128))):
        limit = size[axis : axis + 1, :].reshape(1, 1, 1)
        at = iota(shape, axis)
        taker = at - channel_offsets()[:, 0:1, :]
        masks.append((at.astype(F32) < limit).astype(F32))
        masks.append(((taker >= 0) & (taker.astype(F32) < limit)).astype(F32))
    return masks


def class_sums(maps, masks):
    row, row_taker, col, col_taker = masks

    def by_row(mask):
        return jnp.sum((maps * mask).reshape(32, 4, 8, 128), axis=1)

    plain, taken = by_row(col), by_row(col_taker)
    return [
        jnp.sum(jnp.sum(rows * mask, axis=0), axis=0, keepdims=True)
        for rows, mask in ((plain, row_taker), (taken, row), (plain, row))
    ]


def pixel_masks(valid_ref, image):
    sizes = jnp.where(iota((2, 8), 1) == image, valid_ref[...].astype(F32), 0.0)
    size = jnp.sum(sizes, axis=1, keepdims=True)
    pixel, kind = iota((8, 1024), 1), iota((8, 1024), 0)

    def taker(at, one):
        back, forth = (kind == one).astype(jnp.int32), (kind == one + 1).astype(jnp.int32)
        return (at - back + forth).astype(F32)

    row, column = taker(pixel // 32, 1), taker(pixel % 32, 3)
    inside = (row >= 0.0) & (row < size[0:1]) & (column >= 0.0) & (column < size[1:2])
    return inside.astype(F32).astype(BF)


def place_of(placed):
    if not placed:
        return 0, 0
    shard = lax.axis_index("fsdp")
    return shard // 2, lax.rem(shard, 2)


def pack_kernel(*refs):
    (gain_one, bias_one, w_h, b_h, w_w, b_w, w_c, w_red, b_red, w_exp, b_exp, w_proj, b_proj,
     gain_two, bias_two, w_up, b_up, w_down, b_down, w_conv, b_conv, out, vec) = refs
    conv = out.at[ROWS : ROWS + CONV_ROWS]

    def put(at, values):
        out[16 * at : 16 * at + values.shape[0], 0 : values.shape[1]] = values

    put(B_HEIGHT, w_h[...])
    put(B_WIDTH, w_w[...])
    put(B_CHANNEL, w_c[...])
    put(B_PROJ, w_proj[...])
    blank = jnp.zeros((16, 128), BF)
    put(B_REDUCE, blank)
    put(B_REDUCE, w_red[...])
    for b in range(3):
        vec[...] = jnp.zeros((16, 128), F32)
        vec[0:4, :] = w_exp[:, 128 * b : 128 * b + 128].astype(F32)
        put(B_EXPAND + b, vec[...].astype(BF))
    for b in range(4):
        put(B_UP + b, w_up[:, 128 * b : 128 * b + 128])
    put(B_DOWN, w_down[...])
    conv[16 * (C_BLOCKS - 1) : 16 * C_BLOCKS, :] = blank
    for at, tap in enumerate(TAPS):
        kernel = w_conv.at[tap // 3, tap % 3]
        for b in range(2):
            start = 16 * (C_PAIRS + 2 * at + b)
            conv[start : start + 16, :] = kernel[:, 128 * b : 128 * b + 128]
        start, lane = 16 * (C_EDGES + at // 2), 64 * (at % 2)
        conv[start : start + 16, lane : lane + 64] = kernel[:, 256:320]
    vec[...] = jnp.zeros((16, 128), F32)
    vectors = (gain_one, bias_one, b_h, b_w, b_red, b_exp, b_proj, gain_two, bias_two, b_up, b_down, b_conv)
    for row, (values, length) in enumerate(zip(vectors, LENGTHS)):
        vec[row : row + 1, 0:length] = values[...].astype(F32).reshape(1, length)
    put(B_VEC, vec[...].astype(BF))


def vector_table(packed):
    shards = packed[:, 16 * B_VEC : 16 * B_VEC + 16, :].reshape(128, 128)
    table = jnp.zeros((16, 512), F32)
    rows = iota((16, 512), 0)
    for length in (16, 4, 48, 64, 40):
        step = 16 if length == 4 else length
        lane = iota((1, 512), 1)
        source = iota((128, 512), 0)
        pick = (source == jnp.where(lane % step < length, lane % step, -1)).astype(BF)
        spread = dot(shards, pick)
        mine = (source // 16) == (lane // step)
        whole = jnp.sum(jnp.where(mine, spread, 0.0).reshape(8, 16, 512), axis=0)
        held = functools.reduce(
            jnp.logical_or, [rows == v for v, size in enumerate(LENGTHS) if size == length]
        )
        table = jnp.where(held, whole, table)
    return table


def unit_kernel(
    valid, x_ref, cot_ref, unit_ref, low_ref, sums_ref, main_ref, right_ref, rest_ref, bias_ref, shift
):
    step, count = pl.program_id(0), x_ref.shape[0]

    @pl.when(step == 0)
    def _():
        shift[...] = jnp.zeros(shift.shape, F32)
        bias_ref[...] = jnp.zeros(bias_ref.shape, F32)

    lanes = iota((256, 128), 1) < 64
    blank, line = jnp.zeros((16, 256), BF), jnp.zeros((16, 128), F32)
    for m in range(count):
        cot = cot_ref[m].astype(F32)
        bias_ref[:, 0:320] += fold8(cot)
        shift[0:256, 0:320] = cot
        ahead = shift[1:257, :]
        ahead = jnp.where(iota((256, 384), 0) % 16 == 15, 0.0, ahead)
        main_ref[m, 0:256, :] = cot_ref[m, :, 0:256]
        main_ref[m, 256:272, :] = blank
        right_ref[m, 0:256, :] = ahead[:, 0:256].astype(BF)
        right_ref[m, 256:272, :] = blank
        both = jnp.where(lanes, shift[0:256, 256:384], pltpu.roll(ahead[:, 256:384], 64, 1))
        rest_ref[m, :, 0:128] = both.astype(BF)
        below = jnp.concatenate([both[16:256], line], axis=0)
        rest_ref[m, :, 128:256] = below.astype(BF)

    low = x_ref[...].reshape(count * 1024, 128)
    centre = low.astype(F32) - dot(low, jnp.full((128, 128), 1.0 / 128.0, BF))
    scale = lax.rsqrt(lane_mean(centre * centre) + EPS)
    unit = centre * scale
    here = pl.ds(step * count, count)
    unit_ref[here] = unit.reshape(count, 1024, 128)
    low_ref[here] = unit.astype(BF).reshape(count, 1024, 128)
    for m in range(count):
        image = step * count + m
        maps = unit[1024 * m : 1024 * m + 1024].reshape(32, 32, 128)
        for k, total in enumerate(class_sums(maps, shifted_masks(valid, image))):
            sums_ref[pl.ds(8 * k + image, 1), :] = total


def norm_kernel(
    placed, valid, unit_ref, own, swapped, mine, other,
    norm_ref, head_ref, reduce_ref, expand_ref, mix_ref, vec_ref, pk_ref, sums_ref
):
    chip, core = place_of(placed)
    pk_ref[2 * chip + core] = own[0:ROWS, :]
    pk_ref[2 * chip + (1 - core)] = swapped[0:ROWS, :]
    for peer in range(1, 4):
        shard = 2 * lax.bitwise_xor(chip, peer)
        pk_ref[shard + core] = mine[peer - 1]
        pk_ref[shard + (1 - core)] = other[peer - 1]
    vec = vector_table(pk_ref)
    vec_ref[...] = vec
    head = head_weights(pk_ref, vec)
    gain = vec[V_GAIN1 : V_GAIN1 + 1, 0:128]
    bias = vec[V_BIAS1 : V_BIAS1 + 1, 0:128]
    offsets = channel_offsets()[0, 0:1, :]
    for image in range(unit_ref.shape[0]):
        low = (unit_ref[image] * gain + bias).astype(BF)
        norm_ref[image] = low
        totals = dot(pixel_masks(valid, image), low)
        for k in range(2):
            forth, back = totals[2 * k + 1 : 2 * k + 2], totals[2 * k + 2 : 2 * k + 3]
            total = jnp.where(offsets == 1, forth, jnp.where(offsets == -1, back, totals[0:1]))
            sums_ref[8 * k + image : 8 * k + image + 1, :] = total
        sums_ref[16 + image : 17 + image, :] = totals[0:1]
    sums = [sums_ref[8 * k : 8 * k + 8, :] for k in range(3)]
    branches = jnp.concatenate(branch_weights(pk_ref), axis=0)
    pooled, hidden, slope, mixing = head_forward(sums, count_column(valid), branches, head, vec)
    for at, values in enumerate((pooled, hidden, slope)):
        head_ref[8 * at : 8 * at + 8, :] = values
    reduce_ref[...], expand_ref[...] = head[0], head[1]
    for k in range(3):
        mix_ref[8 * k : 8 * k + 8, :] = mixing[k]


def mlp_kernel(
    placed, x_ref, norm_ref, mix_ref, main_ref, right_ref, rest_ref, bias_ref, vec_ref, pk_ref,
    own, swapped, conv_mine, conv_other,
    pm_ref, gfirst_ref, gcat_ref, dmix_ref, wconv, keep_ref, send_ref,
    wcat, wproj, wup, wdown, wrest,
    gsec, low, act, ghid, norm2, mixes, mixed_s, gtail, gbranch, npad,
    a_conv, a_rest, a_up, a_down, a_proj, a_bup, a_bdown, a_bproj, a_gain2, a_bias2,
):
    step, steps = pl.program_id(0), pl.num_programs(0)
    count = x_ref.shape[0] // steps

    @pl.when(step == 0)
    def _():
        for k, weight in enumerate(branch_weights(pk_ref)):
            wcat[128 * k : 128 * k + 128, :] = weight
        wproj[...] = block(pk_ref, B_PROJ)
        for b in range(4):
            wup[:, 128 * b : 128 * b + 128] = block(pk_ref, B_UP + b)
        wdown[...] = pk_ref[:, 16 * B_DOWN : 16 * B_DOWN + 64, :].reshape(512, 128) * jnp.bfloat16(0.5)
        chip, core = place_of(placed)
        blank = jnp.zeros((16, 64), BF)
        for peer in range(4):
            conv = slice(ROWS, ROWS + CONV_ROWS)
            pair = (own.at[conv], swapped.at[conv])
            if peer > 0:
                pair = (conv_mine.at[peer - 1], conv_other.at[peer - 1])
            for part, odd in zip(pair, (core, 1 - core)):
                shard = 2 * lax.bitwise_xor(chip, peer) + odd
                for at in range(9):
                    rows = pl.ds(pl.multiple_of(128 * at + 16 * shard, 16), 16)
                    for b in range(2):
                        start = 16 * (C_PAIRS + 2 * at + b)
                        wconv[rows, 128 * b : 128 * b + 128] = part[start : start + 16, :]
                    start, lane = 16 * (C_EDGES + at // 2), 64 * (at % 2)
                    edge = part[start : start + 16, :][:, lane : lane + 64]
                    wconv[rows, 256:384] = jnp.concatenate([edge, blank], axis=1)
        none = jnp.zeros((128, 64), BF)
        for output, places in enumerate(((0, None, None, None), (1, 4, None, None), (2, None, 6, None), (3, 5, 7, 8))):
            ends = [none if at is None else wconv[128 * at : 128 * at + 128, 256:320] for at in places]
            rows = slice(128 * output, 128 * output + 128)
            wrest[rows, 0:128] = jnp.concatenate(ends[0:2], axis=1)
            wrest[rows, 128:256] = jnp.concatenate(ends[2:4], axis=1)
        for ref in (low, npad):
            ref[:, 0:1] = jnp.zeros((count, 1, 48, 128), F32)
            ref[:, 33:34] = jnp.zeros((count, 1, 48, 128), F32)
        for ref in (low, npad):
            shape = ref.shape[0:2] + (8, 128)
            ref[:, :, 0:8, :] = jnp.zeros(shape, F32)
            ref[:, :, 40:48, :] = jnp.zeros(shape, F32)
        for ref in (a_conv, a_rest, a_up, a_down, a_proj, a_bup, a_bdown, a_bproj, a_gain2, a_bias2):
            ref[...] = jnp.zeros(ref.shape, ref.dtype)

    def row(at, width=128):
        return vec_ref[at : at + 1, 0:width]

    images = range(count)
    maps = [step * count + m for m in images]
    pixels = [slice(1024 * m, 1024 * m + 1024) for m in images]

    offsets = channel_offsets()
    forth, back = offsets == 1, offsets == -1
    for m in images:
        mixing = [mix_ref[pl.ds(8 * k + maps[m], 1), :] for k in range(3)]
        biases = (row(V_BH), row(V_BW), 0.0)
        normed = norm_ref[maps[m]]
        here = normed.astype(F32).reshape(32, 32, 128)
        npad[m, 1:33, 8:40, :] = here
        high = jnp.where(
            forth, npad[m, 2:34, 8:40, :], jnp.where(back, npad[m, 0:32, 8:40, :], here)
        )
        wide = jnp.where(
            forth, npad[m, 1:33, 9:41, :], jnp.where(back, npad[m, 1:33, 7:39, :], here)
        )
        shifted = (high.reshape(1024, 128).astype(BF), wide.reshape(1024, 128).astype(BF), normed)
        mixed = 0.0
        for k in range(3):
            branch = dot(shifted[k], wcat[128 * k : 128 * k + 128, :]) + biases[k]
            mixes[pixels[m], 128 * k : 128 * k + 128] = branch
            mixed = mixed + branch * mixing[k]
        mixed_s[pixels[m], :] = mixed.astype(BF)
    first, unit, scale = [None] * count, [None] * count, [None] * count
    for m in images:
        added = dot(mixed_s[pixels[m], :], wproj[...]) + row(V_BP)
        first[m] = x_ref[maps[m]].astype(F32) + added
        centre = first[m] - lane_mean(first[m])
        scale[m] = lax.rsqrt(lane_mean(centre * centre) + EPS)
        unit[m] = centre * scale[m]
        norm2[pixels[m], :] = (unit[m] * row(V_GAIN2) + row(V_BIAS2)).astype(BF)

    flat = (count * 256, 256)
    cot_here, cot_right = main_ref[:, 0:256, :].reshape(flat), right_ref[:, 0:256, :].reshape(flat)
    cot_below, cot_both = main_ref[:, 16:272, :].reshape(flat), right_ref[:, 16:272, :].reshape(flat)
    cot_rest = rest_ref[...].reshape(flat)
    ends = dot_nt(cot_rest, wrest[...])
    from_here = dot_nt(cot_here, wconv[0:512, 0:256])
    from_right = dot_nt(cot_right, wconv[512:768, 0:256])
    from_below = dot_nt(cot_below, wconv[768:1024, 0:256])
    from_both = dot_nt(cot_both, wconv[1024:1152, 0:256])
    straight = from_here + ends
    planes = (
        (straight[:, 0:128], straight[:, 128:256] + from_right[:, 0:128]),
        (
            straight[:, 256:384] + from_below[:, 0:128],
            (straight[:, 384:512] + from_right[:, 128:256]) + (from_below[:, 128:256] + from_both),
        ),
    )
    for p in range(2):
        for s in range(2):
            plane = planes[p][s]
            for i in range(16 * count):
                gsec[2 * i + p, pl.ds(s, 16, stride=2), :] = plane[16 * i : 16 * i + 16, :]

    grad_second = [gsec[32 * m : 32 * m + 32].reshape(1024, 128) for m in images]
    for m in images:
        tail = grad_second[m].astype(BF)
        gtail[pixels[m], :] = tail
        a_bdown[...] += fold8(grad_second[m])
        for b in range(2):
            cols = slice(256 * b, 256 * b + 256)
            hidden = dot(norm2[pixels[m], :], wup[:, cols]) + vec_ref[V_BUP : V_BUP + 1, cols]
            grad_act = dot_nt(tail, wdown[cols, :])
            value, slope = gelu_twice(hidden)
            act[pixels[m], cols] = value.astype(BF)
            grad_hidden = grad_act * slope
            ghid[pixels[m], cols] = grad_hidden.astype(BF)
            a_bup[:, cols] += fold8(grad_hidden)
    grad_first = [None] * count
    for m in images:
        second = first[m] + (dot(act[pixels[m], :], wdown[...]) + row(V_BDOWN))
        low[m, 1:33, 8:40, :] = second.reshape(32, 32, 128)
        grad_normed = dot_nt(ghid[pixels[m], :], wup[...])
        a_gain2[...] += fold8(grad_normed * unit[m])
        a_bias2[...] += fold8(grad_normed)
        scaled_grad = grad_normed * row(V_GAIN2)
        grad_first[m] = grad_second[m] + scale[m] * (
            scaled_grad - lane_mean(scaled_grad) - unit[m] * lane_mean(scaled_grad * unit[m])
        )
        gfirst_ref[m] = grad_first[m]
        gbranch[pixels[m], :] = grad_first[m].astype(BF)
        a_bproj[...] += fold8(grad_first[m])
    a_up[...] += dot_tn(norm2[...], ghid[...])
    a_down[...] += dot_tn(gtail[...], act[...])
    for m in images:
        grad_mixed = dot_nt(gbranch[pixels[m], :], wproj[...])
        for k in range(3):
            share = fold8(grad_mixed * mixes[pixels[m], 128 * k : 128 * k + 128])
            dmix_ref[pl.ds(8 * k + maps[m], 1), :] = jnp.sum(share, axis=0, keepdims=True)
        npad[m, 1:33, 8:40, :] = grad_mixed.reshape(32, 32, 128)
        low_grad, image = grad_mixed.astype(BF), maps[m]
        gcat_ref[image, :, 0:128] = low_grad
        gcat_ref[image, 0:32, 128:256] = jnp.zeros((32, 128), BF)
        gcat_ref[image, 32:1024, 128:256] = low_grad[0:992]
        gcat_ref[image, 0:992, 256:384] = low_grad[32:1024]
        gcat_ref[image, 992:1024, 256:384] = jnp.zeros((32, 128), BF)
        gcat_ref[image, :, 384:512] = npad[m, 1:33, 7:39, :].reshape(1024, 128).astype(BF)
        gcat_ref[image, :, 512:640] = npad[m, 1:33, 9:41, :].reshape(1024, 128).astype(BF)

    for at, tap in enumerate(TAPS):
        r, s = tap // 3, tap % 3
        for m in images:
            patch = low[m, pl.ds(r, 16, stride=2), pl.ds(7 + s, 16, stride=2), :]
            pm_ref[m, :, 128 * at : 128 * at + 128] = patch.reshape(256, 128).astype(BF)

    a_proj[...] += dot_tn(mixed_s[...], gbranch[...])
    patches = pm_ref[...].reshape(256 * count, 1152)
    a_conv[...] += dot_tn(patches, cot_here)
    a_rest[...] += dot_tn(patches[:, 0:512], cot_rest)

    @pl.when(step == steps - 1)
    def _():
        chip, core = place_of(placed)[0:2]
        vectors = jnp.concatenate(
            [jnp.sum(bias_ref[:, 128 * b : 128 * b + 128], axis=0, keepdims=True) for b in range(3)]
            + [jnp.sum(a_bup[:, 128 * b : 128 * b + 128], axis=0, keepdims=True) for b in range(4)]
            + [jnp.sum(ref[...], axis=0, keepdims=True) for ref in (a_bdown, a_bproj, a_gain2, a_bias2)]
            + [jnp.zeros((5, 128), F32)],
            axis=0,
        )
        vectors, vectors_low = split_low(vectors)
        down = [0.5 * a_down[:, 128 * b : 128 * b + 128].T for b in range(4)]
        spots = ((0, 0), (1, 0), (2, 0), (3, 0), (1, 1), (3, 1), (2, 2), (3, 2), (3, 3))

        def edge(at, rows):
            patch, place = spots[at]
            rows = slice(128 * patch + rows.start, 128 * patch + rows.stop)
            return a_rest[rows, 64 * place : 64 * place + 64]


        def piece(at, shard):
            rows = slice(16 * shard, 16 * shard + 16)
            if at < G1_EDGE:
                start = 128 * (at // 2) + 16 * shard
                return a_conv[start : start + 16, 128 * (at % 2) : 128 * (at % 2) + 128]
            if at < G1_UP:
                one = edge(2 * (at - G1_EDGE), rows)
                two = jnp.zeros((16, 64), F32)
                if at < G1_UP - 1:
                    two = edge(2 * (at - G1_EDGE) + 1, rows)
                return jnp.concatenate([one, two], axis=1)
            if at < G1_DOWN:
                b = at - G1_UP
                return a_up[rows, 128 * b : 128 * b + 128]
            if at < G1_PROJ:
                start = 64 * (shard % 2) + 16 * (at - G1_DOWN)
                return down[shard // 2][start : start + 16, :]
            return a_proj[rows, :]

        for peer in range(4):
            to = lax.bitwise_xor(chip, peer)
            for at in range(G1_VEC):
                one, two = piece(at, 2 * peer), piece(at, 2 * peer + 1)
                keep_ref[to, 16 * at : 16 * at + 16, :] = jnp.where(core == 0, one, two)
                send_ref[to, 16 * at : 16 * at + 16, :] = jnp.where(core == 0, two, one).astype(BF)
            for at, values in ((G1_VEC, vectors), (G1_VEC_LOW, vectors_low)):
                keep_ref[to, 16 * at : 16 * at + 16, :] = values
                send_ref[to, 16 * at : 16 * at + 16, :] = values.astype(BF)


def branch_kernel(
    placed, valid, unit_ref, mix_ref, head_ref, reduce_ref, expand_ref, units_ref, gcat_ref, dmix_ref,
    vec_ref, pk_ref,
    spread_ref, keep_ref, send_ref,
    wcat, a_cat, a_edge, grads,
):
    step, steps = pl.program_id(0), pl.num_programs(0)
    count = unit_ref.shape[0] // BRANCH_STEPS

    @pl.when(step == 0)
    def _():
        for k, weight in enumerate(branch_weights(pk_ref)):
            wcat[128 * k : 128 * k + 128, :] = weight.astype(F32)
        for ref in (a_cat, a_edge, grads):
            ref[...] = jnp.zeros(ref.shape, ref.dtype)

    def row(at, width=128):
        return vec_ref[at : at + 1, 0:width]

    offsets = (iota((128, 128), 0) + 1) % 3 - 1
    for m in range(count):
        image = step * count + m
        outer = dot_tn(unit_ref[image], gcat_ref[image])
        plain = outer[:, 0:128]
        parts = (
            jnp.where(offsets == 1, outer[:, 128:256], jnp.where(offsets == -1, outer[:, 256:384], plain)),
            jnp.where(offsets == 1, outer[:, 384:512], jnp.where(offsets == -1, outer[:, 512:640], plain)),
            plain,
        )
        maps = gcat_ref[image, :, 0:128].astype(F32).reshape(32, 32, 128)
        by_column = jnp.sum(maps, axis=0)
        total = jnp.sum(by_column, axis=0, keepdims=True)
        left, right = by_column[0:1], by_column[31:32]
        upper = jnp.sum(maps[0], axis=0, keepdims=True)
        lower = jnp.sum(maps[31], axis=0, keepdims=True)
        for k in range(3):
            at = 8 * k + image
            part = parts[k]
            mixing = mix_ref[pl.ds(at, 1), :]
            a_cat[128 * k : 128 * k + 128, :] += part * mixing
            a_edge[k : k + 1, :] += mixing * total
            if k == 0:
                a_edge[3:4, :] += mixing * lower
                a_edge[4:5, :] += mixing * upper
            if k == 1:
                a_edge[5:6, :] += mixing * right
                a_edge[6:7, :] += mixing * left

    @pl.when(step == steps - 1)
    def _():
        counts = count_column(valid)
        pooled, hidden, slope = [head_ref[8 * at : 8 * at + 8, :] for at in range(3)]
        mixing = [mix_ref[8 * k : 8 * k + 8, :] for k in range(3)]
        grads_mix = [dmix_ref[8 * k : 8 * k + 8, :] for k in range(3)]
        mean = sum(m * g for m, g in zip(mixing, grads_mix))
        grad_logits = jnp.concatenate([m * (g - mean) for m, g in zip(mixing, grads_mix)], axis=1)
        grad_pre = dot_wide(grad_logits, expand_ref[...], dot_nt) * slope
        grad_pooled = dot_wide(grad_pre, reduce_ref[...], dot_nt)
        per_pixel = grad_pooled / counts
        branches = jnp.concatenate(branch_weights(pk_ref), axis=0)
        spread = dot_wide(per_pixel, branches, dot_nt)
        for k in range(3):
            spread_ref[8 * k : 8 * k + 8, :] = spread[:, 128 * k : 128 * k + 128]
        for at, part in enumerate(parts_of(outer_wide(pooled, grad_pre), 2)):
            grads[:, 32 * at : 32 * at + 32] = dot_nt(part, spread_matrix())[:, 0:32]
        picks = jnp.concatenate([pick_matrix(k) for k in range(3)], axis=1)
        grads[:, 128:512] = dot_nt(outer_wide(hidden, grad_logits).astype(BF), picks)
        summed = jnp.broadcast_to(jnp.sum(grad_logits, axis=0, keepdims=True), (8, 384))
        expand_bias = dot_wide(summed, picks, dot_nt)[0:1]
        reduce_bias = jnp.sum(grad_pre, axis=0, keepdims=True)
        pooled_sum = jnp.sum(grad_pooled, axis=0, keepdims=True)
        gain, bias = column(row(V_GAIN1)), column(row(V_BIAS1))
        unit_sums = jnp.concatenate([units_ref[8 * k : 8 * k + 8, :] for k in range(3)], axis=1)
        unit_part = a_cat[...] + outer_wide(unit_sums, per_pixel)
        edge_part = outer_wide(jnp.concatenate(inside_counts(valid), axis=1), per_pixel)
        to_gain, to_bias = jnp.zeros((128, 128), F32), jnp.zeros((128, 128), F32)
        for k in range(3):
            here = slice(128 * k, 128 * k + 128)
            edges = edge_part[here] + a_edge[k : k + 1, :]
            if k < 2:
                edges = edges - jnp.where(offsets == 1, a_edge[2 * k + 3 : 2 * k + 4, :], 0.0)
                edges = edges - jnp.where(offsets == -1, a_edge[2 * k + 4 : 2 * k + 5, :], 0.0)
            to_gain = to_gain + unit_part[here] * wcat[here, :]
            to_bias = to_bias + edges * wcat[here, :]
            a_cat[here, :] = gain * unit_part[here] + bias * edges
        ones = jnp.ones((8, 384), BF)
        chip, core = place_of(placed)
        vectors = jnp.concatenate(
            [
                dot_nt(ones, jnp.concatenate(parts_of(to_gain, 3), axis=1))[0:1],
                dot_nt(ones, jnp.concatenate(parts_of(to_bias, 3), axis=1))[0:1],
                a_edge[0:1, :] + pooled_sum,
                a_edge[1:2, :] + pooled_sum,
                reduce_bias,
                expand_bias[:, 0:128],
                expand_bias[:, 128:256],
                expand_bias[:, 256:384],
            ],
            axis=0,
        )
        vectors = jnp.concatenate(split_low(vectors), axis=0)

        def piece(at, shard):
            rows = slice(16 * shard, 16 * shard + 16)
            if at < G2_REDUCE:
                return a_cat[128 * at + 16 * shard : 128 * at + 16 * shard + 16, :]
            if at == G2_REDUCE:
                return grads[rows, 0:128]
            return jnp.concatenate(
                [grads[16 * shard : 16 * shard + 4, 128 * b : 128 * b + 128] for b in range(1, 4)]
                + [jnp.zeros((4, 128), F32)],
                axis=0,
            )

        for peer in range(4):
            to = lax.bitwise_xor(chip, peer)
            for at in range(G2_VEC):
                one, two = piece(at, 2 * peer), piece(at, 2 * peer + 1)
                keep_ref[to, 16 * at : 16 * at + 16, :] = jnp.where(core == 0, one, two)
                send_ref[to, 16 * at : 16 * at + 16, :] = jnp.where(core == 0, two, one).astype(BF)
            keep_ref[to, 16 * G2_VEC : 16 * G2_VEC + 16, :] = vectors
            send_ref[to, 16 * G2_VEC : 16 * G2_VEC + 16, :] = vectors.astype(BF)


def input_kernel(base, valid, x_ref, mix_ref, spread, gcat_ref, gfirst_ref, vec_ref, pk_ref, *rest):
    grad_ref, token, wcat = rest[-3:]
    token[...] = jnp.zeros((8, 128), F32)
    step, count = pl.program_id(0), grad_ref.shape[0]

    @pl.when(step == 0)
    def _():
        offsets = (iota((128, 128), 0) + 1) % 3 - 1
        height, width, channel = [weight.astype(F32) for weight in branch_weights(pk_ref)]
        for at, (weight, offset) in enumerate(
            ((height, 0), (height, 1), (height, -1), (width, 0), (width, 1), (width, -1))
        ):
            wcat[:, 128 * at : 128 * at + 128] = jnp.where(offsets == offset, weight, 0.0)
        wcat[:, 768:896] = channel

    for m in range(count):
        image = base + step * count + m
        by_height, by_width, by_channel = [mix_ref[pl.ds(8 * k + image, 1), :] for k in range(3)]
        scaled = jnp.concatenate(
            [
                wcat[:, 0:128] * by_height + wcat[:, 384:512] * by_width + wcat[:, 768:896] * by_channel,
                wcat[:, 128:256] * by_height,
                wcat[:, 256:384] * by_height,
                wcat[:, 512:640] * by_width,
                wcat[:, 640:768] * by_width,
            ],
            axis=1,
        ).astype(BF)
        row, row_taker, col, col_taker = shifted_masks(valid, image)
        high, wide, plain = [spread[pl.ds(8 * k + image, 1), :].reshape(1, 1, 128) for k in range(3)]
        even = row * (col_taker * wide + col * plain) + row_taker * (col * high)
        grad_ref[m] = dot_nt(gcat_ref[image], scaled) + even.reshape(1024, 128)
    pixels = 1024 * count
    scaled_grad = grad_ref[...].reshape(pixels, 128) * vec_ref[V_GAIN1 : V_GAIN1 + 1, 0:128]
    here = pl.ds(base + step * count, count)
    values = x_ref[here].reshape(pixels, 128).astype(F32)
    centre = values - lane_mean(values)
    scale = lax.rsqrt(lane_mean(centre * centre) + EPS)
    unit = centre * scale
    grad = gfirst_ref[here].reshape(pixels, 128) + scale * (
        scaled_grad - lane_mean(scaled_grad) - unit * lane_mean(scaled_grad * unit)
    )
    grad_ref[...] = grad.reshape(count, 1024, 128)


def conv_kernel(pm_ref, vec_ref, wconv, after, map_ref, token):
    token[...] = jnp.zeros((8, 128), F32)
    count = map_ref.shape[0]
    out = dot(pm_ref[...].reshape(256 * count, 1152), wconv[...])
    out = out + vec_ref[V_BCONV : V_BCONV + 1, 0:384]
    map_ref[...] = out[:, 0:320].astype(BF).reshape(count, 256, 320)


def sds(shape, dtype):
    return jax.ShapeDtypeStruct(shape, dtype)


def whole(shape):
    return pl.BlockSpec(shape, lambda s: (0,) * len(shape))


def params(mega):
    return pltpu.CompilerParams(vmem_limit_bytes=mega * 1024 * 1024)


def cost(microseconds):
    return pl.CostEstimate(
        flops=int(microseconds * 3e8), bytes_accessed=int(microseconds * 3e6), transcendentals=0
    )


VMEM_SPEC = pl.BlockSpec(memory_space=pltpu.VMEM)
ANY_SPEC = pl.BlockSpec(memory_space=pl.ANY)


def in_vmem(value):
    return pltpu.with_memory_space_constraint(value, pltpu.VMEM)


def in_hbm(value):
    return pltpu.with_memory_space_constraint(value, pltpu.HBM)


def per_step(shape, index):
    return pl.BlockSpec(shape, lambda s: (index(s),) + (0,) * (len(shape) - 1))


def same(step):
    return step


UNIT_IMAGES, MLP_IMAGES, INPUT_IMAGES, CONV_IMAGES = 2, 2, 2, 2
BRANCH_STEPS = 1
SMALL_MB, UNIT_MB, NORM_MB, MLP_MB, BRANCH_MB, INPUT_MB, CONV_MB = 8, 16, 16, 35, 16, 20, 16


def cot_specs(count):
    return [per_step((count, rows, 256), same) for rows in (272, 272, 256)]


def run_unit(valid, x, cot):
    images, count = x.shape[0], UNIT_IMAGES
    return pl.pallas_call(
        unit_kernel,
        grid=(images // count,),
        in_specs=[VMEM_SPEC, per_step((count, 1024, 128), same), per_step((count, 256, 320), same)],
        out_specs=[VMEM_SPEC] * 3 + cot_specs(count) + [VMEM_SPEC],
        out_shape=[
            pltpu.VMEM((images, 1024, 128), F32),
            pltpu.VMEM((images, 1024, 128), BF),
            sds((24, 128), F32),
            sds((images, 272, 256), BF),
            sds((images, 272, 256), BF),
            sds((images, 256, 256), BF),
            sds((8, 384), F32),
        ],
        scratch_shapes=[pltpu.VMEM((264, 384), F32)],
        compiler_params=params(UNIT_MB),
        cost_estimate=cost(4),
        name="unit",
    )(valid, in_hbm(x), in_hbm(cot))


def run_norm(placed, valid, unit, *parts):
    images = unit.shape[0]
    return pl.pallas_call(
        functools.partial(norm_kernel, placed),
        in_specs=[VMEM_SPEC] * 6,
        out_specs=[VMEM_SPEC] * 7,
        out_shape=[
            pltpu.VMEM((images, 1024, 128), BF),
            sds((24, 128), F32),
            sds((128, 128), BF),
            sds((128, 384), BF),
            sds((24, 128), F32),
            sds((16, 512), F32),
            pltpu.VMEM((SHARDS, ROWS, 128), BF),
        ],
        scratch_shapes=[pltpu.VMEM((24, 128), F32)],
        compiler_params=params(NORM_MB),
        cost_estimate=cost(5),
        name="norm",
    )(valid, in_vmem(unit), *parts)


def run_mlp(placed, x, normed, mix, cot, vec, packed, *conv):
    images, count = x.shape[0], MLP_IMAGES
    pixels = 1024 * count
    g1 = (4, 16 * G1_BLOCKS, 128)
    shapes = [
        ((384, 128), BF), ((128, 128), BF), ((128, 512), BF), ((512, 128), BF), ((512, 256), BF),
        ((32 * count, 32, 128), F32), ((count, 34, 48, 128), F32),
        ((pixels, 512), BF), ((pixels, 512), BF), ((pixels, 128), BF), ((pixels, 384), F32), ((pixels, 128), BF),
        ((pixels, 128), BF), ((pixels, 128), BF), ((count, 34, 48, 128), F32),
        ((1152, 256), F32), ((512, 256), F32), ((128, 512), F32), ((128, 512), F32), ((128, 128), F32),
        ((8, 512), F32), ((8, 128), F32), ((8, 128), F32), ((8, 128), F32), ((8, 128), F32),
    ]
    return pl.pallas_call(
        functools.partial(mlp_kernel, placed),
        grid=(images // count,),
        in_specs=[VMEM_SPEC]
        + [VMEM_SPEC] * 2
        + cot_specs(count)
        + [VMEM_SPEC] * 7,
        out_specs=[per_step((count, 256, 1152), same), per_step((count, 1024, 128), same)] + [VMEM_SPEC] * 5,
        out_shape=[
            sds((images, 256, 1152), BF),
            sds((images, 1024, 128), F32),
            pltpu.VMEM((images, 1024, 640), BF),
            sds((24, 128), F32),
            pltpu.VMEM((1152, 384), BF),
            pltpu.VMEM(g1, F32),
            pltpu.VMEM(g1, BF),
        ],
        scratch_shapes=[pltpu.VMEM(*shape) for shape in shapes],
        compiler_params=params(MLP_MB),
        cost_estimate=cost(35),
        name="mlp",
    )(in_vmem(x), in_vmem(normed), mix, *[in_hbm(part) for part in cot[0:3]], cot[3], vec, in_vmem(packed), *conv)


def run_branches(placed, valid, unit, mix, head, reduce, expand, units, gcat, dmix, vec, packed):
    g2 = (4, 16 * G2_BLOCKS, 128)
    shapes = [
        ((384, 128), F32), ((384, 128), F32), ((8, 128), F32), ((128, 512), F32),
    ]
    return pl.pallas_call(
        functools.partial(branch_kernel, placed),
        grid=(BRANCH_STEPS,),
        in_specs=[VMEM_SPEC] * 11,
        out_specs=[VMEM_SPEC] * 3,
        out_shape=[sds((24, 128), F32), sds(g2, F32), sds(g2, BF)],
        scratch_shapes=[pltpu.VMEM(*shape) for shape in shapes],
        compiler_params=params(BRANCH_MB),
        cost_estimate=cost(8),
        name="branches",
    )(valid, in_vmem(unit), mix, head, reduce, expand, units, in_vmem(gcat), dmix, vec, in_vmem(packed))


def run_input(base, held, valid, x, mix, spread, gcat, gfirst, vec, packed, after):
    images, count = x.shape[0], INPUT_IMAGES
    maps = per_step((count, 1024, 128), lambda s: s + base // count)
    more = [] if held is None else [held]
    return pl.pallas_call(
        functools.partial(input_kernel, base),
        grid=(images // count // 2,),
        in_specs=[
            VMEM_SPEC, VMEM_SPEC, VMEM_SPEC, VMEM_SPEC, VMEM_SPEC, VMEM_SPEC, VMEM_SPEC, VMEM_SPEC, ANY_SPEC,
        ]
        + [ANY_SPEC] * len(more),
        out_specs=[maps, whole((8, 128))],
        out_shape=[sds((images, 1024, 128), F32), sds((8, 128), F32)],
        scratch_shapes=[pltpu.VMEM((128, 896), F32)],
        compiler_params=params(INPUT_MB),
        input_output_aliases={9: 0} if more else {},
        cost_estimate=cost(4),
        name="input_grad",
    )(valid, in_vmem(x), mix, spread, in_vmem(gcat), in_vmem(gfirst), vec, in_vmem(packed), after, *more)


def run_conv(pm, vec, wconv, after):
    images, count = pm.shape[0], CONV_IMAGES
    return pl.pallas_call(
        conv_kernel,
        grid=(images // count,),
        in_specs=[per_step((count, 256, 1152), same), VMEM_SPEC, VMEM_SPEC, ANY_SPEC],
        out_specs=[per_step((count, 256, 320), same), whole((8, 128))],
        out_shape=[sds((images, 256, 320), BF), sds((8, 128), F32)],
        compiler_params=params(CONV_MB),
        cost_estimate=cost(4),
        name="conv_out",
    )(in_hbm(pm), vec, in_vmem(wconv), after)


def pack_weights(weights):
    return pl.pallas_call(
        pack_kernel,
        out_shape=pltpu.VMEM((ROWS + CONV_ROWS, 128), BF),
        in_specs=[VMEM_SPEC] * 21,
        out_specs=VMEM_SPEC,
        scratch_shapes=[pltpu.VMEM((16, 128), F32)],
        compiler_params=params(60),
        name="pack",
    )(*weights)


def join_kernel(one, two, three, after, small, conv):
    for at, part in enumerate((one, two, three)):
        small[at] = part[0:ROWS, :]
        conv[at] = part[ROWS : ROWS + CONV_ROWS, :]


def join(near, after):
    return pl.pallas_call(
        join_kernel,
        out_shape=[sds((3, ROWS, 128), BF), sds((3, CONV_ROWS, 128), BF)],
        in_specs=[VMEM_SPEC] * 3 + [ANY_SPEC],
        out_specs=[VMEM_SPEC] * 2,
        compiler_params=params(SMALL_MB),
        cost_estimate=cost(1),
        name="join",
    )(*near, after)


def refine(ref, values):
    ref[...] = values.astype(BF)
    at = 16 * G1_VEC
    both = split_low(values[at : at + 16] + values[at + 16 : at + 32])
    ref[at : at + 32, :] = jnp.concatenate(both, axis=0).astype(BF)
    at = 16 * (G1_BLOCKS + G2_VEC)
    both = split_low(values[at : at + 8] + values[at + 8 : at + 16])
    ref[at : at + 16, :] = jnp.concatenate(both, axis=0).astype(BF)
    at = 16 * (G1_BLOCKS + G2_REDUCE)
    both = split_low(values[at : at + 16, 0:32] + values[at : at + 16, 32:64])
    ref[at : at + 16, 0:64] = jnp.concatenate(both, axis=1).astype(BF)


def sum_pair_kernel(keep1, got1, keep2, got2, own, *others):
    for peer in range(4):
        one = keep1[peer] + got1[peer].astype(F32)
        two = keep2[peer] + got2[peer].astype(F32)
        values = jnp.concatenate([one, two], axis=0)
        if peer == 0:
            own[...] = values
        else:
            refine(others[peer - 1], values)


def sum_four_kernel(own, one, two, three, after, total, low):
    value = own[...] + one[...].astype(F32) + two[...].astype(F32) + three[...].astype(F32)
    total[...] = value
    refine(low, value)


def sum_two_kernel(own, one, after, total, low):
    value = own[...] + one[...].astype(F32)
    total[...] = value
    refine(low, value)


def sum_two(*values):
    shape = values[0].shape
    return pl.pallas_call(
        sum_two_kernel,
        out_shape=[sds(shape, F32), sds(shape, BF)],
        in_specs=[VMEM_SPEC] * 2 + [ANY_SPEC],
        out_specs=[VMEM_SPEC] * 2,
        compiler_params=params(SMALL_MB),
        cost_estimate=cost(1),
        name="sum_two",
    )(*values)


def sum_pair(keep1, got1, keep2, got2):
    rows = keep1.shape[1] + keep2.shape[1]
    return pl.pallas_call(
        sum_pair_kernel,
        out_shape=[sds((rows, 128), F32)] + [sds((rows, 128), BF)] * 3,
        in_specs=[VMEM_SPEC] * 4,
        out_specs=[VMEM_SPEC] * 4,
        compiler_params=params(SMALL_MB),
        cost_estimate=cost(2),
        name="sum_pair",
    )(keep1, got1, keep2, got2)


def sum_four(*values):
    shape = values[0].shape
    return pl.pallas_call(
        sum_four_kernel,
        out_shape=[sds(shape, F32), sds(shape, BF)],
        in_specs=[VMEM_SPEC] * 4 + [ANY_SPEC],
        out_specs=[VMEM_SPEC] * 2,
        compiler_params=params(SMALL_MB),
        cost_estimate=cost(2),
        name="sum_four",
    )(*values)


def finish_kernel(*refs):
    (own, far,
     gain_one, bias_one, w_h, b_h, w_w, b_w, w_c, w_red, b_red, w_exp, b_exp, w_proj, b_proj,
     gain_two, bias_two, w_up, b_up, w_down, b_down, w_conv, b_conv) = refs
    shard = lax.axis_index("fsdp")

    def first(at, rows=16):
        here = slice(16 * at, 16 * at + rows)
        return own[here, :] + far[here, :].astype(F32)

    def second(at, rows=16):
        return first(G1_BLOCKS + at, rows)

    w_h[...] = second(G2_HEIGHT)
    w_w[...] = second(G2_WIDTH)
    w_c[...] = second(G2_CHANNEL)
    reduce = second(G2_REDUCE)
    w_red[...] = reduce[:, 0:32] + reduce[:, 32:64]
    expand = second(G2_EXPAND)
    for b in range(3):
        w_exp[:, 128 * b : 128 * b + 128] = expand[4 * b : 4 * b + 4, :]
    w_proj[...] = first(G1_PROJ)
    for b in range(4):
        w_up[:, 128 * b : 128 * b + 128] = first(G1_UP + b)
    w_down[...] = first(G1_DOWN, 64)
    for at, tap in enumerate(TAPS):
        kernel = w_conv.at[tap // 3, tap % 3]
        for b in range(2):
            kernel[:, 128 * b : 128 * b + 128] = first(G1_CONV + 2 * at + b)
        edge = 64 * (at % 2)
        kernel[:, 256:320] = first(G1_EDGE + at // 2)[:, edge : edge + 64]
    table_one, table_two = first(G1_VEC) + first(G1_VEC_LOW), second(G2_VEC)
    table_two = table_two[0:8, :] + table_two[8:16, :]

    def share(table, row, blocks, length, stride):
        total = jnp.zeros((1, 128), F32)
        for b in range(blocks):
            pick = iota((128, 128), 0) + 128 * b == iota((128, 128), 1) + shard * stride
            total = total + dot_wide(table, pick.astype(BF))[row + b : row + b + 1, :]
        return total[:, 0:length].reshape(length)

    gain_one[...] = share(table_two, G2_GAIN1, 1, 16, 16)
    bias_one[...] = share(table_two, G2_BIAS1, 1, 16, 16)
    b_h[...] = share(table_two, G2_BH, 1, 16, 16)
    b_w[...] = share(table_two, G2_BW, 1, 16, 16)
    b_red[...] = share(table_two, G2_BR, 1, 4, 16)
    b_exp[...] = share(table_two, G2_BE, 3, 48, 48)
    b_proj[...] = share(table_one, G1_BPROJ, 1, 16, 16)
    gain_two[...] = share(table_one, G1_GAIN2, 1, 16, 16)
    bias_two[...] = share(table_one, G1_BIAS2, 1, 16, 16)
    b_up[...] = share(table_one, G1_BUP, 4, 64, 64)
    b_down[...] = share(table_one, G1_BDOWN, 1, 16, 16)
    b_conv[...] = share(table_one, G1_BCONV, 3, 40, 40)


def finish(sums, weights):
    return pl.pallas_call(
        finish_kernel,
        out_shape=[sds(w.shape, F32) for w in weights],
        in_specs=[VMEM_SPEC] * 2,
        out_specs=[VMEM_SPEC] * 21,
        compiler_params=params(SMALL_MB),
        name="finish",
    )(*sums)


def early(placed, input_map, valid_size, cotangent, gathered):
    images = input_map.shape[0]
    x = input_map.reshape(images, 1024, 128)
    valid_size = valid_size.T
    cot = cotangent.reshape(images, 256, 320)
    unit, unit_low, units, main, right, rest, bias = run_unit(valid_size, x, cot)
    small, conv = gathered(units)
    normed, head, reduce, expand, mix, vec, packed = run_norm(placed, valid_size, unit, *small)
    pm, gfirst, gcat, dmix, wconv, keep1, send1 = run_mlp(
        placed, x, normed, mix, (main, right, rest, bias), vec, packed, *conv
    )
    spread, keep2, send2 = run_branches(
        placed, valid_size, unit_low, mix, head, reduce, expand, units, gcat, dmix, vec, packed
    )

    def late_map(after):
        out, token = run_conv(pm, vec, wconv, after)
        return out.reshape(images, 16, 16, 320), token

    def late_grad(after, held=None):
        base = 0 if held is None else images // 2
        return run_input(base, held, valid_size, x, mix, spread, gcat, gfirst, vec, packed, after)

    return (keep1, send1, keep2, send2), late_map, late_grad


def spread_out(packed):
    own = (packed[0], packed[1])
    return [
        own + (packed[2::2, rows], packed[3::2, rows]) for rows in (slice(0, ROWS), slice(ROWS, None))
    ]


def compute(placed, input_map, valid_size, cotangent, packed):
    sums, late_map, late_grad = early(
        placed,
        input_map,
        valid_size,
        cotangent,
        lambda after: spread_out(packed),
    )
    input_grad = late_grad(sums[0], late_grad(sums[0])[0])[0]
    return late_map(sums[0])[0], input_grad.reshape(input_map.shape), sums


def pack_whole(weights):
    (gain_one, bias_one, w_h, b_h, w_w, b_w, w_c, w_red, b_red, w_exp, b_exp, w_proj, b_proj,
     gain_two, bias_two, w_up, b_up, w_down, b_down, w_conv, b_conv) = weights

    def split(weight):
        weight = weight.reshape(SHARDS, weight.shape[0] // SHARDS, weight.shape[1])
        rows, cols = -weight.shape[1] % 16, -weight.shape[2] % 128
        weight = jnp.pad(weight, ((0, 0), (0, rows), (0, cols)))
        return [weight[:, :, at : at + 128] for at in range(0, weight.shape[2], 128)]

    pieces = split(w_h) + split(w_w) + split(w_c) + split(w_proj) + split(w_red) + split(w_exp)
    pieces = pieces + split(w_up) + split(w_down)
    taps = [split(w_conv[tap // 3, tap % 3]) for tap in TAPS]
    edges = [tap[2][:, :, 0:64] for tap in taps]
    edges.append(jnp.zeros_like(edges[0]))
    conv = [part for tap in taps for part in tap[0:2]]
    conv = conv + [jnp.concatenate(edges[at : at + 2], axis=2) for at in range(0, 10, 2)]
    vectors = (gain_one, bias_one, b_h, b_w, b_red, b_exp, b_proj, gain_two, bias_two, b_up, b_down, b_conv)
    rows = [
        jnp.pad(v.reshape(SHARDS, 1, v.shape[0] // SHARDS), ((0, 0), (0, 0), (0, 128 - v.shape[0] // SHARDS)))
        for v in vectors
    ]
    rows = rows + [jnp.zeros((SHARDS, 4, 128), BF)]
    return jnp.concatenate(pieces + [jnp.concatenate(rows, axis=1)] + conv, axis=1)


def unpack_whole(sums):
    one = jnp.stack([sums[0], sums[1].astype(F32)], axis=1).reshape(SHARDS, -1, 128)
    two = jnp.stack([sums[2], sums[3].astype(F32)], axis=1).reshape(SHARDS, -1, 128)

    def join(buffer, at, blocks, rows=16):
        parts = [buffer[:, 16 * (at + b) : 16 * (at + b) + rows, :] for b in range(blocks)]
        return jnp.concatenate(parts, axis=2).reshape(SHARDS * rows, 128 * blocks)

    def vector(buffer, at, row, blocks=1):
        start, rest = 16 * at + row, 16 if at == G1_VEC else 8
        both = buffer[0, start : start + blocks, :] + buffer[0, start + rest : start + rest + blocks, :]
        return both.reshape(128 * blocks)

    expand = two[:, 16 * G2_EXPAND : 16 * G2_EXPAND + 12, :].reshape(SHARDS, 3, 4, 128)
    taps = []
    for tap in range(9):
        at = TAPS.index(tap)
        edge = join(one, G1_EDGE + at // 2, 1)[:, 64 * (at % 2) : 64 * (at % 2) + 64]
        taps.append(jnp.concatenate([join(one, G1_CONV + 2 * at, 2), edge], axis=1))
    return (
        vector(two, G2_VEC, G2_GAIN1),
        vector(two, G2_VEC, G2_BIAS1),
        join(two, G2_HEIGHT, 1),
        vector(two, G2_VEC, G2_BH),
        join(two, G2_WIDTH, 1),
        vector(two, G2_VEC, G2_BW),
        join(two, G2_CHANNEL, 1),
        join(two, G2_REDUCE, 1)[:, 0:32] + join(two, G2_REDUCE, 1)[:, 32:64],
        vector(two, G2_VEC, G2_BR).reshape(SHARDS, 16)[:, 0:4].reshape(32),
        expand.transpose(0, 2, 1, 3).reshape(32, 384),
        vector(two, G2_VEC, G2_BE, 3),
        join(one, G1_PROJ, 1),
        vector(one, G1_VEC, G1_BPROJ),
        vector(one, G1_VEC, G1_GAIN2),
        vector(one, G1_VEC, G1_BIAS2),
        join(one, G1_UP, 4),
        vector(one, G1_VEC, G1_BUP, 4),
        one[:, 16 * G1_DOWN : 16 * G1_DOWN + 64, :].reshape(512, 128),
        vector(one, G1_VEC, G1_BDOWN),
        jnp.stack(taps).reshape(3, 3, 128, 320),
        vector(one, G1_VEC, G1_BCONV, 3)[0:320],
    )


def shards_of(mesh):
    shards, copies = mesh.shape["fsdp"], mesh.shape["rep"]

    def eight(input_map, valid_size, *rest):
        weights, cotangent = rest[:-1], rest[-1]
        sibling = [(i, i ^ 1) for i in range(shards)]
        packs = pack_weights(weights)
        swapped = lax.ppermute(packs, "fsdp", sibling)
        near = [
            lax.ppermute(packs, "fsdp", [(i, i ^ (2 * peer)) for i in range(shards)])
            for peer in range(1, 4)
        ]

        def gathered(after):
            small, conv = join(near, after)
            own = (packs, swapped)
            return own + (small, lax.ppermute(small, "fsdp", sibling)), (
                own + (conv, lax.ppermute(conv, "fsdp", sibling))
            )

        (keep1, send1, keep2, send2), late_map, late_grad = early(
            True, input_map, valid_size, cotangent, gathered
        )
        got1, got2 = lax.ppermute(send1, "fsdp", sibling), lax.ppermute(send2, "fsdp", sibling)
        own, *others = sum_pair(keep1, got1, keep2, got2)
        moved = [
            lax.ppermute(value, "fsdp", [(i, i ^ (2 * (peer + 1))) for i in range(shards)])
            for peer, value in enumerate(others)
        ]
        out, token = late_map(own)
        total, low = sum_four(own, *moved, token)
        both = [(copy, shard) for copy in range(copies) for shard in range(shards)]
        steps = [
            [(z * shards + f, (z ^ (1 + (f + at) % 2)) * shards + f) for z, f in both] for at in range(2)
        ]
        far = lax.ppermute(low, ("rep", "fsdp"), steps[0])
        held, token = late_grad(total)
        total, low = sum_two(total, far, token)
        far = lax.ppermute(low, ("rep", "fsdp"), steps[1])
        input_grad = late_grad(total, held)[0].reshape(input_map.shape)
        return (out, input_grad) + tuple(finish((total, far), weights))

    def general(input_map, valid_size, *rest):
        weights, cotangent = rest[:-1], rest[-1]
        dims = [2 if w.ndim == 4 else 0 for w in weights]
        full = [lax.all_gather(w, "fsdp", axis=d, tiled=True) for w, d in zip(weights, dims)]
        packed = pack_whole(full)
        out, input_grad, sums = compute(False, input_map, valid_size, cotangent, packed)
        grads = [
            lax.psum_scatter(g, "fsdp", scatter_dimension=d, tiled=True)
            for g, d in zip(unpack_whole(sums), dims)
        ]
        return (out, input_grad) + tuple(lax.psum(grads, "rep"))

    return eight if shards == SHARDS and copies == 4 else general


def solution(mesh):
    maps = P(("rep", "fsdp"), None, None, None)
    vector, matrix = P("fsdp"), P("fsdp", None)
    weights = (
        vector, vector, matrix, vector, matrix, vector, matrix, matrix, vector, matrix, vector,
        matrix, vector, vector, vector, matrix, vector, matrix, vector,
        P(None, None, "fsdp", None), vector,
    )
    return jax.shard_map(
        shards_of(mesh),
        mesh=mesh,
        in_specs=(maps, P(("rep", "fsdp"), None)) + weights + (maps,),
        out_specs=(maps, maps) + weights,
        check_vma=False,
    )
```
